128 devices in a mesh: slab: 32 (over z, y, core), chan: 4 (over x).
Axes of the slice: x: 4, y: 4, z: 4, core: 2. Of those that a mesh axis runs over, the one named last changes fastest.
Arguments:
- field: bfloat16 [64, 64, 128, 512], P('slab', None, 'chan'), may hold values from -8 to 8
- spectral_weights: float32 [2, 64, 8, 8, 128, 128], P(None, 'slab', None, None, 'chan'), may hold values from -0.5 to 0.5
- bias: float32 [128], P('chan'), may hold values from -3 to 3
Outputs:
- updated: float32 [64, 64, 128, 512], P('slab', None, 'chan')
The draws below stay inside these ranges and needn't reach their ends.
All inputs are finite; a program needn't handle non-finite values.
Results may differ from the reference program's by a relative error of at most 0.0003.
Values sent between devices are 32-bit elements; how exact they have to be, the bound alone decides.
A program may use at most 128 MiB of HBM per device.

```python
import math
import jax
import jax.numpy as jnp
from jax import lax

GX = 64
GY = 64
GZ = 32
GT = 16
MX = 8
MY = 8
MZ = 8
MT = 8
CH = 128
KQ = 64
ZT = 512


def draw_field(key, part):
    key = jax.random.fold_in(key, 7)
    rough_key = jax.random.fold_in(key, 1)
    amp_key = jax.random.fold_in(key, 2)
    phase_key = jax.random.fold_in(key, 3)
    x_pos = jnp.arange(GX).astype(jnp.int32)[:, None, None, None]
    y_pos = jnp.arange(GY).astype(jnp.int32)[None, :, None, None]
    cell_pos = jnp.arange(GZ * GT).astype(jnp.int32)[None, None, None, :]
    depth_pos = cell_pos // GT
    time_pos = cell_pos % GT
    full_shape = (GX, GY, CH, GZ * GT)
    total = 0.7 * jnp.clip(jax.random.normal(rough_key, full_shape, jnp.float32), -4.0, 4.0)
    amplitudes = jax.random.uniform(amp_key, (6, CH), jnp.float32, 0.3, 0.8)
    phases = jax.random.uniform(phase_key, (6, CH), jnp.float32, 0.0, 2.0 * math.pi)
    for wave in range(6):
        freq_key = jax.random.fold_in(key, 10 + wave)
        freq_x = jax.random.randint(jax.random.fold_in(freq_key, 0), (), 0, MX)
        freq_y = jax.random.randint(jax.random.fold_in(freq_key, 1), (), 0, MY)
        freq_z = jax.random.randint(jax.random.fold_in(freq_key, 2), (), 0, MZ)
        freq_t = jax.random.randint(jax.random.fold_in(freq_key, 3), (), 0, MT)
        fraction = (freq_x * x_pos % GX).astype(jnp.float32) / GX
        fraction = fraction + (freq_y * y_pos % GY).astype(jnp.float32) / GY
        fraction = fraction + (freq_z * depth_pos % GZ).astype(jnp.float32) / GZ
        fraction = fraction + (freq_t * time_pos % GT).astype(jnp.float32) / GT
        total = total + amplitudes[wave][None, None, :, None] * jnp.cos(2.0 * math.pi * fraction + phases[wave][None, None, :, None])
    return total.astype(jnp.bfloat16)


def shard_levels(rng, dims, shards, smallest, top_value):
    loudness, own = 1.0, jax.random.fold_in(rng, 6)
    for dim, shards_of in shards:
        draws = jnp.exp(jax.random.uniform(jax.random.fold_in(own, dim), (shards_of,), jnp.float32, smallest / len(shards), top_value / len(shards)))
        loudness = loudness * jnp.repeat(draws, dims[dim] // shards_of).reshape([-1 if axis == dim else 1 for axis in range(len(dims))])
    return loudness


def normal_values(own_key, shape, spread, limit, cuts=(), held_as=jnp.bfloat16):
    result = jax.random.normal(own_key, shape, jnp.float32) * spread
    if len(cuts) > 0:
        result = shard_levels(own_key, shape, cuts, -0.22, 0.18) * result
    return jnp.clip(result, min=-limit, max=limit).astype(held_as)


def setup_inputs(seed: int = 0) -> dict:
    arg_keys = jax.random.split(jax.random.key(seed), 4)
    field = draw_field(jax.random.fold_in(arg_keys[3], 71), 0)
    spectral_weights = normal_values(arg_keys[1], (2, KQ, MX, MY, CH, CH), CH ** -0.5, 0.5, ((1, 32), (4, 4)), jnp.float32)
    bias = normal_values(arg_keys[2], (CH,), 0.5, 3.0, ((0, 4),), jnp.float32)
    return dict(field=field, spectral_weights=spectral_weights, bias=bias)


highest = lax.Precision.HIGHEST


def dft_tables(count_modes, count_cells, length, offset):
    mode_ids = jnp.arange(count_modes).astype(jnp.int32)[:, None]
    cell_ids = (jnp.arange(count_cells).astype(jnp.int32) + offset)[None, :]
    angles = 2.0 * math.pi * ((mode_ids * cell_ids) % length).astype(jnp.float32) / length
    return jnp.cos(angles), jnp.sin(angles)


def zt_angles():
    cell_ids = jnp.arange(ZT).astype(jnp.int32)[:, None]
    depth_pos = cell_ids // GT
    time_pos = cell_ids % GT
    mode_ids = jnp.arange(KQ).astype(jnp.int32)[None, :]
    depth_mode = mode_ids // MT
    time_mode = mode_ids % MT
    counted = ((depth_mode * depth_pos) % GZ) * GT + ((time_mode * time_pos) % GT) * GZ
    return 2.0 * math.pi * counted.astype(jnp.float32) / (GZ * GT)


def forward_table():
    angles = zt_angles()
    return jnp.stack([jnp.cos(angles), -jnp.sin(angles)], axis=2).reshape(ZT, 2 * KQ)


def inverse_table():
    angles = zt_angles().T
    time_mode = jnp.arange(KQ).astype(jnp.int32) % MT
    weighting = jnp.where(time_mode == 0, 1.0, 2.0).astype(jnp.float32) / (GX * GY * GZ * GT)
    weighting = weighting[:, None]
    return jnp.stack([weighting * jnp.cos(angles), -weighting * jnp.sin(angles)], axis=1).reshape(2 * KQ, ZT)


def complex_dft(values, along, cosines, sines, direction):
    cos_part = jnp.moveaxis(jnp.tensordot(cosines, values, axes=((1,), (along,)), precision=highest), 0, along)
    sin_part = jnp.moveaxis(jnp.tensordot(sines, values, axes=((1,), (along,)), precision=highest), 0, along)
    real_part = cos_part[:, :, :, 0] - direction * sin_part[:, :, :, 1]
    imag_part = cos_part[:, :, :, 1] + direction * sin_part[:, :, :, 0]
    return jnp.stack([real_part, imag_part], axis=3)


def mix_modes(spectrum, weights):
    spec_real = spectrum[:, :, :, 0]
    spec_imag = spectrum[:, :, :, 1]
    weight_real = weights[0]
    weight_imag = weights[1]
    real_part = jnp.einsum('abqi,qabio->abqo', spec_real, weight_real, precision=highest) - jnp.einsum('abqi,qabio->abqo', spec_imag, weight_imag, precision=highest)
    imag_part = jnp.einsum('abqi,qabio->abqo', spec_real, weight_imag, precision=highest) + jnp.einsum('abqi,qabio->abqo', spec_imag, weight_real, precision=highest)
    return jnp.stack([real_part, imag_part], axis=3)


def reference(field, spectral_weights, bias):
    zt_forward = forward_table()

    def forward_plane(one_plane):
        return jnp.einsum('ycs,sk->ykc', one_plane.astype(jnp.float32), zt_forward, precision=highest)

    zt_modes = lax.map(forward_plane, field).reshape(GX, GY, KQ, 2, CH)
    cos_y, sin_y = dft_tables(MY, GY, GY, 0)
    cos_x, sin_x = dft_tables(MX, GX, GX, 0)
    spectrum = complex_dft(complex_dft(zt_modes, 1, cos_y, sin_y, -1.0), 0, cos_x, sin_x, -1.0)
    mixed_modes = mix_modes(spectrum, spectral_weights)
    spatial = complex_dft(mixed_modes, 0, cos_x.T, sin_x.T, 1.0)
    returned = complex_dft(spatial, 1, cos_y.T, sin_y.T, 1.0).reshape(GX, GY, 2 * KQ, CH)
    zt_inverse = inverse_table()

    def inverse_plane(pairing):
        modes_plane, field_plane = pairing
        branch = jnp.einsum('ykc,ks->ycs', modes_plane, zt_inverse, precision=highest)
        return field_plane.astype(jnp.float32) + jax.nn.gelu(branch + bias[None, :, None], approximate=False)

    return lax.map(inverse_plane, (returned, field))
```

```python
import functools
import math

import jax
import jax.numpy as jnp
import ml_dtypes
import numpy as np
from jax import lax
from jax.experimental import pallas as pl
from jax.experimental.pallas import tpu as pltpu
from jax.sharding import PartitionSpec as P

GX, GY, GZ, GT = 64, 64, 32, 16
MX, MY, MT = 8, 8, 8
KQ, ZT = 64, 512
SLABS, CHANS = 32, 4
XL = GX // SLABS
QL = KQ // SLABS
CL = 32
LANES = 128
BLOCK = 16
MESH = pl.DeviceIdType.MESH
MIB = 1 << 20

GELU_Q = (
    7.97884216e-01,
    3.63342835e-02,
    -3.31299940e-05,
    -5.52401584e-05,
    3.96910946e-06,
    -1.33446409e-07,
    1.80561642e-09,
)
GELU_H = tuple(c * 2.0 * 4.0**k for k, c in enumerate(GELU_Q))


def split_bf16(table):
    high = table.astype(np.float32).astype(ml_dtypes.bfloat16)
    low = (table - high.astype(np.float64)).astype(np.float32).astype(ml_dtypes.bfloat16)
    return high, low


def zt_angles():
    cells = np.arange(ZT)[:, None]
    lanes = np.arange(KQ)[None, :]
    modes = (lanes % SLABS) * QL + lanes // SLABS
    counted = (modes // MT) * (cells // GT) % GZ * GT + (modes % MT) * (cells % GT) % GT * GZ
    return 2.0 * math.pi * counted / (GZ * GT), modes


def forward_zt_table():
    angles, _ = zt_angles()
    high, low = split_bf16(np.concatenate([np.cos(angles), -np.sin(angles)], axis=1))
    return np.concatenate([high, low], axis=1)


def inverse_zt_table():
    angles, modes = zt_angles()
    weight = np.where(modes % MT == 0, 1.0, 2.0) / (GX * GY * GZ * GT) / 2.0
    table = np.concatenate([weight * np.cos(angles), -weight * np.sin(angles)], axis=1).T
    high, low = split_bf16(table)
    return np.concatenate([high, high, low], axis=0)


def forward_x_table():
    angles = 2.0 * math.pi * (np.arange(MX)[:, None] * np.arange(GX)[None, :] % GX) / GX
    cos, sin = np.cos(angles), np.sin(angles)
    real = np.concatenate([cos, sin], axis=1)
    imag = np.concatenate([-sin, cos], axis=1)
    return np.stack([real, imag], axis=1).reshape(2 * MX, 2 * GX).astype(np.float32)


def inverse_x_table():
    angles = 2.0 * math.pi * (np.arange(GX)[:, None] * np.arange(MX)[None, :] % GX) / GX
    cos, sin = np.cos(angles), np.sin(angles)
    real = np.stack([cos, -sin], axis=2).reshape(GX, 2 * MX)
    imag = np.stack([sin, cos], axis=2).reshape(GX, 2 * MX)
    return np.concatenate([real, imag], axis=0).astype(np.float32)


def cos_y(k, y):
    return math.cos(2.0 * math.pi * (k * y % GY) / GY)


def sin_y(k, y):
    return math.sin(2.0 * math.pi * (k * y % GY) / GY)


def dot(a, b, precision=None):
    return jnp.dot(a, b, preferred_element_type=jnp.float32, precision=precision)


def total(terms):
    terms = list(terms)
    while len(terms) > 1:
        terms = [
            terms[i] + terms[i + 1] if i + 1 < len(terms) else terms[i]
            for i in range(0, len(terms), 2)
        ]
    return terms[0]


def rotate_parts(values, sign):
    lane = lax.broadcasted_iota(jnp.int32, values.shape, values.ndim - 1)
    swapped = pltpu.roll(values, LANES // 2, values.ndim - 1)
    return jnp.where(lane < LANES // 2, sign, -sign) * swapped


def forward_kernel(field_ref, table_ref, out_ref, modes_ref, kept_ref):
    plane, chunk = pl.program_id(0), pl.program_id(1)
    chunks = pl.num_programs(1)
    rows_y = field_ref.shape[1]
    both = dot(field_ref[...].reshape(rows_y * CL, ZT), table_ref[...])
    modes_ref[pl.ds(chunk * rows_y, rows_y)] = (both[:, :LANES] + both[:, LANES:]).reshape(
        rows_y, CL, LANES
    )

    @pl.when(chunk == chunks - 1)
    def _():
        half = GY // 2
        for group in range(CL // 8):
            rows = pl.ds(group * 8, 8)

            def load(y):
                return modes_ref[y, rows, :]

            first, middle = load(0), load(half)
            even, odd = first + middle, first - middle
            cosines = [even if k % 2 == 0 else odd for k in range(MY)]
            first, middle = load(half // 2), load(half // 2 + half)
            even, odd = first + middle, first - middle
            sines = [None] * MY
            for k in range(MY):
                if k % 2 == 0:
                    cosines[k] = cosines[k] + (even if k % 4 == 0 else -even)
                else:
                    sines[k] = odd if k % 4 == 1 else -odd
            for y in range(1, half // 2):
                a, b, c, d = load(y), load(GY - y), load(half - y), load(half + y)
                sum1, dif1, sum2, dif2 = a + b, a - b, c + d, c - d
                for_even, for_odd = sum1 + sum2, sum1 - sum2
                sin_odd, sin_even = dif1 + dif2, dif1 - dif2
                for k in range(MY):
                    cosines[k] = cosines[k] + cos_y(k, y) * (for_even if k % 2 == 0 else for_odd)
                    if k > 0:
                        term = sin_y(k, y) * (sin_even if k % 2 == 0 else sin_odd)
                        sines[k] = term if sines[k] is None else sines[k] + term
            for k in range(MY):
                value = cosines[k]
                if k > 0:
                    value = value + rotate_parts(sines[k], 1.0)
                kept_ref[pl.ds(k * CL + group * 8, 8), :] = value
        for ky_half in range(2):
            turned = kept_ref[pl.ds(ky_half * LANES, LANES), :].T
            for part in range(4):
                for owners in range(SLABS // 8):
                    start = owners * 8 * BLOCK + plane * 8 + ky_half * 4 + part
                    out_ref[pl.ds(start, 8, stride=BLOCK), :] = turned[
                        part * SLABS + owners * 8 : part * SLABS + owners * 8 + 8
                    ]


def forward(field, table):
    rows_y = 16
    return pl.pallas_call(
        forward_kernel,
        grid=(XL, GY // rows_y),
        in_specs=[
            pl.BlockSpec((1, rows_y, CL, ZT), lambda x, y: (x, y, 0, 0)),
            pl.BlockSpec((ZT, 2 * LANES), lambda x, y: (0, 0)),
        ],
        out_specs=pl.BlockSpec((SLABS * BLOCK, LANES), lambda x, y: (0, 0)),
        out_shape=jax.ShapeDtypeStruct((SLABS * BLOCK, LANES), jnp.float32),
        scratch_shapes=[
            pltpu.VMEM((GY, CL, LANES), jnp.float32),
            pltpu.VMEM((MY * CL, LANES), jnp.float32),
        ],
        compiler_params=pltpu.CompilerParams(vmem_limit_bytes=32 * MIB),
    )(field, table)


def exchange_kernel(
    ready_ref,
    weights_ref,
    x_forward_ref,
    x_inverse_ref,
    out_ref,
    arrived,
    staged,
    high_ref,
    low_ref,
    spectrum_ref,
    partial_ref,
    parcels,
    parcels_in,
    outgoing,
    weight_sem,
    local_sem,
    send_sem,
    recv_sem,
    chan_send,
    chan_recv,
    back_send,
    back_recv,
):
    slab, chan = lax.axis_index("slab"), lax.axis_index("chan")
    highest = lax.Precision.HIGHEST

    def weight_copy(part):
        return pltpu.make_async_copy(weights_ref.at[part], staged.at[part], weight_sem.at[part])

    for part in range(2):
        weight_copy(part).start()

    barrier = pltpu.get_barrier_semaphore()

    def greet_slab(i, carry):
        pl.semaphore_signal(
            barrier, inc=1, device_id=(lax.rem(slab + i, SLABS), chan), device_id_type=MESH
        )
        return carry

    def greet_chan(i, carry):
        pl.semaphore_signal(
            barrier, inc=1, device_id=(slab, lax.rem(chan + i, CHANS)), device_id_type=MESH
        )
        return carry

    lax.fori_loop(1, SLABS, greet_slab, 0)
    lax.fori_loop(1, CHANS, greet_chan, 0)
    pl.semaphore_wait(barrier, SLABS + CHANS - 2)

    def block_of(owner):
        return pl.ds(pl.multiple_of(owner * BLOCK, BLOCK), BLOCK)

    def send_all(source, target, send, recv):
        def step(i, carry):
            other = lax.rem(slab + i, SLABS)
            pltpu.make_async_remote_copy(
                src_ref=source.at[block_of(other)],
                dst_ref=target.at[block_of(slab)],
                send_sem=send,
                recv_sem=recv,
                device_id=(other, chan),
                device_id_type=MESH,
            ).start()
            return carry

        lax.fori_loop(1, SLABS, step, 0)
        own = pltpu.make_async_copy(
            source.at[block_of(slab)], target.at[block_of(slab)], local_sem
        )
        own.start()
        return own

    def wait_bytes(ref, rows, sem):
        piece = ref.at[pl.ds(0, rows)]
        pltpu.make_async_copy(piece, piece, sem).wait()

    own = send_all(ready_ref, arrived, send_sem, recv_sem)

    for part in range(2):
        weight_copy(part).wait()

        def split_weights(i, carry, part=part):
            value = staged[part, i]
            high = value.astype(jnp.bfloat16)
            low = (value - high.astype(jnp.float32)).astype(jnp.bfloat16)
            high_ref[i, :, part * LANES : (part + 1) * LANES] = high
            low_ref[i, :, part * LANES : (part + 1) * LANES] = low
            return carry

        lax.fori_loop(0, QL * MX, split_weights, 0)

    own.wait()
    rows_sent = (SLABS - 1) * BLOCK
    wait_bytes(arrived, rows_sent, recv_sem)

    columns = []
    for parity in range(QL):
        for ky_half in range(2):
            columns.append(
                jnp.concatenate(
                    [
                        arrived[pl.ds(ky_half * 4 + part * 2 + parity, GX, stride=8), :]
                        for part in range(2)
                    ],
                    axis=0,
                )
            )
    spectrum = dot(x_forward_ref[...], jnp.concatenate(columns, axis=1), highest)
    for parity in range(QL):
        spectrum_ref[parity] = spectrum[:, parity * 256 : (parity + 1) * 256]

    row = lax.broadcasted_iota(jnp.int32, (MY, 256), 0)
    lane = lax.broadcasted_iota(jnp.int32, (MY, 256), 1)
    own_ky = row == lane // CL

    def mix(parity, carry):
        for kx in range(MX):
            spread = jnp.concatenate(
                [
                    jnp.where(own_ky, spectrum_ref[parity, pl.ds(2 * kx + part, 1), :], 0.0)
                    for part in range(2)
                ],
                axis=0,
            )
            high = spread.astype(jnp.bfloat16)
            low = (spread - high.astype(jnp.float32)).astype(jnp.bfloat16)
            main = dot(jnp.concatenate([high, low], axis=0), high_ref[parity * MX + kx])
            rest = dot(high, low_ref[parity * MX + kx])
            both = main[:16] + main[16:] + rest
            real = both[:8, :LANES] - both[8:, LANES:]
            imag = both[:8, LANES:] + both[8:, :LANES]
            partial_ref[pl.ds(parity * LANES + kx * 16, 8), :] = real
            partial_ref[pl.ds(parity * LANES + kx * 16 + 8, 8), :] = imag
        return carry

    lax.fori_loop(0, QL, mix, 0)

    lane = lax.broadcasted_iota(jnp.int32, (8, LANES), 1) // CL
    for parity in range(QL):
        for ky_half in range(2):
            for rows in range(2):
                pieces = [
                    partial_ref[
                        pl.ds(parity * LANES + rows * 64 + ky_half * 4 + ky, 8, stride=8), :
                    ]
                    for ky in range(4)
                ]
                for other in range(CHANS):
                    packed = None
                    for ky in range(4):
                        shift = (ky - other) % CHANS * CL
                        moved = pltpu.roll(pieces[ky], shift, 1) if shift else pieces[ky]
                        packed = moved if packed is None else jnp.where(lane == ky, moved, packed)
                    start = (parity * 2 + ky_half) * 16 + rows * 8
                    parcels[other, pl.ds(start, 8), :] = packed

    chan_copies = []
    for i in range(1, CHANS):
        other = lax.rem(chan + i, CHANS)
        copy = pltpu.make_async_remote_copy(
            src_ref=parcels.at[other],
            dst_ref=parcels_in.at[i - 1],
            send_sem=chan_send.at[i - 1],
            recv_sem=chan_recv.at[i - 1],
            device_id=(slab, other),
            device_id_type=MESH,
        )
        copy.start()
        chan_copies.append(copy)
    mixed = parcels[chan]
    for i in range(1, CHANS):
        chan_copies[i - 1].wait_recv()
        mixed = mixed + parcels_in[i - 1]

    side = jnp.concatenate([mixed[16 * i : 16 * i + 16] for i in range(4)], axis=1)
    spatial = dot(x_inverse_ref[...], side, highest)
    for parity in range(QL):
        for ky_half in range(2):
            for part in range(2):
                at = parity * 2 + ky_half
                outgoing[pl.ds(ky_half * 4 + part * 2 + parity, GX, stride=8), :] = spatial[
                    part * GX : (part + 1) * GX, at * LANES : (at + 1) * LANES
                ]

    own = send_all(outgoing, out_ref, back_send, back_recv)
    own.wait()
    for copy in chan_copies:
        copy.wait_send()
    wait_bytes(ready_ref, rows_sent, send_sem)
    wait_bytes(out_ref, rows_sent, back_recv)
    wait_bytes(outgoing, rows_sent, back_send)


def exchange(ready, weights, x_forward, x_inverse):
    vmem = pl.BlockSpec(memory_space=pltpu.VMEM)
    rows = SLABS * BLOCK
    return pl.pallas_call(
        exchange_kernel,
        in_specs=[vmem, pl.BlockSpec(memory_space=pl.ANY), vmem, vmem],
        out_specs=vmem,
        out_shape=jax.ShapeDtypeStruct((rows, LANES), jnp.float32),
        scratch_shapes=[
            pltpu.VMEM((rows, LANES), jnp.float32),
            pltpu.VMEM((2, QL * MX, 256, LANES), jnp.float32),
            pltpu.VMEM((QL * MX, 256, 256), jnp.bfloat16),
            pltpu.VMEM((QL * MX, 256, 256), jnp.bfloat16),
            pltpu.VMEM((QL, 16, 256), jnp.float32),
            pltpu.VMEM((QL * LANES, LANES), jnp.float32),
            pltpu.VMEM((CHANS, 64, LANES), jnp.float32),
            pltpu.VMEM((CHANS - 1, 64, LANES), jnp.float32),
            pltpu.VMEM((rows, LANES), jnp.float32),
            pltpu.SemaphoreType.DMA((2,)),
            pltpu.SemaphoreType.DMA,
            pltpu.SemaphoreType.DMA,
            pltpu.SemaphoreType.DMA,
            pltpu.SemaphoreType.DMA((CHANS - 1,)),
            pltpu.SemaphoreType.DMA((CHANS - 1,)),
            pltpu.SemaphoreType.DMA,
            pltpu.SemaphoreType.DMA,
        ],
        compiler_params=pltpu.CompilerParams(
            collective_id=0, has_side_effects=True, vmem_limit_bytes=40 * MIB
        ),
    )(ready, weights, x_forward, x_inverse)


def inverse_kernel(modes_ref, field_ref, table_ref, bias_ref, out_ref, lhs_ref):
    plane, chunk = pl.program_id(0), pl.program_id(1)
    rows_y = field_ref.shape[1]

    @pl.when(chunk == 0)
    def _():
        turned = []
        for ky_half in range(2):
            piece = jnp.concatenate(
                [
                    modes_ref[
                        pl.ds(plane * 8 + ky_half * 4 + part, SLABS, stride=BLOCK), :
                    ]
                    for part in range(4)
                ],
                axis=0,
            )
            turned.append(piece.T)
        for group in range(CL // 16):
            kept = [
                turned[k // 4][k % 4 * CL + group * 16 : k % 4 * CL + group * 16 + 16]
                for k in range(MY)
            ]
            spun = [None] + [rotate_parts(kept[k], -1.0) for k in range(1, MY)]

            def put(y, value):
                high = value.astype(jnp.bfloat16)
                low = (value - high.astype(jnp.float32)).astype(jnp.bfloat16)
                rows = pl.ds(y * CL + group * 16, 16)
                lhs_ref[rows, :LANES] = high
                lhs_ref[rows, LANES:] = low

            half = GY // 2
            even, odd = total(kept[0::2]), total(kept[1::2])
            put(0, even + odd)
            put(half, even - odd)
            even = (kept[0] + kept[4]) - (kept[2] + kept[6])
            odd = (spun[1] + spun[5]) - (spun[3] + spun[7])
            put(half // 2, even + odd)
            put(half // 2 + half, even - odd)
            for y in range(1, half // 2):
                cos_even = total([kept[0]] + [cos_y(k, y) * kept[k] for k in (2, 4, 6)])
                cos_odd = total([cos_y(k, y) * kept[k] for k in (1, 3, 5, 7)])
                sin_even = total([sin_y(k, y) * spun[k] for k in (2, 4, 6)])
                sin_odd = total([sin_y(k, y) * spun[k] for k in (1, 3, 5, 7)])
                cos_sum, cos_dif = cos_even + cos_odd, cos_even - cos_odd
                sin_sum, sin_dif = sin_even + sin_odd, sin_odd - sin_even
                put(y, cos_sum + sin_sum)
                put(GY - y, cos_sum - sin_sum)
                put(half - y, cos_dif + sin_dif)
                put(half + y, cos_dif - sin_dif)

    bias = bias_ref[...]
    step_y = 4

    def step(i, carry):
        start = pl.multiple_of(chunk * (rows_y * CL) + i * (step_y * CL), step_y * CL)
        high = lhs_ref[pl.ds(start, step_y * CL), :LANES]
        low = lhs_ref[pl.ds(start, step_y * CL), LANES:]
        branch = dot(jnp.concatenate([high, low, high], axis=1), table_ref[...])
        h = branch.reshape(step_y, CL, ZT) + bias[None]
        square = h * h
        poly = GELU_H[6]
        for coefficient in GELU_H[5::-1]:
            poly = poly * square + coefficient
        value = h + h * jnp.tanh(h * poly)
        at = pl.ds(i * step_y, step_y)
        out_ref[0, at] = field_ref[0, at].astype(jnp.float32) + value
        return carry

    lax.fori_loop(0, rows_y // step_y, step, 0)


def inverse(modes, field, table, bias):
    rows_y = 16
    return pl.pallas_call(
        inverse_kernel,
        grid=(XL, GY // rows_y),
        in_specs=[
            pl.BlockSpec((SLABS * BLOCK, LANES), lambda x, y: (0, 0)),
            pl.BlockSpec((1, rows_y, CL, ZT), lambda x, y: (x, y, 0, 0)),
            pl.BlockSpec((3 * LANES, ZT), lambda x, y: (0, 0)),
            pl.BlockSpec((CL, 1), lambda x, y: (0, 0)),
        ],
        out_specs=pl.BlockSpec((1, rows_y, CL, ZT), lambda x, y: (x, y, 0, 0)),
        out_shape=jax.ShapeDtypeStruct((XL, GY, CL, ZT), jnp.float32),
        scratch_shapes=[pltpu.VMEM((GY * CL, 2 * LANES), jnp.bfloat16)],
        compiler_params=pltpu.CompilerParams(vmem_limit_bytes=32 * MIB),
    )(modes, field, table, bias)


def shards(field, spectral_weights, bias):
    weights = spectral_weights.reshape(2, QL * MX, MY * CL, LANES)
    ready = forward(field, jnp.asarray(forward_zt_table()))
    back = exchange(
        ready, weights, jnp.asarray(forward_x_table()), jnp.asarray(inverse_x_table())
    )
    half_bias = (0.5 * bias).reshape(CL, 1)
    return inverse(back, field, jnp.asarray(inverse_zt_table()), half_bias)


def solution(mesh):
    return jax.shard_map(
        shards,
        mesh=mesh,
        in_specs=(
            P("slab", None, "chan", None),
            P(None, "slab", None, None, "chan", None),
            P("chan"),
        ),
        out_specs=P("slab", None, "chan", None),
        check_vma=False,
    )
```

```python
import functools
import math

import jax
import jax.numpy as jnp
import ml_dtypes
import numpy as np
from jax import lax
from jax.experimental import pallas as pl
from jax.experimental.pallas import tpu as pltpu
from jax.sharding import PartitionSpec as P

GX, GY, GZ, GT = 64, 64, 32, 16
MX, MY, MT = 8, 8, 8
KQ, ZT = 64, 512
SLABS, CHANS = 32, 4
XL = GX // SLABS
QL = KQ // SLABS
CL = 32
LANES = 128
BLOCK = 16
MESH = pl.DeviceIdType.MESH
VMEM_LIMIT = 62 << 20
CHUNKS = 2

DC_SCALE = float(GX * GY * GZ * GT)
ROOT_HALF = math.sqrt(0.5)


def split_bf16(table):
    high = table.astype(np.float32).astype(ml_dtypes.bfloat16)
    low = (table - high.astype(np.float64)).astype(np.float32).astype(ml_dtypes.bfloat16)
    return high, low


def zt_angles():
    cells = np.arange(ZT)[:, None]
    lanes = np.arange(KQ)[None, :]
    modes = (lanes % SLABS) * QL + lanes // SLABS
    counted = (modes // MT) * (cells // GT) % GZ * GT + (modes % MT) * (cells % GT) % GT * GZ
    return 2.0 * math.pi * counted / (GZ * GT), modes


def forward_zt_table():
    angles, _ = zt_angles()
    high, low = split_bf16(np.concatenate([np.cos(angles), -np.sin(angles)], axis=1))
    return np.concatenate([high, low], axis=1)


def inverse_zt_table():
    angles, modes = zt_angles()
    weight = np.where(modes % MT == 0, 1.0, 2.0) * (ROOT_HALF / (GX * GY * GZ * GT))
    table = np.concatenate([weight * np.cos(angles), -weight * np.sin(angles)], axis=1).T
    high, low = split_bf16(table)
    return np.concatenate([high, high, low], axis=0)


def forward_x_table():
    angles = 2.0 * math.pi * (np.arange(MX)[:, None] * np.arange(GX)[None, :] % GX) / GX
    cos, sin = np.cos(angles), np.sin(angles)
    real = np.concatenate([cos, sin], axis=1)
    imag = np.concatenate([-sin, cos], axis=1)
    return np.stack([real, imag], axis=1).reshape(2 * MX, 2 * GX).astype(np.float32)


def inverse_x_table():
    angles = 2.0 * math.pi * (np.arange(GX)[:, None] * np.arange(MX)[None, :] % GX) / GX
    cos, sin = np.cos(angles), np.sin(angles)
    real = np.stack([cos, -sin], axis=2).reshape(GX, 2 * MX)
    imag = np.stack([sin, cos], axis=2).reshape(GX, 2 * MX)
    return np.concatenate([real, imag], axis=0).astype(np.float32)


def cos_y(k, y):
    return math.cos(2.0 * math.pi * (k * y % GY) / GY)


def sin_y(k, y):
    return math.sin(2.0 * math.pi * (k * y % GY) / GY)


def dot(a, b, precision=None):
    return jnp.dot(a, b, preferred_element_type=jnp.float32, precision=precision)


def total(terms):
    terms = list(terms)
    while len(terms) > 1:
        terms = [
            terms[i] + terms[i + 1] if i + 1 < len(terms) else terms[i]
            for i in range(0, len(terms), 2)
        ]
    return terms[0]


def rotate_parts(values, sign):
    lane = lax.broadcasted_iota(jnp.int32, values.shape, values.ndim - 1)
    swapped = pltpu.roll(values, LANES // 2, values.ndim - 1)
    return jnp.where(lane < LANES // 2, sign, -sign) * swapped


def forward_y(modes_ref, kept_ref, out_ref, plane):
    half = GY // 2
    for group in range(CL // 8):
        rows = pl.ds(group * 8, 8)

        def load(y):
            return modes_ref[y, rows, :]

        first, middle = load(0), load(half)
        even, odd = first + middle, first - middle
        cosines = [even if k % 2 == 0 else odd for k in range(MY)]
        first, middle = load(half // 2), load(half // 2 + half)
        even, odd = first + middle, first - middle
        sines = [None] * MY
        for k in range(MY):
            if k % 2 == 0:
                cosines[k] = cosines[k] + (even if k % 4 == 0 else -even)
            else:
                sines[k] = odd if k % 4 == 1 else -odd
        for y in range(1, half // 2):
            a, b, c, d = load(y), load(GY - y), load(half - y), load(half + y)
            sum1, dif1, sum2, dif2 = a + b, a - b, c + d, c - d
            for_even, for_odd = sum1 + sum2, sum1 - sum2
            sin_odd, sin_even = dif1 + dif2, dif1 - dif2
            for k in range(MY):
                cosines[k] = cosines[k] + cos_y(k, y) * (for_even if k % 2 == 0 else for_odd)
                if k > 0:
                    term = sin_y(k, y) * (sin_even if k % 2 == 0 else sin_odd)
                    sines[k] = term if sines[k] is None else sines[k] + term
        for k in range(MY):
            value = cosines[k]
            if k > 0:
                value = value + rotate_parts(sines[k], 1.0)
            kept_ref[pl.ds(k * CL + group * 8, 8), :] = value
    for ky_half in range(2):
        turned = kept_ref[pl.ds(ky_half * LANES, LANES), :].T
        for part in range(4):
            for owners in range(SLABS // 8):
                start = owners * 8 * BLOCK + plane * 8 + ky_half * 4 + part
                out_ref[pl.ds(start, 8, stride=BLOCK), :] = turned[
                    part * SLABS + owners * 8 : part * SLABS + owners * 8 + 8
                ]


def exchange_kernel(
    field_ref,
    weights_ref,
    zt_hbm,
    x_forward_hbm,
    x_inverse_hbm,
    out_ref,
    zt_ref,
    x_forward_ref,
    x_inverse_ref,
    field_in,
    modes_ref,
    kept_ref,
    ready_ref,
    arrived,
    staged,
    high_ref,
    low_ref,
    spectrum_ref,
    partial_ref,
    parcels,
    parcels_in,
    outgoing,
    table_sem,
    field_sem,
    weight_sem,
    local_sem,
    send_sem,
    recv_sem,
    chan_send,
    chan_recv,
    back_send,
    back_recv,
):
    slab, chan = lax.axis_index("slab"), lax.axis_index("chan")
    highest = lax.Precision.HIGHEST

    def weight_copy(part):
        return pltpu.make_async_copy(weights_ref.at[part], staged.at[part], weight_sem.at[part])

    chunk = GY // CHUNKS

    def field_copy(plane, piece):
        rows = pl.ds(piece * chunk, chunk)
        return pltpu.make_async_copy(
            field_ref.at[plane, rows], field_in.at[plane, rows], field_sem.at[plane, piece]
        )

    table_copies = [
        pltpu.make_async_copy(source, target, table_sem.at[i])
        for i, (source, target) in enumerate(
            [(zt_hbm, zt_ref), (x_forward_hbm, x_forward_ref), (x_inverse_hbm, x_inverse_ref)]
        )
    ]
    table_copies[0].start()
    for plane in range(XL):
        for piece in range(CHUNKS):
            field_copy(plane, piece).start()
    for copy in table_copies[1:]:
        copy.start()
    for part in range(2):
        weight_copy(part).start()

    barrier = pltpu.get_barrier_semaphore()

    def greet_slab(i, carry):
        pl.semaphore_signal(
            barrier, inc=1, device_id=(lax.rem(slab + i, SLABS), chan), device_id_type=MESH
        )
        return carry

    def greet_chan(i, carry):
        pl.semaphore_signal(
            barrier, inc=1, device_id=(slab, lax.rem(chan + i, CHANS)), device_id_type=MESH
        )
        return carry

    lax.fori_loop(1, SLABS, greet_slab, 0)
    lax.fori_loop(1, CHANS, greet_chan, 0)
    table_copies[0].wait()

    for plane in range(XL):
        for piece in range(CHUNKS):
            field_copy(plane, piece).wait()
            rows = pl.ds(piece * chunk, chunk)
            both = dot(field_in[plane, rows].reshape(chunk * CL, ZT), zt_ref[...])
            both = both[:, :LANES] + both[:, LANES:]
            modes_ref[rows] = both.reshape(chunk, CL, LANES)
        forward_y(modes_ref, kept_ref, ready_ref, plane)

    pl.semaphore_wait(barrier, SLABS + CHANS - 2)

    def block_of(owner):
        return pl.ds(pl.multiple_of(owner * BLOCK, BLOCK), BLOCK)

    def send_all(source, target, send, recv):
        def step(i, carry):
            other = lax.rem(slab + i, SLABS)
            pltpu.make_async_remote_copy(
                src_ref=source.at[block_of(other)],
                dst_ref=target.at[block_of(slab)],
                send_sem=send,
                recv_sem=recv,
                device_id=(other, chan),
                device_id_type=MESH,
            ).start()
            return carry

        lax.fori_loop(1, SLABS, step, 0)
        own = pltpu.make_async_copy(
            source.at[block_of(slab)], target.at[block_of(slab)], local_sem
        )
        own.start()
        return own

    def wait_bytes(ref, rows, sem):
        piece = ref.at[pl.ds(0, rows)]
        pltpu.make_async_copy(piece, piece, sem).wait()

    own = send_all(ready_ref, arrived, send_sem, recv_sem)

    for part in range(2):
        weight_copy(part).wait()

        def split_weights(i, carry, part=part):
            value = staged[part, i]
            high = value.astype(jnp.bfloat16)
            low = (value - high.astype(jnp.float32)).astype(jnp.bfloat16)
            high_ref[i, :, part * LANES : (part + 1) * LANES] = high
            low_ref[i, :, part * LANES : (part + 1) * LANES] = low
            return carry

        lax.fori_loop(0, QL * MX, split_weights, 0)

    for copy in table_copies[1:]:
        copy.wait()
    own.wait()
    rows_sent = (SLABS - 1) * BLOCK
    wait_bytes(arrived, rows_sent, recv_sem)

    columns = []
    for parity in range(QL):
        for ky_half in range(2):
            columns.append(
                jnp.concatenate(
                    [
                        arrived[pl.ds(ky_half * 4 + part * 2 + parity, GX, stride=8), :]
                        for part in range(2)
                    ],
                    axis=0,
                )
            )
    spectrum = dot(x_forward_ref[...], jnp.concatenate(columns, axis=1), highest)
    for parity in range(QL):
        spectrum_ref[parity] = spectrum[:, parity * 256 : (parity + 1) * 256]

    row = lax.broadcasted_iota(jnp.int32, (MY, 256), 0)
    lane = lax.broadcasted_iota(jnp.int32, (MY, 256), 1)
    own_ky = row == lane // CL

    def mix(parity, carry):
        for kx in range(MX):
            spread = jnp.concatenate(
                [
                    jnp.where(own_ky, spectrum_ref[parity, pl.ds(2 * kx + part, 1), :], 0.0)
                    for part in range(2)
                ],
                axis=0,
            )
            high = spread.astype(jnp.bfloat16)
            low = (spread - high.astype(jnp.float32)).astype(jnp.bfloat16)
            main = dot(jnp.concatenate([high, low], axis=0), high_ref[parity * MX + kx])
            rest = dot(high, low_ref[parity * MX + kx])
            both = main[:16] + main[16:] + rest
            real = both[:8, :LANES] - both[8:, LANES:]
            imag = both[:8, LANES:] + both[8:, :LANES]
            partial_ref[pl.ds(parity * LANES + kx * 16, 8), :] = real
            partial_ref[pl.ds(parity * LANES + kx * 16 + 8, 8), :] = imag
        return carry

    lax.fori_loop(0, QL, mix, 0)

    lane = lax.broadcasted_iota(jnp.int32, (8, LANES), 1) // CL
    for parity in range(QL):
        for ky_half in range(2):
            for rows in range(2):
                pieces = [
                    partial_ref[
                        pl.ds(parity * LANES + rows * 64 + ky_half * 4 + ky, 8, stride=8), :
                    ]
                    for ky in range(4)
                ]
                for other in range(CHANS):
                    packed = None
                    for ky in range(4):
                        shift = (ky - other) % CHANS * CL
                        moved = pltpu.roll(pieces[ky], shift, 1) if shift else pieces[ky]
                        packed = moved if packed is None else jnp.where(lane == ky, moved, packed)
                    start = (parity * 2 + ky_half) * 16 + rows * 8
                    parcels[other, pl.ds(start, 8), :] = packed

    chan_copies = []
    for i in range(1, CHANS):
        other = lax.rem(chan + i, CHANS)
        copy = pltpu.make_async_remote_copy(
            src_ref=parcels.at[other],
            dst_ref=parcels_in.at[i - 1],
            send_sem=chan_send.at[i - 1],
            recv_sem=chan_recv.at[i - 1],
            device_id=(slab, other),
            device_id_type=MESH,
        )
        copy.start()
        chan_copies.append(copy)
    mixed = parcels[chan]
    for i in range(1, CHANS):
        chan_copies[i - 1].wait_recv()
        mixed = mixed + parcels_in[i - 1]

    side = jnp.concatenate([mixed[16 * i : 16 * i + 16] for i in range(4)], axis=1)
    spatial = dot(x_inverse_ref[...], side, highest)
    for parity in range(QL):
        for ky_half in range(2):
            for part in range(2):
                at = parity * 2 + ky_half
                outgoing[pl.ds(ky_half * 4 + part * 2 + parity, GX, stride=8), :] = spatial[
                    part * GX : (part + 1) * GX, at * LANES : (at + 1) * LANES
                ]

    own = send_all(outgoing, out_ref, back_send, back_recv)
    own.wait()
    for copy in chan_copies:
        copy.wait_send()
    wait_bytes(ready_ref, rows_sent, send_sem)
    wait_bytes(out_ref, rows_sent, back_recv)
    wait_bytes(outgoing, rows_sent, back_send)


def exchange(field, weights, zt_table, x_forward, x_inverse):
    vmem = pl.BlockSpec(memory_space=pltpu.VMEM)
    hbm = pl.BlockSpec(memory_space=pl.ANY)
    rows = SLABS * BLOCK
    return pl.pallas_call(
        exchange_kernel,
        in_specs=[hbm] * 5,
        out_specs=vmem,
        out_shape=jax.ShapeDtypeStruct((rows, LANES), jnp.float32),
        scratch_shapes=[
            pltpu.VMEM((ZT, 2 * LANES), jnp.bfloat16),
            pltpu.VMEM((2 * MX, 2 * GX), jnp.float32),
            pltpu.VMEM((2 * GX, 2 * MX), jnp.float32),
            pltpu.VMEM((XL, GY, CL, ZT), jnp.bfloat16),
            pltpu.VMEM((GY, CL, LANES), jnp.float32),
            pltpu.VMEM((MY * CL, LANES), jnp.float32),
            pltpu.VMEM((rows, LANES), jnp.float32),
            pltpu.VMEM((rows, LANES), jnp.float32),
            pltpu.VMEM((2, QL * MX, 256, LANES), jnp.float32),
            pltpu.VMEM((QL * MX, 256, 256), jnp.bfloat16),
            pltpu.VMEM((QL * MX, 256, 256), jnp.bfloat16),
            pltpu.VMEM((QL, 16, 256), jnp.float32),
            pltpu.VMEM((QL * LANES, LANES), jnp.float32),
            pltpu.VMEM((CHANS, 64, LANES), jnp.float32),
            pltpu.VMEM((CHANS - 1, 64, LANES), jnp.float32),
            pltpu.VMEM((rows, LANES), jnp.float32),
            pltpu.SemaphoreType.DMA((3,)),
            pltpu.SemaphoreType.DMA((XL, CHUNKS)),
            pltpu.SemaphoreType.DMA((2,)),
            pltpu.SemaphoreType.DMA,
            pltpu.SemaphoreType.DMA,
            pltpu.SemaphoreType.DMA,
            pltpu.SemaphoreType.DMA((CHANS - 1,)),
            pltpu.SemaphoreType.DMA((CHANS - 1,)),
            pltpu.SemaphoreType.DMA,
            pltpu.SemaphoreType.DMA,
        ],
        compiler_params=pltpu.CompilerParams(
            collective_id=0, has_side_effects=True, vmem_limit_bytes=VMEM_LIMIT
        ),
    )(field, weights, zt_table, x_forward, x_inverse)


def inverse_kernel(modes_ref, field_ref, table_ref, bias_ref, out_ref, lhs_ref, shift_ref):
    plane, chunk = pl.program_id(0), pl.program_id(1)
    rows_y = field_ref.shape[1]

    @pl.when(chunk == 0)
    def _():
        shift_ref[...] = jnp.zeros_like(shift_ref)
        shift_ref[0:1, :CL] = bias_ref[...] * DC_SCALE
        turned = []
        for ky_half in range(2):
            piece = jnp.concatenate(
                [
                    modes_ref[
                        pl.ds(plane * 8 + ky_half * 4 + part, SLABS, stride=BLOCK), :
                    ]
                    for part in range(4)
                ],
                axis=0,
            )
            if ky_half == 0:
                piece = jnp.concatenate([piece[:8] + shift_ref[...], piece[8:]], axis=0)
            turned.append(piece.T)
        for group in range(CL // 16):
            kept = [
                turned[k // 4][k % 4 * CL + group * 16 : k % 4 * CL + group * 16 + 16]
                for k in range(MY)
            ]
            spun = [None] + [rotate_parts(kept[k], -1.0) for k in range(1, MY)]

            def put(y, value):
                high = value.astype(jnp.bfloat16)
                low = (value - high.astype(jnp.float32)).astype(jnp.bfloat16)
                rows = pl.ds(y * CL + group * 16, 16)
                lhs_ref[rows, :LANES] = high
                lhs_ref[rows, LANES:] = low

            half = GY // 2
            even, odd = total(kept[0::2]), total(kept[1::2])
            put(0, even + odd)
            put(half, even - odd)
            even = (kept[0] + kept[4]) - (kept[2] + kept[6])
            odd = (spun[1] + spun[5]) - (spun[3] + spun[7])
            put(half // 2, even + odd)
            put(half // 2 + half, even - odd)
            for y in range(1, half // 2):
                cos_even = total([kept[0]] + [cos_y(k, y) * kept[k] for k in (2, 4, 6)])
                cos_odd = total([cos_y(k, y) * kept[k] for k in (1, 3, 5, 7)])
                sin_even = total([sin_y(k, y) * spun[k] for k in (2, 4, 6)])
                sin_odd = total([sin_y(k, y) * spun[k] for k in (1, 3, 5, 7)])
                cos_sum, cos_dif = cos_even + cos_odd, cos_even - cos_odd
                sin_sum, sin_dif = sin_even + sin_odd, sin_odd - sin_even
                put(y, cos_sum + sin_sum)
                put(GY - y, cos_sum - sin_sum)
                put(half - y, cos_dif + sin_dif)
                put(half + y, cos_dif - sin_dif)

    rows = pl.ds(pl.multiple_of(chunk * (rows_y * CL), rows_y * CL), rows_y * CL)
    high, low = lhs_ref[rows, :LANES], lhs_ref[rows, LANES:]
    scaled = dot(jnp.concatenate([high, low, high], axis=1), table_ref[...])
    value = (ROOT_HALF * scaled) * (1.0 + lax.erf(scaled))
    out_ref[0] = field_ref[0].astype(jnp.float32) + value.reshape(rows_y, CL, ZT)


def inverse(modes, field, table, bias):
    rows_y = 16
    return pl.pallas_call(
        inverse_kernel,
        grid=(XL, GY // rows_y),
        in_specs=[
            pl.BlockSpec((SLABS * BLOCK, LANES), lambda x, y: (0, 0)),
            pl.BlockSpec((1, rows_y, CL, ZT), lambda x, y: (x, y, 0, 0)),
            pl.BlockSpec((3 * LANES, ZT), lambda x, y: (0, 0)),
            pl.BlockSpec((1, CL), lambda x, y: (0, 0)),
        ],
        out_specs=pl.BlockSpec((1, rows_y, CL, ZT), lambda x, y: (x, y, 0, 0)),
        out_shape=jax.ShapeDtypeStruct((XL, GY, CL, ZT), jnp.float32),
        scratch_shapes=[
            pltpu.VMEM((GY * CL, 2 * LANES), jnp.bfloat16),
            pltpu.VMEM((8, LANES), jnp.float32),
        ],
        compiler_params=pltpu.CompilerParams(vmem_limit_bytes=VMEM_LIMIT),
    )(modes, field, table, bias)


def shards(field, spectral_weights, bias):
    weights = spectral_weights.reshape(2, QL * MX, MY * CL, LANES)
    back = exchange(
        field,
        weights,
        jnp.asarray(forward_zt_table()),
        jnp.asarray(forward_x_table()),
        jnp.asarray(inverse_x_table()),
    )
    return inverse(back, field, jnp.asarray(inverse_zt_table()), bias.reshape(1, CL))


def solution(mesh):
    return jax.shard_map(
        shards,
        mesh=mesh,
        in_specs=(
            P("slab", None, "chan", None),
            P(None, "slab", None, None, "chan", None),
            P("chan"),
        ),
        out_specs=P("slab", None, "chan", None),
        check_vma=False,
    )
```

```python
import functools
import math

import jax
import jax.numpy as jnp
import ml_dtypes
import numpy as np
from jax import lax
from jax.experimental import pallas as pl
from jax.experimental.pallas import tpu as pltpu
from jax.sharding import PartitionSpec as P

GX, GY, GZ, GT = 64, 64, 32, 16
MX, MY, MT = 8, 8, 8
KQ, ZT = 64, 512
SLABS, CHANS = 32, 4
XL = GX // SLABS
QL = KQ // SLABS
CL = 32
LANES = 128
BLOCK = 16
MESH = pl.DeviceIdType.MESH
VMEM_LIMIT = 40 << 20
CHUNKS = 2

DC_SCALE = float(GX * GY * GZ * GT)
ROOT_HALF = math.sqrt(0.5)


def split_bf16(table):
    high = table.astype(np.float32).astype(ml_dtypes.bfloat16)
    low = (table - high.astype(np.float64)).astype(np.float32).astype(ml_dtypes.bfloat16)
    return high, low


def zt_angles():
    cells = np.arange(ZT)[:, None]
    lanes = np.arange(KQ)[None, :]
    modes = (lanes % SLABS) * QL + lanes // SLABS
    counted = (modes // MT) * (cells // GT) % GZ * GT + (modes % MT) * (cells % GT) % GT * GZ
    return 2.0 * math.pi * counted / (GZ * GT), modes


def forward_zt_table():
    angles, _ = zt_angles()
    high, low = split_bf16(np.concatenate([np.cos(angles), -np.sin(angles)], axis=1))
    return np.concatenate([high, low], axis=1)


def inverse_zt_table():
    cells = np.arange(ZT // 2)[None, :]
    row = np.arange(KQ // 2)[:, None]
    tables = []
    for odd in range(2):
        kz = 2 * (row // 4 % 4) + odd
        kt = 2 * (row % 4) + row // 16
        counted = kz * (cells // GT) % GZ * GT + kt * (cells % GT) % GT * GZ
        angles = 2.0 * math.pi * counted / (GZ * GT)
        weight = np.where(kt == 0, 1.0, 2.0) * (ROOT_HALF / (GX * GY * GZ * GT))
        tables.append(np.concatenate([weight * np.cos(angles), -weight * np.sin(angles)], axis=0))
    (even, even_low), (odd, odd_low) = map(split_bf16, tables)
    zero = np.zeros_like(even)
    return np.concatenate(
        [
            np.concatenate([even, even, even_low, zero], axis=0),
            np.concatenate([zero, odd_low, odd, odd], axis=0),
        ],
        axis=1,
    )


def forward_x_table():
    angles = 2.0 * math.pi * (np.arange(MX)[:, None] * np.arange(GX)[None, :] % GX) / GX
    cos, sin = np.cos(angles), np.sin(angles)
    real = np.concatenate([cos, sin], axis=1)
    imag = np.concatenate([-sin, cos], axis=1)
    return np.stack([real, imag], axis=1).reshape(2 * MX, 2 * GX).astype(np.float32)


def inverse_x_table():
    angles = 2.0 * math.pi * (np.arange(GX)[:, None] * np.arange(MX)[None, :] % GX) / GX
    cos, sin = np.cos(angles), np.sin(angles)
    real = np.stack([cos, -sin], axis=2).reshape(GX, 2 * MX)
    imag = np.stack([sin, cos], axis=2).reshape(GX, 2 * MX)
    return np.concatenate([real, imag], axis=0).astype(np.float32)


def cos_y(k, y):
    return math.cos(2.0 * math.pi * (k * y % GY) / GY)


def sin_y(k, y):
    return math.sin(2.0 * math.pi * (k * y % GY) / GY)


def dot(a, b, precision=None):
    return jnp.dot(a, b, preferred_element_type=jnp.float32, precision=precision)


def total(terms):
    terms = list(terms)
    while len(terms) > 1:
        terms = [
            terms[i] + terms[i + 1] if i + 1 < len(terms) else terms[i]
            for i in range(0, len(terms), 2)
        ]
    return terms[0]


def rotate_forward(values):
    lane = lax.broadcasted_iota(jnp.int32, values.shape, 1)
    swapped = pltpu.roll(values, LANES // 2, 1)
    return jnp.where(lane < LANES // 2, swapped, -swapped)


def rotate_inverse(values):
    lane = lax.broadcasted_iota(jnp.int32, values.shape, 1)
    ahead = pltpu.roll(values, LANES - 32, 1)
    behind = pltpu.roll(values, 32, 1)
    return jnp.where(lane % 64 < 32, -ahead, behind)


def forward_y(modes_ref, kept_ref, out_ref, plane):
    half = GY // 2
    for group in range(CL // 8):
        rows = pl.ds(group * 8, 8)

        def load(y):
            return modes_ref[y, rows, :]

        first, middle = load(0), load(half)
        even, odd = first + middle, first - middle
        cosines = [even if k % 2 == 0 else odd for k in range(MY)]
        first, middle = load(half // 2), load(half // 2 + half)
        even, odd = first + middle, first - middle
        sines = [None] * MY
        for k in range(MY):
            if k % 2 == 0:
                cosines[k] = cosines[k] + (even if k % 4 == 0 else -even)
            else:
                sines[k] = odd if k % 4 == 1 else -odd
        for y in range(1, half // 2):
            a, b, c, d = load(y), load(GY - y), load(half - y), load(half + y)
            sum1, dif1, sum2, dif2 = a + b, a - b, c + d, c - d
            for_even, for_odd = sum1 + sum2, sum1 - sum2
            sin_odd, sin_even = dif1 + dif2, dif1 - dif2
            for k in range(MY):
                cosines[k] = cosines[k] + cos_y(k, y) * (for_even if k % 2 == 0 else for_odd)
                if k > 0:
                    term = sin_y(k, y) * (sin_even if k % 2 == 0 else sin_odd)
                    sines[k] = term if sines[k] is None else sines[k] + term
        for k in range(MY):
            value = cosines[k]
            if k > 0:
                value = value + rotate_forward(sines[k])
            kept_ref[pl.ds(k * CL + group * 8, 8), :] = value
    for ky_half in range(2):
        turned = kept_ref[pl.ds(ky_half * LANES, LANES), :].T
        for part in range(4):
            for owners in range(SLABS // 8):
                start = owners * 8 * BLOCK + plane * 8 + ky_half * 4 + part
                out_ref[pl.ds(start, 8, stride=BLOCK), :] = turned[
                    part * SLABS + owners * 8 : part * SLABS + owners * 8 + 8
                ]


def exchange_kernel(
    field_ref,
    weights_ref,
    zt_hbm,
    x_forward_hbm,
    x_inverse_hbm,
    zt_back_hbm,
    bias_hbm,
    out_ref,
    field_in,
    zt_back_ref,
    zt_ref,
    x_forward_ref,
    x_inverse_ref,
    bias_ref,
    shift_ref,
    modes_ref,
    kept_ref,
    ready_ref,
    arrived,
    staged,
    high_ref,
    low_ref,
    spectrum_ref,
    partial_ref,
    parcels,
    parcels_in,
    outgoing,
    table_sem,
    field_sem,
    weight_sem,
    local_sem,
    send_sem,
    recv_sem,
    chan_send,
    chan_recv,
    back_send,
    back_recv,
):
    slab, chan = lax.axis_index("slab"), lax.axis_index("chan")
    highest = lax.Precision.HIGHEST

    def weight_copy(part):
        return pltpu.make_async_copy(weights_ref.at[part], staged.at[part], weight_sem.at[part])

    chunk = GY // CHUNKS

    def field_copy(plane, piece):
        rows = pl.ds(piece * chunk, chunk)
        return pltpu.make_async_copy(
            field_ref.at[plane, rows], field_in.at[plane, rows], field_sem.at[plane, piece]
        )

    table_copies = [
        pltpu.make_async_copy(source, target, table_sem.at[i])
        for i, (source, target) in enumerate(
            [
                (zt_hbm, zt_ref),
                (x_forward_hbm, x_forward_ref),
                (x_inverse_hbm, x_inverse_ref),
                (bias_hbm, bias_ref),
                (zt_back_hbm, zt_back_ref),
            ]
        )
    ]
    table_copies[0].start()
    for plane in range(XL):
        for piece in range(CHUNKS):
            field_copy(plane, piece).start()
    for copy in table_copies[1:4]:
        copy.start()
    for part in range(2):
        weight_copy(part).start()
    table_copies[4].start()

    barrier = pltpu.get_barrier_semaphore()

    def greet_slab(i, carry):
        pl.semaphore_signal(
            barrier, inc=1, device_id=(lax.rem(slab + i, SLABS), chan), device_id_type=MESH
        )
        return carry

    def greet_chan(i, carry):
        pl.semaphore_signal(
            barrier, inc=1, device_id=(slab, lax.rem(chan + i, CHANS)), device_id_type=MESH
        )
        return carry

    lax.fori_loop(1, SLABS, greet_slab, 0)
    lax.fori_loop(1, CHANS, greet_chan, 0)
    table_copies[0].wait()

    for plane in range(XL):
        for piece in range(CHUNKS):
            field_copy(plane, piece).wait()
            rows = pl.ds(piece * chunk, chunk)
            both = dot(field_in[plane, rows].reshape(chunk * CL, ZT), zt_ref[...])
            both = both[:, :LANES] + both[:, LANES:]
            modes_ref[rows] = both.reshape(chunk, CL, LANES)
        forward_y(modes_ref, kept_ref, ready_ref, plane)

    pl.semaphore_wait(barrier, SLABS + CHANS - 2)

    def block_of(owner):
        return pl.ds(pl.multiple_of(owner * BLOCK, BLOCK), BLOCK)

    def send_all(source, target, place, send, recv):
        def step(i, carry):
            other = lax.rem(slab + i, SLABS)
            pltpu.make_async_remote_copy(
                src_ref=source.at[block_of(other)],
                dst_ref=target.at[block_of(place)],
                send_sem=send,
                recv_sem=recv,
                device_id=(other, chan),
                device_id_type=MESH,
            ).start()
            return carry

        lax.fori_loop(1, SLABS, step, 0)
        own = pltpu.make_async_copy(
            source.at[block_of(slab)], target.at[block_of(place)], local_sem
        )
        own.start()
        return own

    def wait_bytes(ref, rows, sem):
        piece = ref.at[pl.ds(0, rows)]
        pltpu.make_async_copy(piece, piece, sem).wait()

    own = send_all(ready_ref, arrived, slab, send_sem, recv_sem)

    for part in range(2):
        weight_copy(part).wait()

        def split_weights(i, carry, part=part):
            value = staged[part, i]
            high = value.astype(jnp.bfloat16)
            low = (value - high.astype(jnp.float32)).astype(jnp.bfloat16)
            high_ref[i, :, part * LANES : (part + 1) * LANES] = high
            low_ref[i, :, part * LANES : (part + 1) * LANES] = low
            return carry

        lax.fori_loop(0, QL * MX, split_weights, 0)

    for copy in table_copies[1:]:
        copy.wait()
    own.wait()
    rows_sent = (SLABS - 1) * BLOCK
    wait_bytes(arrived, rows_sent, recv_sem)

    columns = []
    for parity in range(QL):
        for ky_half in range(2):
            columns.append(
                jnp.concatenate(
                    [
                        arrived[pl.ds(ky_half * 4 + part * 2 + parity, GX, stride=8), :]
                        for part in range(2)
                    ],
                    axis=0,
                )
            )
    spectrum = dot(x_forward_ref[...], jnp.concatenate(columns, axis=1), highest)
    for parity in range(QL):
        spectrum_ref[parity] = spectrum[:, parity * 256 : (parity + 1) * 256]

    row = lax.broadcasted_iota(jnp.int32, (MY, 256), 0)
    lane = lax.broadcasted_iota(jnp.int32, (MY, 256), 1)
    own_ky = row == lane // CL

    def mix(parity, carry):
        for kx in range(MX):
            spread = jnp.concatenate(
                [
                    jnp.where(own_ky, spectrum_ref[parity, pl.ds(2 * kx + part, 1), :], 0.0)
                    for part in range(2)
                ],
                axis=0,
            )
            high = spread.astype(jnp.bfloat16)
            low = (spread - high.astype(jnp.float32)).astype(jnp.bfloat16)
            main = dot(jnp.concatenate([high, low], axis=0), high_ref[parity * MX + kx])
            rest = dot(high, low_ref[parity * MX + kx])
            both = main[:16] + main[16:] + rest
            real = both[:8, :LANES] - both[8:, LANES:]
            imag = both[:8, LANES:] + both[8:, :LANES]
            partial_ref[pl.ds(parity * LANES + kx * 16, 8), :] = real
            partial_ref[pl.ds(parity * LANES + kx * 16 + 8, 8), :] = imag
        return carry

    lax.fori_loop(0, QL, mix, 0)

    lane = lax.broadcasted_iota(jnp.int32, (8, LANES), 1) // CL
    for parity in range(QL):
        for ky_half in range(2):
            for rows in range(2):
                pieces = [
                    partial_ref[
                        pl.ds(parity * LANES + rows * 64 + ky_half * 4 + ky, 8, stride=8), :
                    ]
                    for ky in range(4)
                ]
                for other in range(CHANS):
                    packed = None
                    for ky in range(4):
                        shift = (ky - other) % CHANS * CL
                        moved = pltpu.roll(pieces[ky], shift, 1) if shift else pieces[ky]
                        packed = moved if packed is None else jnp.where(lane == ky, moved, packed)
                    start = (parity * 2 + ky_half) * 16 + rows * 8
                    parcels[other, pl.ds(start, 8), :] = packed

    chan_copies = []
    for i in range(1, CHANS):
        other = lax.rem(chan + i, CHANS)
        copy = pltpu.make_async_remote_copy(
            src_ref=parcels.at[other],
            dst_ref=parcels_in.at[i - 1],
            send_sem=chan_send.at[i - 1],
            recv_sem=chan_recv.at[i - 1],
            device_id=(slab, other),
            device_id_type=MESH,
        )
        copy.start()
        chan_copies.append(copy)
    mixed = parcels[chan]
    for i in range(1, CHANS):
        chan_copies[i - 1].wait_recv()
        mixed = mixed + parcels_in[i - 1]

    shift_ref[...] = jnp.zeros_like(shift_ref)
    shift_ref[0:1, :CL] = bias_ref[...] * DC_SCALE
    shift = jnp.where(slab == 0, shift_ref[...], 0.0)
    mixed = jnp.concatenate([mixed[:8] + shift, mixed[8:]], axis=0)

    side = jnp.concatenate([mixed[16 * i : 16 * i + 16] for i in range(4)], axis=1)
    spatial = dot(x_inverse_ref[...], side, highest)
    for parity in range(QL):
        for ky_half in range(2):
            for part in range(2):
                at = parity * 2 + ky_half
                outgoing[pl.ds(ky_half * 4 + part * 2 + parity, GX, stride=8), :] = spatial[
                    part * GX : (part + 1) * GX, at * LANES : (at + 1) * LANES
                ]

    place = slab // 4 % 2 * 16 + slab // 8 * 4 + slab % 4
    own = send_all(outgoing, out_ref, place, back_send, back_recv)
    own.wait()
    for copy in chan_copies:
        copy.wait_send()
    wait_bytes(ready_ref, rows_sent, send_sem)
    wait_bytes(out_ref, rows_sent, back_recv)
    wait_bytes(outgoing, rows_sent, back_send)


def exchange(*operands):
    rows = SLABS * BLOCK
    return pl.pallas_call(
        exchange_kernel,
        in_specs=[pl.BlockSpec(memory_space=pl.ANY)] * len(operands),
        out_specs=[pl.BlockSpec(memory_space=pltpu.VMEM)] * 3,
        out_shape=[
            pltpu.VMEM((rows, LANES), jnp.float32),
            pltpu.VMEM((XL, GY, CL, ZT), jnp.bfloat16),
            pltpu.VMEM((2 * LANES, ZT), jnp.bfloat16),
        ],
        scratch_shapes=[
            pltpu.VMEM((ZT, 2 * LANES), jnp.bfloat16),
            pltpu.VMEM((2 * MX, 2 * GX), jnp.float32),
            pltpu.VMEM((2 * GX, 2 * MX), jnp.float32),
            pltpu.VMEM((1, CL), jnp.float32),
            pltpu.VMEM((8, LANES), jnp.float32),
            pltpu.VMEM((GY, CL, LANES), jnp.float32),
            pltpu.VMEM((MY * CL, LANES), jnp.float32),
            pltpu.VMEM((rows, LANES), jnp.float32),
            pltpu.VMEM((rows, LANES), jnp.float32),
            pltpu.VMEM((2, QL * MX, 256, LANES), jnp.float32),
            pltpu.VMEM((QL * MX, 256, 256), jnp.bfloat16),
            pltpu.VMEM((QL * MX, 256, 256), jnp.bfloat16),
            pltpu.VMEM((QL, 16, 256), jnp.float32),
            pltpu.VMEM((QL * LANES, LANES), jnp.float32),
            pltpu.VMEM((CHANS, 64, LANES), jnp.float32),
            pltpu.VMEM((CHANS - 1, 64, LANES), jnp.float32),
            pltpu.VMEM((rows, LANES), jnp.float32),
            pltpu.SemaphoreType.DMA((5,)),
            pltpu.SemaphoreType.DMA((XL, CHUNKS)),
            pltpu.SemaphoreType.DMA((2,)),
            pltpu.SemaphoreType.DMA,
            pltpu.SemaphoreType.DMA,
            pltpu.SemaphoreType.DMA,
            pltpu.SemaphoreType.DMA((CHANS - 1,)),
            pltpu.SemaphoreType.DMA((CHANS - 1,)),
            pltpu.SemaphoreType.DMA,
            pltpu.SemaphoreType.DMA,
        ],
        compiler_params=pltpu.CompilerParams(
            collective_id=0, has_side_effects=True, vmem_limit_bytes=VMEM_LIMIT
        ),
    )(*[pltpu.with_memory_space_constraint(operand, pltpu.HBM) for operand in operands])


def inverse_modes(modes_ref, kept_ref, plane):
    for ky_half in range(2):
        piece = jnp.concatenate(
            [
                modes_ref[
                    pl.ds(odd * (16 * BLOCK) + plane * 8 + ky_half * 4 + part, 16, stride=BLOCK), :
                ]
                for odd in range(2)
                for part in range(4)
            ],
            axis=0,
        )
        turned = piece.T
        for k in range(4):
            value = turned[k * CL : k * CL + CL]
            kept_ref[0, ky_half * 4 + k] = value
            kept_ref[1, ky_half * 4 + k] = rotate_inverse(value)


def inverse_y(kept_ref, y, rows):
    kept = [kept_ref[0, k, rows, :] for k in range(MY)]
    spun = [kept_ref[1, k, rows, :] for k in range(MY)]
    half = GY // 2
    if y == 0:
        even, odd = total(kept[0::2]), total(kept[1::2])
        values = {0: even + odd, half: even - odd}
        even = (kept[0] + kept[4]) - (kept[2] + kept[6])
        odd = (spun[1] + spun[5]) - (spun[3] + spun[7])
        values.update({half // 2: even + odd, half // 2 + half: even - odd})
        return values
    cos_even = total([kept[0]] + [cos_y(k, y) * kept[k] for k in (2, 4, 6)])
    cos_odd = total([cos_y(k, y) * kept[k] for k in (1, 3, 5, 7)])
    sin_even = total([sin_y(k, y) * spun[k] for k in (2, 4, 6)])
    sin_odd = total([sin_y(k, y) * spun[k] for k in (1, 3, 5, 7)])
    cos_sum, cos_dif = cos_even + cos_odd, cos_even - cos_odd
    sin_sum, sin_dif = sin_even + sin_odd, sin_odd - sin_even
    return {
        y: cos_sum + sin_sum,
        GY - y: cos_sum - sin_sum,
        half - y: cos_dif + sin_dif,
        half + y: cos_dif - sin_dif,
    }


def inverse_kernel(modes_ref, field_ref, table_ref, out_hbm, kept_ref, lhs_ref, out_ref, out_sem):
    def each_plane(plane, carry):
        inverse_modes(modes_ref, kept_ref, plane)
        for quarter in range(4):
            places = []
            for y in range(quarter * 4, quarter * 4 + 4):
                for group in range(CL // 16):
                    values = inverse_y(kept_ref, y, pl.ds(group * 16, 16))
                    for at, (place, value) in enumerate(values.items()):
                        if group == 0:
                            places.append(place)
                        high = value.astype(jnp.bfloat16)
                        low = (value - high.astype(jnp.float32)).astype(jnp.bfloat16)
                        rows = pl.ds(((y % 4) * 4 + at) * CL + group * 16, 16)
                        even = jnp.concatenate([high[:, :64], low[:, :64]], axis=1)
                        odd = jnp.concatenate([high[:, 64:], low[:, 64:]], axis=1)
                        lhs_ref[quarter, rows, :LANES] = even
                        lhs_ref[quarter, rows, LANES : 2 * LANES] = high
                        lhs_ref[quarter, rows, 2 * LANES :] = odd
            even = dot(lhs_ref[quarter, :, : 2 * LANES], table_ref[:, : ZT // 2])
            odd = dot(lhs_ref[quarter, :, LANES:], table_ref[:, ZT // 2 :])
            for at, y in enumerate(places):
                part_even = even[at * CL : at * CL + CL]
                part_odd = odd[at * CL : at * CL + CL]
                sides = ((part_even + part_odd, 0), (part_even - part_odd, ZT // 2))
                for scaled, first in sides:
                    value = (ROOT_HALF * scaled) * (1.0 + lax.erf(scaled))
                    cells = pl.ds(first, ZT // 2)
                    out_ref[plane, y, :, cells] = (
                        field_ref[plane, y, :, cells].astype(jnp.float32) + value
                    )
                pltpu.make_async_copy(out_ref.at[plane, y], out_hbm.at[plane, y], out_sem).start()
        return carry

    lax.fori_loop(0, XL, each_plane, 0)
    pltpu.make_async_copy(out_ref, out_hbm, out_sem).wait()


def inverse(*operands):
    return pl.pallas_call(
        inverse_kernel,
        in_specs=[pl.BlockSpec(memory_space=pltpu.VMEM)] * len(operands),
        out_specs=pl.BlockSpec(memory_space=pl.ANY),
        out_shape=jax.ShapeDtypeStruct((XL, GY, CL, ZT), jnp.float32),
        scratch_shapes=[
            pltpu.VMEM((2, MY, CL, LANES), jnp.float32),
            pltpu.VMEM((4, GY // 4 * CL, 3 * LANES), jnp.bfloat16),
            pltpu.VMEM((XL, GY, CL, ZT), jnp.float32),
            pltpu.SemaphoreType.DMA,
        ],
        compiler_params=pltpu.CompilerParams(vmem_limit_bytes=VMEM_LIMIT),
    )(*[pltpu.with_memory_space_constraint(operand, pltpu.VMEM) for operand in operands])


def shards(field, spectral_weights, bias):
    weights = spectral_weights.reshape(2, QL * MX, MY * CL, LANES)
    modes, field_near, zt_back = exchange(
        field,
        weights,
        jnp.asarray(forward_zt_table()),
        jnp.asarray(forward_x_table()),
        jnp.asarray(inverse_x_table()),
        jnp.asarray(inverse_zt_table()),
        bias.reshape(1, CL),
    )
    return inverse(modes, field_near, zt_back)


def solution(mesh):
    return jax.shard_map(
        shards,
        mesh=mesh,
        in_specs=(
            P("slab", None, "chan", None),
            P(None, "slab", None, None, "chan", None),
            P("chan"),
        ),
        out_specs=P("slab", None, "chan", None),
        check_vma=False,
    )
```

```python
import functools
import math

import jax
import jax.numpy as jnp
import ml_dtypes
import numpy as np
from jax import lax
from jax.experimental import pallas as pl
from jax.experimental.pallas import tpu as pltpu
from jax.sharding import PartitionSpec as P

GX, GY, GZ, GT = 64, 64, 32, 16
MX, MY, MT = 8, 8, 8
KQ, ZT = 64, 512
SLABS, CHANS = 32, 4
XL = GX // SLABS
QL = KQ // SLABS
CL = 32
LANES = 128
BLOCK = 8
MESH = pl.DeviceIdType.MESH
VMEM_LIMIT = 40 << 20
CHUNKS = 2

DC_SCALE = float(GX * GY * GZ * GT)
ROOT_HALF = math.sqrt(0.5)


def split_bf16(table):
    high = table.astype(np.float32).astype(ml_dtypes.bfloat16)
    low = (table - high.astype(np.float64)).astype(np.float32).astype(ml_dtypes.bfloat16)
    return high, low


def zt_angles():
    cells = np.arange(ZT)[:, None]
    lanes = np.arange(KQ)[None, :]
    modes = (lanes % SLABS) * QL + lanes // SLABS
    counted = (modes // MT) * (cells // GT) % GZ * GT + (modes % MT) * (cells % GT) % GT * GZ
    return 2.0 * math.pi * counted / (GZ * GT), modes


def forward_zt_table():
    angles, _ = zt_angles()
    high, low = split_bf16(np.concatenate([np.cos(angles), -np.sin(angles)], axis=1))
    return np.concatenate([high, low], axis=1)


def inverse_zt_table():
    cells = np.arange(ZT // 2)[None, :]
    row = np.arange(KQ // 2)[:, None]
    tables = []
    for odd in range(2):
        kz = 2 * (row // 4 % 4) + odd
        kt = 2 * (row % 4) + row // 16
        counted = kz * (cells // GT) % GZ * GT + kt * (cells % GT) % GT * GZ
        angles = 2.0 * math.pi * counted / (GZ * GT)
        weight = np.where(kt == 0, 1.0, 2.0) * (ROOT_HALF / (GX * GY * GZ * GT))
        tables.append(np.concatenate([weight * np.cos(angles), -weight * np.sin(angles)], axis=0))
    (even, even_low), (odd, odd_low) = map(split_bf16, tables)
    zero = np.zeros_like(even)
    return np.concatenate(
        [
            np.concatenate([even, even, even_low, zero], axis=0),
            np.concatenate([zero, odd_low, odd, odd], axis=0),
        ],
        axis=1,
    )


def forward_x_table():
    angles = 2.0 * math.pi * (np.arange(MX)[:, None] * np.arange(GX)[None, :] % GX) / GX
    cos, sin = np.cos(angles), np.sin(angles)
    real = np.concatenate([cos, sin], axis=1)
    imag = np.concatenate([-sin, cos], axis=1)
    return np.stack([real, imag], axis=1).reshape(2 * MX, 2 * GX).astype(np.float32)


def inverse_x_table():
    angles = 2.0 * math.pi * (np.arange(GX)[:, None] * np.arange(MX)[None, :] % GX) / GX
    cos, sin = np.cos(angles), np.sin(angles)
    real = np.stack([cos, -sin], axis=2).reshape(GX, 2 * MX)
    imag = np.stack([sin, cos], axis=2).reshape(GX, 2 * MX)
    return np.concatenate([real, imag], axis=0).astype(np.float32)


def cos_y(k, y):
    return math.cos(2.0 * math.pi * (k * y % GY) / GY)


def sin_y(k, y):
    return math.sin(2.0 * math.pi * (k * y % GY) / GY)


def dot(a, b, precision=None):
    return jnp.dot(a, b, preferred_element_type=jnp.float32, precision=precision)


def total(terms):
    terms = list(terms)
    while len(terms) > 1:
        terms = [
            terms[i] + terms[i + 1] if i + 1 < len(terms) else terms[i]
            for i in range(0, len(terms), 2)
        ]
    return terms[0]


def rotate_forward(values):
    lane = lax.broadcasted_iota(jnp.int32, values.shape, 1)
    swapped = pltpu.roll(values, LANES // 2, 1)
    return jnp.where(lane < LANES // 2, swapped, -swapped)


def rotate_inverse(values):
    lane = lax.broadcasted_iota(jnp.int32, values.shape, 1)
    ahead = pltpu.roll(values, LANES - 32, 1)
    behind = pltpu.roll(values, 32, 1)
    return jnp.where(lane % 64 < 32, -ahead, behind)


def forward_y(modes_ref, kept_ref, group):
    rows = pl.ds(group * 8, 8)
    half, quarter = GY // 2, GY // 4
    cosines, sines = [None] * MY, [None] * MY

    def load(y):
        return modes_ref[y, rows, :]

    def add(sums, k, factor, value):
        if factor == 1.0:
            term = value
        elif factor == -1.0:
            term = -value
        else:
            term = factor * value
        sums[k] = term if sums[k] is None else sums[k] + term

    def fold(y):
        a, b, c, d = load(y), load(GY - y), load(half - y), load(half + y)
        sum1, dif1, sum2, dif2 = a + b, a - b, c + d, c - d
        return sum1 + sum2, sum1 - sum2, dif1 - dif2, dif1 + dif2

    first, middle = load(0), load(half)
    low, high = load(quarter), load(quarter + half)
    ends = first + middle
    sides = low + high
    for k in range(MY):
        if k % 4 == 0:
            add(cosines, k, 1.0, ends + sides)
        elif k % 4 == 2:
            add(cosines, k, 1.0, ends - sides)
        else:
            add(cosines, k, 1.0, first - middle)
            add(sines, k, 1.0 if k % 4 == 1 else -1.0, low - high)
    for y in range(1, quarter // 2 + 1):
        pairs = [(y, fold(y))]
        if y < quarter // 2:
            pairs.append((quarter - y, fold(quarter - y)))
        for at, (_, cos_odd, _, sin_odd) in pairs:
            for k in range(1, MY, 2):
                add(cosines, k, cos_y(k, at), cos_odd)
                add(sines, k, sin_y(k, at), sin_odd)
        cos_even, sin_even = pairs[0][1][0], pairs[0][1][2]
        cos_sum = cos_dif = cos_even
        sin_sum = sin_dif = sin_even
        if len(pairs) > 1:
            cos_more, sin_more = pairs[1][1][0], pairs[1][1][2]
            cos_sum, cos_dif = cos_even + cos_more, cos_even - cos_more
            sin_sum, sin_dif = sin_even + sin_more, sin_even - sin_more
        add(cosines, 0, 1.0, cos_sum)
        add(cosines, 4, cos_y(4, y), cos_sum)
        for k in (2, 6):
            if len(pairs) > 1:
                add(cosines, k, cos_y(k, y), cos_dif)
            add(sines, k, sin_y(k, y), sin_sum)
        if len(pairs) > 1:
            add(sines, 4, sin_y(4, y), sin_dif)
    for k in range(MY):
        value = cosines[k]
        if k > 0:
            value = value + rotate_forward(sines[k])
        kept_ref[pl.ds(k * CL + group * 8, 8), :] = value


def forward_turn(kept_ref, out_ref, plane):
    for ky_half in range(2):
        turned = kept_ref[pl.ds(ky_half * LANES, LANES), :].T
        for at in range(4):
            part, parity = at // 2, at % 2
            for owners in range(SLABS // 8):
                start = owners * 8 * BLOCK + plane * 4 + ky_half * 2 + part
                out_ref[parity, pl.ds(start, 8, stride=BLOCK), :] = turned[
                    at * SLABS + owners * 8 : at * SLABS + owners * 8 + 8
                ]


def exchange_kernel(
    field_ref,
    weights_ref,
    zt_hbm,
    x_forward_hbm,
    x_inverse_hbm,
    zt_back_hbm,
    bias_hbm,
    out_ref,
    field_in,
    zt_back_ref,
    zt_ref,
    x_forward_ref,
    x_inverse_ref,
    bias_ref,
    shift_ref,
    modes_even,
    modes_odd,
    kept_even,
    kept_odd,
    ready_ref,
    arrived,
    staged,
    high_ref,
    low_ref,
    spectrum_ref,
    partial_ref,
    parcels,
    parcels_in,
    outgoing,
    table_sem,
    field_sem,
    weight_sem,
    local_sem,
    send_sem,
    recv_sem,
    chan_send,
    chan_recv,
    back_local,
    back_send,
    back_recv,
):
    slab, chan = lax.axis_index("slab"), lax.axis_index("chan")

    def weight_copy(part):
        return pltpu.make_async_copy(weights_ref.at[part], staged.at[part], weight_sem.at[part])

    chunk = GY // CHUNKS

    def field_copy(plane, piece):
        rows = pl.ds(piece * chunk, chunk)
        return pltpu.make_async_copy(
            field_ref.at[plane, rows], field_in.at[plane, rows], field_sem.at[plane, piece]
        )

    table_copies = [
        pltpu.make_async_copy(source, target, table_sem.at[i])
        for i, (source, target) in enumerate(
            [
                (zt_hbm, zt_ref),
                (x_forward_hbm, x_forward_ref),
                (x_inverse_hbm, x_inverse_ref),
                (bias_hbm, bias_ref),
                (zt_back_hbm, zt_back_ref),
            ]
        )
    ]
    table_copies[0].start()
    for plane in range(XL):
        for piece in range(CHUNKS):
            field_copy(plane, piece).start()
    for copy in table_copies[1:4]:
        copy.start()
    for part in range(2):
        weight_copy(part).start()
    table_copies[4].start()

    barrier = pltpu.get_barrier_semaphore()

    def greet_slab(i, carry):
        pl.semaphore_signal(
            barrier, inc=1, device_id=(lax.rem(slab + i, SLABS), chan), device_id_type=MESH
        )
        return carry

    def greet_chan(i, carry):
        pl.semaphore_signal(
            barrier, inc=1, device_id=(slab, lax.rem(chan + i, CHANS)), device_id_type=MESH
        )
        return carry

    lax.fori_loop(1, SLABS, greet_slab, 0)
    lax.fori_loop(1, CHANS, greet_chan, 0)
    table_copies[0].wait()

    modes = (modes_even, modes_odd)
    kept = (kept_even, kept_odd)

    def forward_zt(plane, first, count):
        rows = pl.ds(first, count)
        both = dot(field_in[plane, rows].reshape(count * CL, ZT), zt_ref[...])
        both = both[:, :LANES] + both[:, LANES:]
        modes[plane][rows] = both.reshape(count, CL, LANES)

    for piece in range(CHUNKS):
        field_copy(0, piece).wait()
        forward_zt(0, piece * chunk, chunk)
    field_copy(1, 0).wait()
    for group in range(CL // 8):
        forward_zt(1, group * chunk // 4, chunk // 4)
        forward_y(modes[0], kept[0], group)
    forward_turn(kept[0], ready_ref, 0)
    for piece in range(1, CHUNKS):
        field_copy(1, piece).wait()
        forward_zt(1, piece * chunk, chunk)
    for group in range(CL // 8):
        forward_y(modes[1], kept[1], group)
    forward_turn(kept[1], ready_ref, 1)

    pl.semaphore_wait(barrier, SLABS + CHANS - 2)

    def block_of(owner):
        return pl.ds(pl.multiple_of(owner * BLOCK, BLOCK), BLOCK)

    def send_all(source, target, place, parity, local, send, recv):
        def step(i, carry):
            other = lax.rem(slab + i, SLABS)
            pltpu.make_async_remote_copy(
                src_ref=source.at[parity, block_of(other)],
                dst_ref=target.at[parity, block_of(place)],
                send_sem=send.at[parity],
                recv_sem=recv.at[parity],
                device_id=(other, chan),
                device_id_type=MESH,
            ).start()
            return carry

        lax.fori_loop(1, SLABS, step, 0)
        own = pltpu.make_async_copy(
            source.at[parity, block_of(slab)], target.at[parity, block_of(place)], local.at[parity]
        )
        own.start()
        return own

    def wait_sent(ref, parity, sem):
        piece = ref.at[parity, pl.ds(0, (SLABS - 1) * BLOCK)]
        pltpu.make_async_copy(piece, piece, sem.at[parity]).wait()

    owns = [
        send_all(ready_ref, arrived, slab, parity, local_sem, send_sem, recv_sem)
        for parity in range(QL)
    ]

    for part in range(2):
        weight_copy(part).wait()

        def split_weights(i, carry, part=part):
            value = staged[part, i]
            high = value.astype(jnp.bfloat16)
            low = (value - high.astype(jnp.float32)).astype(jnp.bfloat16)
            high_ref[i, :, part * LANES : (part + 1) * LANES] = high
            low_ref[i, :, part * LANES : (part + 1) * LANES] = low
            return carry

        lax.fori_loop(0, QL * MX, split_weights, 0)

    for copy in table_copies[1:]:
        copy.wait()
    row = lax.broadcasted_iota(jnp.int32, (MY, 256), 0)
    lane = lax.broadcasted_iota(jnp.int32, (MY, 256), 1)
    own_ky = row == lane // CL
    out_lane = lax.broadcasted_iota(jnp.int32, (8, LANES), 1) // CL
    chan_copies = []

    for parity in range(QL):
        owns[parity].wait()
        wait_sent(arrived, parity, recv_sem)
        columns = [
            jnp.concatenate(
                [
                    arrived[parity, pl.ds(ky_half * 2 + part, GX, stride=4), :]
                    for part in range(2)
                ],
                axis=0,
            )
            for ky_half in range(2)
        ]
        spectrum_ref[...] = dot(
            x_forward_ref[...], jnp.concatenate(columns, axis=1), lax.Precision.HIGH
        )

        for kx in range(MX):
            spread = jnp.concatenate(
                [
                    jnp.where(own_ky, spectrum_ref[pl.ds(2 * kx + part, 1), :], 0.0)
                    for part in range(2)
                ],
                axis=0,
            )
            high = spread.astype(jnp.bfloat16)
            low = (spread - high.astype(jnp.float32)).astype(jnp.bfloat16)
            main = dot(jnp.concatenate([high, low], axis=0), high_ref[parity * MX + kx])
            rest = dot(high, low_ref[parity * MX + kx])
            both = main[:16] + main[16:] + rest
            partial_ref[pl.ds(kx * 16, 8), :] = both[:8, :LANES] - both[8:, LANES:]
            partial_ref[pl.ds(kx * 16 + 8, 8), :] = both[:8, LANES:] + both[8:, :LANES]

        for ky_half in range(2):
            for rows in range(2):
                pieces = [
                    partial_ref[pl.ds(rows * 64 + ky_half * 4 + ky, 8, stride=8), :]
                    for ky in range(4)
                ]
                for other in range(CHANS):
                    packed = None
                    for ky in range(4):
                        shift = (ky - other) % CHANS * CL
                        moved = pltpu.roll(pieces[ky], shift, 1) if shift else pieces[ky]
                        packed = (
                            moved if packed is None else jnp.where(out_lane == ky, moved, packed)
                        )
                    parcels[parity, other, pl.ds(ky_half * 16 + rows * 8, 8), :] = packed

        copies = []
        for i in range(1, CHANS):
            other = lax.rem(chan + i, CHANS)
            copy = pltpu.make_async_remote_copy(
                src_ref=parcels.at[parity, other],
                dst_ref=parcels_in.at[parity, i - 1],
                send_sem=chan_send.at[parity, i - 1],
                recv_sem=chan_recv.at[parity, i - 1],
                device_id=(slab, other),
                device_id_type=MESH,
            )
            copy.start()
            copies.append(copy)
        chan_copies.append(copies)

    shift_ref[...] = jnp.zeros_like(shift_ref)
    shift_ref[0:1, :CL] = bias_ref[...] * DC_SCALE
    bias_shift = jnp.where(slab == 0, shift_ref[...], 0.0)
    place = slab // 4 % 2 * 16 + slab // 8 * 4 + slab % 4
    owns = []

    for parity in range(QL):
        mixed = parcels[parity, chan]
        for i in range(1, CHANS):
            chan_copies[parity][i - 1].wait_recv()
            mixed = mixed + parcels_in[parity, i - 1]
        if parity == 0:
            mixed = jnp.concatenate([mixed[:8] + bias_shift, mixed[8:]], axis=0)
        side = jnp.concatenate([mixed[:16], mixed[16:]], axis=1)
        spatial = dot(x_inverse_ref[...], side, lax.Precision.HIGH)
        for ky_half in range(2):
            for part in range(2):
                outgoing[parity, pl.ds(ky_half * 2 + part, GX, stride=4), :] = spatial[
                    part * GX : (part + 1) * GX, ky_half * LANES : (ky_half + 1) * LANES
                ]
        owns.append(
            send_all(outgoing, out_ref, place, parity, back_local, back_send, back_recv)
        )

    for parity in range(QL):
        owns[parity].wait()
        for copy in chan_copies[parity]:
            copy.wait_send()
        wait_sent(ready_ref, parity, send_sem)
        wait_sent(out_ref, parity, back_recv)
        wait_sent(outgoing, parity, back_send)


def exchange(*operands):
    blocks = (QL, SLABS * BLOCK, LANES)
    return pl.pallas_call(
        exchange_kernel,
        in_specs=[pl.BlockSpec(memory_space=pl.ANY)] * len(operands),
        out_specs=[pl.BlockSpec(memory_space=pltpu.VMEM)] * 3,
        out_shape=[
            pltpu.VMEM(blocks, jnp.float32),
            pltpu.VMEM((XL, GY, CL, ZT), jnp.bfloat16),
            pltpu.VMEM((2 * LANES, ZT), jnp.bfloat16),
        ],
        scratch_shapes=[
            pltpu.VMEM((ZT, 2 * LANES), jnp.bfloat16),
            pltpu.VMEM((2 * MX, 2 * GX), jnp.float32),
            pltpu.VMEM((2 * GX, 2 * MX), jnp.float32),
            pltpu.VMEM((1, CL), jnp.float32),
            pltpu.VMEM((8, LANES), jnp.float32),
            pltpu.VMEM((GY, CL, LANES), jnp.float32),
            pltpu.VMEM((GY, CL, LANES), jnp.float32),
            pltpu.VMEM((MY * CL, LANES), jnp.float32),
            pltpu.VMEM((MY * CL, LANES), jnp.float32),
            pltpu.VMEM(blocks, jnp.float32),
            pltpu.VMEM(blocks, jnp.float32),
            pltpu.VMEM((2, QL * MX, 256, LANES), jnp.float32),
            pltpu.VMEM((QL * MX, 256, 256), jnp.bfloat16),
            pltpu.VMEM((QL * MX, 256, 256), jnp.bfloat16),
            pltpu.VMEM((16, 256), jnp.float32),
            pltpu.VMEM((LANES, LANES), jnp.float32),
            pltpu.VMEM((QL, CHANS, 32, LANES), jnp.float32),
            pltpu.VMEM((QL, CHANS - 1, 32, LANES), jnp.float32),
            pltpu.VMEM(blocks, jnp.float32),
            pltpu.SemaphoreType.DMA((5,)),
            pltpu.SemaphoreType.DMA((XL, CHUNKS)),
            pltpu.SemaphoreType.DMA((2,)),
            pltpu.SemaphoreType.DMA((QL,)),
            pltpu.SemaphoreType.DMA((QL,)),
            pltpu.SemaphoreType.DMA((QL,)),
            pltpu.SemaphoreType.DMA((QL, CHANS - 1)),
            pltpu.SemaphoreType.DMA((QL, CHANS - 1)),
            pltpu.SemaphoreType.DMA((QL,)),
            pltpu.SemaphoreType.DMA((QL,)),
            pltpu.SemaphoreType.DMA((QL,)),
        ],
        compiler_params=pltpu.CompilerParams(
            collective_id=0, has_side_effects=True, vmem_limit_bytes=VMEM_LIMIT
        ),
    )(*[pltpu.with_memory_space_constraint(operand, pltpu.HBM) for operand in operands])


def inverse_modes(modes_ref, kept_ref, plane):
    for ky_half in range(2):
        piece = jnp.concatenate(
            [
                modes_ref[
                    parity,
                    pl.ds(odd * (16 * BLOCK) + plane * 4 + ky_half * 2 + part, 16, stride=BLOCK),
                    :,
                ]
                for odd in range(2)
                for part in range(2)
                for parity in range(2)
            ],
            axis=0,
        )
        turned = piece.T
        for k in range(4):
            value = turned[k * CL : k * CL + CL]
            kept_ref[0, ky_half * 4 + k] = value
            kept_ref[1, ky_half * 4 + k] = rotate_inverse(value)


def inverse_y(kept_ref, y, rows):
    kept = [kept_ref[0, k, rows, :] for k in range(MY)]
    spun = [kept_ref[1, k, rows, :] for k in range(MY)]
    half = GY // 2
    if y == 0:
        even, odd = total(kept[0::2]), total(kept[1::2])
        values = {0: even + odd, half: even - odd}
        even = (kept[0] + kept[4]) - (kept[2] + kept[6])
        odd = (spun[1] + spun[5]) - (spun[3] + spun[7])
        values.update({half // 2: even + odd, half // 2 + half: even - odd})
        return values
    cos_even = total([kept[0]] + [cos_y(k, y) * kept[k] for k in (2, 4, 6)])
    cos_odd = total([cos_y(k, y) * kept[k] for k in (1, 3, 5, 7)])
    sin_even = total([sin_y(k, y) * spun[k] for k in (2, 4, 6)])
    sin_odd = total([sin_y(k, y) * spun[k] for k in (1, 3, 5, 7)])
    cos_sum, cos_dif = cos_even + cos_odd, cos_even - cos_odd
    sin_sum, sin_dif = sin_even + sin_odd, sin_odd - sin_even
    return {
        y: cos_sum + sin_sum,
        GY - y: cos_sum - sin_sum,
        half - y: cos_dif + sin_dif,
        half + y: cos_dif - sin_dif,
    }


def inverse_kernel(modes_ref, field_ref, table_ref, out_hbm, kept_ref, lhs_ref, out_ref, out_sem):
    def each_plane(plane, carry):
        inverse_modes(modes_ref, kept_ref, plane)
        for quarter in range(4):
            places = []
            for y in range(quarter * 4, quarter * 4 + 4):
                for group in range(CL // 16):
                    values = inverse_y(kept_ref, y, pl.ds(group * 16, 16))
                    for at, (place, value) in enumerate(values.items()):
                        if group == 0:
                            places.append(place)
                        high = value.astype(jnp.bfloat16)
                        low = (value - high.astype(jnp.float32)).astype(jnp.bfloat16)
                        rows = pl.ds(((y % 4) * 4 + at) * CL + group * 16, 16)
                        even = jnp.concatenate([high[:, :64], low[:, :64]], axis=1)
                        odd = jnp.concatenate([high[:, 64:], low[:, 64:]], axis=1)
                        lhs_ref[quarter, rows, :LANES] = even
                        lhs_ref[quarter, rows, LANES : 2 * LANES] = high
                        lhs_ref[quarter, rows, 2 * LANES :] = odd
            even = dot(lhs_ref[quarter, :, : 2 * LANES], table_ref[:, : ZT // 2])
            odd = dot(lhs_ref[quarter, :, LANES:], table_ref[:, ZT // 2 :])
            for at, y in enumerate(places):
                part_even = even[at * CL : at * CL + CL]
                part_odd = odd[at * CL : at * CL + CL]
                sides = ((part_even + part_odd, 0), (part_even - part_odd, ZT // 2))
                for scaled, first in sides:
                    value = (ROOT_HALF * scaled) * (1.0 + lax.erf(scaled))
                    cells = pl.ds(first, ZT // 2)
                    out_ref[plane, y, :, cells] = (
                        field_ref[plane, y, :, cells].astype(jnp.float32) + value
                    )
                pltpu.make_async_copy(out_ref.at[plane, y], out_hbm.at[plane, y], out_sem).start()
        return carry

    lax.fori_loop(0, XL, each_plane, 0)
    pltpu.make_async_copy(out_ref, out_hbm, out_sem).wait()


def inverse(*operands):
    return pl.pallas_call(
        inverse_kernel,
        in_specs=[pl.BlockSpec(memory_space=pltpu.VMEM)] * len(operands),
        out_specs=pl.BlockSpec(memory_space=pl.ANY),
        out_shape=jax.ShapeDtypeStruct((XL, GY, CL, ZT), jnp.float32),
        scratch_shapes=[
            pltpu.VMEM((2, MY, CL, LANES), jnp.float32),
            pltpu.VMEM((4, GY // 4 * CL, 3 * LANES), jnp.bfloat16),
            pltpu.VMEM((XL, GY, CL, ZT), jnp.float32),
            pltpu.SemaphoreType.DMA,
        ],
        compiler_params=pltpu.CompilerParams(vmem_limit_bytes=VMEM_LIMIT),
    )(*[pltpu.with_memory_space_constraint(operand, pltpu.VMEM) for operand in operands])


def shards(field, spectral_weights, bias):
    weights = spectral_weights.reshape(2, QL * MX, MY * CL, LANES)
    modes, field_near, zt_back = exchange(
        field,
        weights,
        jnp.asarray(forward_zt_table()),
        jnp.asarray(forward_x_table()),
        jnp.asarray(inverse_x_table()),
        jnp.asarray(inverse_zt_table()),
        bias.reshape(1, CL),
    )
    return inverse(modes, field_near, zt_back)


def solution(mesh):
    return jax.shard_map(
        shards,
        mesh=mesh,
        in_specs=(
            P("slab", None, "chan", None),
            P(None, "slab", None, None, "chan", None),
            P("chan"),
        ),
        out_specs=P("slab", None, "chan", None),
        check_vma=False,
    )
```

```python
import functools
import math

import jax
import jax.numpy as jnp
import ml_dtypes
import numpy as np
from jax import lax
from jax.experimental import pallas as pl
from jax.experimental.pallas import tpu as pltpu
from jax.sharding import PartitionSpec as P

GX, GY, GZ, GT = 64, 64, 32, 16
MX, MY, MT = 8, 8, 8
KQ, ZT = 64, 512
SLABS, CHANS = 32, 4
XL = GX // SLABS
QL = KQ // SLABS
CL = 32
LANES = 128
BLOCK = 8
MESH = pl.DeviceIdType.MESH
VMEM_LIMIT = 40 << 20
CHUNKS = 2

DC_SCALE = float(GX * GY * GZ * GT)
ROOT_HALF = math.sqrt(0.5)


FAR_FIRST = sorted(
    [(z, y, c) for z in range(4) for y in range(4) for c in range(2) if (z, y, c) != (0, 0, 0)],
    key=lambda step: -min(step[0], 4 - step[0]) - min(step[1], 4 - step[1]),
)


def split_bf16(table):
    high = table.astype(np.float32).astype(ml_dtypes.bfloat16)
    low = (table - high.astype(np.float64)).astype(np.float32).astype(ml_dtypes.bfloat16)
    return high, low


def zt_angles():
    cells = np.arange(ZT)[:, None]
    lanes = np.arange(KQ)[None, :]
    modes = (lanes % SLABS) * QL + lanes // SLABS
    counted = (modes // MT) * (cells // GT) % GZ * GT + (modes % MT) * (cells % GT) % GT * GZ
    return 2.0 * math.pi * counted / (GZ * GT), modes


def forward_zt_table():
    angles, _ = zt_angles()
    high, low = split_bf16(np.concatenate([np.cos(angles), -np.sin(angles)], axis=1))
    return np.concatenate([high, low], axis=1)


def inverse_zt_table():
    cells = np.arange(ZT // 2)[None, :]
    row = np.arange(KQ // 2)[:, None]
    tables = []
    for odd in range(2):
        kz = 2 * (row // 4 % 4) + odd
        kt = 2 * (row % 4) + row // 16
        counted = kz * (cells // GT) % GZ * GT + kt * (cells % GT) % GT * GZ
        angles = 2.0 * math.pi * counted / (GZ * GT)
        weight = np.where(kt == 0, 1.0, 2.0) * (ROOT_HALF / (GX * GY * GZ * GT))
        tables.append(np.concatenate([weight * np.cos(angles), -weight * np.sin(angles)], axis=0))
    (even, even_low), (odd, odd_low) = map(split_bf16, tables)
    zero = np.zeros_like(even)
    return np.concatenate(
        [
            np.concatenate([even, even, even_low, zero], axis=0),
            np.concatenate([zero, odd_low, odd, odd], axis=0),
        ],
        axis=1,
    )


def forward_x_table():
    angles = 2.0 * math.pi * (np.arange(MX)[:, None] * np.arange(GX)[None, :] % GX) / GX
    cos, sin = np.cos(angles), np.sin(angles)
    real = np.concatenate([cos, sin], axis=1)
    imag = np.concatenate([-sin, cos], axis=1)
    return np.stack([real, imag], axis=1).reshape(2 * MX, 2 * GX).astype(np.float32)


def inverse_x_table():
    angles = 2.0 * math.pi * (np.arange(GX)[:, None] * np.arange(MX)[None, :] % GX) / GX
    cos, sin = np.cos(angles), np.sin(angles)
    real = np.stack([cos, -sin], axis=2).reshape(GX, 2 * MX)
    imag = np.stack([sin, cos], axis=2).reshape(GX, 2 * MX)
    return np.concatenate([real, imag], axis=0).astype(np.float32)


def cos_y(k, y):
    return math.cos(2.0 * math.pi * (k * y % GY) / GY)


def sin_y(k, y):
    return math.sin(2.0 * math.pi * (k * y % GY) / GY)


def dot(a, b, precision=None):
    return jnp.dot(a, b, preferred_element_type=jnp.float32, precision=precision)


def total(terms):
    terms = list(terms)
    while len(terms) > 1:
        terms = [
            terms[i] + terms[i + 1] if i + 1 < len(terms) else terms[i]
            for i in range(0, len(terms), 2)
        ]
    return terms[0]


def rotate_forward(values):
    lane = lax.broadcasted_iota(jnp.int32, values.shape, 1)
    swapped = pltpu.roll(values, LANES // 2, 1)
    return jnp.where(lane < LANES // 2, swapped, -swapped)


def rotate_inverse(values):
    lane = lax.broadcasted_iota(jnp.int32, values.shape, 1)
    ahead = pltpu.roll(values, LANES - 32, 1)
    behind = pltpu.roll(values, 32, 1)
    return jnp.where(lane % 64 < 32, -ahead, behind)


def forward_y(modes_ref, kept_ref, group):
    rows = pl.ds(group * 8, 8)
    half, quarter = GY // 2, GY // 4
    cosines, sines = [None] * MY, [None] * MY

    def load(y):
        return modes_ref[y, rows, :]

    def add(sums, k, factor, value):
        if factor == 1.0:
            term = value
        elif factor == -1.0:
            term = -value
        else:
            term = factor * value
        sums[k] = term if sums[k] is None else sums[k] + term

    def fold(y):
        a, b, c, d = load(y), load(GY - y), load(half - y), load(half + y)
        sum1, dif1, sum2, dif2 = a + b, a - b, c + d, c - d
        return sum1 + sum2, sum1 - sum2, dif1 - dif2, dif1 + dif2

    first, middle = load(0), load(half)
    low, high = load(quarter), load(quarter + half)
    ends = first + middle
    sides = low + high
    for k in range(MY):
        if k % 4 == 0:
            add(cosines, k, 1.0, ends + sides)
        elif k % 4 == 2:
            add(cosines, k, 1.0, ends - sides)
        else:
            add(cosines, k, 1.0, first - middle)
            add(sines, k, 1.0 if k % 4 == 1 else -1.0, low - high)
    for y in range(1, quarter // 2 + 1):
        pairs = [(y, fold(y))]
        if y < quarter // 2:
            pairs.append((quarter - y, fold(quarter - y)))
        for at, (_, cos_odd, _, sin_odd) in pairs:
            for k in range(1, MY, 2):
                add(cosines, k, cos_y(k, at), cos_odd)
                add(sines, k, sin_y(k, at), sin_odd)
        cos_even, sin_even = pairs[0][1][0], pairs[0][1][2]
        cos_sum = cos_dif = cos_even
        sin_sum = sin_dif = sin_even
        if len(pairs) > 1:
            cos_more, sin_more = pairs[1][1][0], pairs[1][1][2]
            cos_sum, cos_dif = cos_even + cos_more, cos_even - cos_more
            sin_sum, sin_dif = sin_even + sin_more, sin_even - sin_more
        add(cosines, 0, 1.0, cos_sum)
        add(cosines, 4, cos_y(4, y), cos_sum)
        for k in (2, 6):
            if len(pairs) > 1:
                add(cosines, k, cos_y(k, y), cos_dif)
            add(sines, k, sin_y(k, y), sin_sum)
        if len(pairs) > 1:
            add(sines, 4, sin_y(4, y), sin_dif)
    for k in range(MY):
        value = cosines[k]
        if k > 0:
            value = value + rotate_forward(sines[k])
        kept_ref[pl.ds(k * CL + group * 8, 8), :] = value


def forward_turn(kept_ref, out_ref, plane):
    for ky_half in range(2):
        turned = kept_ref[pl.ds(ky_half * LANES, LANES), :].T
        for at in range(4):
            part, parity = at // 2, at % 2
            for owners in range(SLABS // 8):
                start = owners * 8 * BLOCK + plane * 4 + ky_half * 2 + part
                out_ref[parity, pl.ds(start, 8, stride=BLOCK), :] = turned[
                    at * SLABS + owners * 8 : at * SLABS + owners * 8 + 8
                ]


def exchange_kernel(
    field_ref,
    weights_ref,
    zt_hbm,
    x_forward_hbm,
    x_inverse_hbm,
    zt_back_hbm,
    bias_hbm,
    out_ref,
    field_wide,
    zt_back_ref,
    field_in,
    zt_ref,
    x_forward_ref,
    x_inverse_ref,
    bias_ref,
    shift_ref,
    modes_even,
    modes_odd,
    kept_even,
    kept_odd,
    ready_ref,
    arrived,
    staged,
    high_ref,
    low_ref,
    spectrum_ref,
    partial_ref,
    parcels,
    parcels_in,
    outgoing,
    table_sem,
    field_sem,
    weight_sem,
    local_sem,
    send_sem,
    recv_sem,
    chan_send,
    chan_recv,
    back_local,
    back_send,
    back_recv,
):
    slab, chan = lax.axis_index("slab"), lax.axis_index("chan")

    def weight_copy(part):
        return pltpu.make_async_copy(weights_ref.at[part], staged.at[part], weight_sem.at[part])

    chunk = GY // CHUNKS

    def field_copy(plane, piece):
        rows = pl.ds(piece * chunk, chunk)
        return pltpu.make_async_copy(
            field_ref.at[plane, rows], field_in.at[plane, rows], field_sem.at[plane, piece]
        )

    table_copies = [
        pltpu.make_async_copy(source, target, table_sem.at[i])
        for i, (source, target) in enumerate(
            [
                (zt_hbm, zt_ref),
                (x_forward_hbm, x_forward_ref),
                (x_inverse_hbm, x_inverse_ref),
                (bias_hbm, bias_ref),
                (zt_back_hbm, zt_back_ref),
            ]
        )
    ]
    table_copies[0].start()
    for plane in range(XL):
        for piece in range(CHUNKS):
            field_copy(plane, piece).start()
    for copy in table_copies[1:4]:
        copy.start()

    barrier = pltpu.get_barrier_semaphore()

    def greet_slab(i, carry):
        pl.semaphore_signal(
            barrier, inc=1, device_id=(lax.rem(slab + i, SLABS), chan), device_id_type=MESH
        )
        return carry

    def greet_chan(i, carry):
        pl.semaphore_signal(
            barrier, inc=1, device_id=(slab, lax.rem(chan + i, CHANS)), device_id_type=MESH
        )
        return carry

    lax.fori_loop(1, SLABS, greet_slab, 0)
    lax.fori_loop(1, CHANS, greet_chan, 0)
    table_copies[0].wait()

    modes = (modes_even, modes_odd)
    kept = (kept_even, kept_odd)

    def forward_zt(plane, first, count):
        rows = pl.ds(first, count)
        both = dot(field_in[plane, rows].reshape(count * CL, ZT), zt_ref[...])
        both = both[:, :LANES] + both[:, LANES:]
        modes[plane][rows] = both.reshape(count, CL, LANES)

    for piece in range(CHUNKS):
        field_copy(0, piece).wait()
        forward_zt(0, piece * chunk, chunk)
    field_copy(1, 0).wait()
    for group in range(CL // 8):
        forward_zt(1, group * chunk // 4, chunk // 4)
        forward_y(modes[0], kept[0], group)
    forward_turn(kept[0], ready_ref, 0)
    for piece in range(1, CHUNKS):
        field_copy(1, piece).wait()
        if piece == CHUNKS - 1:
            for part in range(2):
                weight_copy(part).start()
            table_copies[4].start()
        forward_zt(1, piece * chunk, chunk)
    for group in range(CL // 8):
        forward_y(modes[1], kept[1], group)
    forward_turn(kept[1], ready_ref, 1)

    pl.semaphore_wait(barrier, SLABS + CHANS - 2)

    def wrapped(position, size):
        ahead = [position + step for step in range(size)]
        return [jnp.where(at >= size, at - size, at) for at in ahead]

    z = lax.div(slab, 8)
    y = lax.div(slab - z * 8, 2)
    at_z = [at * 8 for at in wrapped(z, 4)]
    at_y = [at * 2 for at in wrapped(y, 4)]
    at_core = wrapped(slab - z * 8 - y * 2, 2)

    def block_of(owner):
        return pl.ds(pl.multiple_of(owner * BLOCK, BLOCK), BLOCK)

    def send_all(source, target, place, parity, local, send, recv):
        for dz, dy, dc in FAR_FIRST:
            other = at_z[dz] + at_y[dy] + at_core[dc]
            pltpu.make_async_remote_copy(
                src_ref=source.at[parity, block_of(other)],
                dst_ref=target.at[parity, block_of(place)],
                send_sem=send.at[parity],
                recv_sem=recv.at[parity],
                device_id=(other, chan),
                device_id_type=MESH,
            ).start()
        own = pltpu.make_async_copy(
            source.at[parity, block_of(slab)], target.at[parity, block_of(place)], local.at[parity]
        )
        own.start()
        return own

    def wait_sent(ref, parity, sem):
        piece = ref.at[parity, pl.ds(0, (SLABS - 1) * BLOCK)]
        pltpu.make_async_copy(piece, piece, sem.at[parity]).wait()

    owns = [
        send_all(ready_ref, arrived, slab, parity, local_sem, send_sem, recv_sem)
        for parity in range(QL)
    ]

    for part in range(2):
        weight_copy(part).wait()

        def split_weights(i, carry, part=part):
            value = staged[part, i]
            high = value.astype(jnp.bfloat16)
            low = (value - high.astype(jnp.float32)).astype(jnp.bfloat16)
            high_ref[i, :, part * LANES : (part + 1) * LANES] = high
            low_ref[i, :, part * LANES : (part + 1) * LANES] = low
            return carry

        lax.fori_loop(0, QL * MX, split_weights, 0)

    def widen(i, carry):
        field_wide[i // GY, i % GY] = field_in[i // GY, i % GY].astype(jnp.float32)
        return carry

    lax.fori_loop(0, XL * GY, widen, 0)

    for copy in table_copies[1:]:
        copy.wait()
    row = lax.broadcasted_iota(jnp.int32, (MY, 256), 0)
    lane = lax.broadcasted_iota(jnp.int32, (MY, 256), 1)
    own_ky = row == lane // CL
    out_lane = lax.broadcasted_iota(jnp.int32, (8, LANES), 1) // CL
    chan_copies = []

    for parity in range(QL):
        owns[parity].wait()
        wait_sent(arrived, parity, recv_sem)
        columns = [
            jnp.concatenate(
                [
                    arrived[parity, pl.ds(ky_half * 2 + part, GX, stride=4), :]
                    for part in range(2)
                ],
                axis=0,
            )
            for ky_half in range(2)
        ]
        spectrum_ref[...] = dot(
            x_forward_ref[...], jnp.concatenate(columns, axis=1), lax.Precision.HIGH
        )

        for kx in range(MX):
            spread = jnp.concatenate(
                [
                    jnp.where(own_ky, spectrum_ref[pl.ds(2 * kx + part, 1), :], 0.0)
                    for part in range(2)
                ],
                axis=0,
            )
            high = spread.astype(jnp.bfloat16)
            low = (spread - high.astype(jnp.float32)).astype(jnp.bfloat16)
            main = dot(jnp.concatenate([high, low], axis=0), high_ref[parity * MX + kx])
            rest = dot(high, low_ref[parity * MX + kx])
            both = main[:16] + main[16:] + rest
            partial_ref[pl.ds(kx * 16, 8), :] = both[:8, :LANES] - both[8:, LANES:]
            partial_ref[pl.ds(kx * 16 + 8, 8), :] = both[:8, LANES:] + both[8:, :LANES]

        for ky_half in range(2):
            for rows in range(2):
                pieces = [
                    partial_ref[pl.ds(rows * 64 + ky_half * 4 + ky, 8, stride=8), :]
                    for ky in range(4)
                ]
                for other in range(CHANS):
                    packed = None
                    for ky in range(4):
                        shift = (ky - other) % CHANS * CL
                        moved = pltpu.roll(pieces[ky], shift, 1) if shift else pieces[ky]
                        packed = (
                            moved if packed is None else jnp.where(out_lane == ky, moved, packed)
                        )
                    parcels[parity, other, pl.ds(ky_half * 16 + rows * 8, 8), :] = packed

        copies = []
        for i in (2, 1, 3):
            other = lax.rem(chan + i, CHANS)
            copy = pltpu.make_async_remote_copy(
                src_ref=parcels.at[parity, other],
                dst_ref=parcels_in.at[parity, i - 1],
                send_sem=chan_send.at[parity, i - 1],
                recv_sem=chan_recv.at[parity, i - 1],
                device_id=(slab, other),
                device_id_type=MESH,
            )
            copy.start()
            copies.append(copy)
        chan_copies.append([copies[1], copies[0], copies[2]])

    shift_ref[...] = jnp.zeros_like(shift_ref)
    shift_ref[0:1, :CL] = bias_ref[...] * DC_SCALE
    bias_shift = jnp.where(slab == 0, shift_ref[...], 0.0)
    place = slab // 4 % 2 * 16 + slab // 8 * 4 + slab % 4
    owns = []

    for parity in range(QL):
        mixed = parcels[parity, chan]
        for i in range(1, CHANS):
            chan_copies[parity][i - 1].wait_recv()
            mixed = mixed + parcels_in[parity, i - 1]
        if parity == 0:
            mixed = jnp.concatenate([mixed[:8] + bias_shift, mixed[8:]], axis=0)
        side = jnp.concatenate([mixed[:16], mixed[16:]], axis=1)
        spatial = dot(x_inverse_ref[...], side, lax.Precision.HIGH)
        for ky_half in range(2):
            for part in range(2):
                outgoing[parity, pl.ds(ky_half * 2 + part, GX, stride=4), :] = spatial[
                    part * GX : (part + 1) * GX, ky_half * LANES : (ky_half + 1) * LANES
                ]
        owns.append(
            send_all(outgoing, out_ref, place, parity, back_local, back_send, back_recv)
        )

    for parity in range(QL):
        owns[parity].wait()
        for copy in chan_copies[parity]:
            copy.wait_send()
        wait_sent(ready_ref, parity, send_sem)
        wait_sent(out_ref, parity, back_recv)
        wait_sent(outgoing, parity, back_send)


def exchange(*operands):
    blocks = (QL, SLABS * BLOCK, LANES)
    return pl.pallas_call(
        exchange_kernel,
        in_specs=[pl.BlockSpec(memory_space=pl.ANY)] * len(operands),
        out_specs=[pl.BlockSpec(memory_space=pltpu.VMEM)] * 3,
        out_shape=[
            pltpu.VMEM(blocks, jnp.float32),
            pltpu.VMEM((XL, GY, CL, ZT), jnp.float32),
            pltpu.VMEM((2 * LANES, ZT), jnp.bfloat16),
        ],
        scratch_shapes=[
            pltpu.VMEM((XL, GY, CL, ZT), jnp.bfloat16),
            pltpu.VMEM((ZT, 2 * LANES), jnp.bfloat16),
            pltpu.VMEM((2 * MX, 2 * GX), jnp.float32),
            pltpu.VMEM((2 * GX, 2 * MX), jnp.float32),
            pltpu.VMEM((1, CL), jnp.float32),
            pltpu.VMEM((8, LANES), jnp.float32),
            pltpu.VMEM((GY, CL, LANES), jnp.float32),
            pltpu.VMEM((GY, CL, LANES), jnp.float32),
            pltpu.VMEM((MY * CL, LANES), jnp.float32),
            pltpu.VMEM((MY * CL, LANES), jnp.float32),
            pltpu.VMEM(blocks, jnp.float32),
            pltpu.VMEM(blocks, jnp.float32),
            pltpu.VMEM((2, QL * MX, 256, LANES), jnp.float32),
            pltpu.VMEM((QL * MX, 256, 256), jnp.bfloat16),
            pltpu.VMEM((QL * MX, 256, 256), jnp.bfloat16),
            pltpu.VMEM((16, 256), jnp.float32),
            pltpu.VMEM((LANES, LANES), jnp.float32),
            pltpu.VMEM((QL, CHANS, 32, LANES), jnp.float32),
            pltpu.VMEM((QL, CHANS - 1, 32, LANES), jnp.float32),
            pltpu.VMEM(blocks, jnp.float32),
            pltpu.SemaphoreType.DMA((5,)),
            pltpu.SemaphoreType.DMA((XL, CHUNKS)),
            pltpu.SemaphoreType.DMA((2,)),
            pltpu.SemaphoreType.DMA((QL,)),
            pltpu.SemaphoreType.DMA((QL,)),
            pltpu.SemaphoreType.DMA((QL,)),
            pltpu.SemaphoreType.DMA((QL, CHANS - 1)),
            pltpu.SemaphoreType.DMA((QL, CHANS - 1)),
            pltpu.SemaphoreType.DMA((QL,)),
            pltpu.SemaphoreType.DMA((QL,)),
            pltpu.SemaphoreType.DMA((QL,)),
        ],
        compiler_params=pltpu.CompilerParams(
            collective_id=0, has_side_effects=True, vmem_limit_bytes=VMEM_LIMIT
        ),
    )(*[pltpu.with_memory_space_constraint(operand, pltpu.HBM) for operand in operands])


def inverse_modes(modes_ref, kept_ref, plane):
    for ky_half in range(2):
        piece = jnp.concatenate(
            [
                modes_ref[
                    parity,
                    pl.ds(odd * (16 * BLOCK) + plane * 4 + ky_half * 2 + part, 16, stride=BLOCK),
                    :,
                ]
                for odd in range(2)
                for part in range(2)
                for parity in range(2)
            ],
            axis=0,
        )
        turned = piece.T
        for k in range(4):
            value = turned[k * CL : k * CL + CL]
            kept_ref[0, ky_half * 4 + k] = value
            kept_ref[1, ky_half * 4 + k] = rotate_inverse(value)


def inverse_y(kept_ref, y, rows):
    kept = [kept_ref[0, k, rows, :] for k in range(MY)]
    spun = [kept_ref[1, k, rows, :] for k in range(MY)]
    half, quarter = GY // 2, GY // 4
    if y == 0:
        even, odd = total(kept[0::2]), total(kept[1::2])
        values = {0: even + odd, half: even - odd}
        even = (kept[0] + kept[4]) - (kept[2] + kept[6])
        odd = (spun[1] + spun[5]) - (spun[3] + spun[7])
        values.update({quarter: even + odd, quarter + half: even - odd})
        return values
    values = {}

    def put(at, cos_even, sin_even):
        cos_odd = total([cos_y(k, at) * kept[k] for k in (1, 3, 5, 7)])
        sin_odd = total([sin_y(k, at) * spun[k] for k in (1, 3, 5, 7)])
        cos_sum, cos_dif = cos_even + cos_odd, cos_even - cos_odd
        sin_sum, sin_dif = sin_even + sin_odd, sin_odd - sin_even
        values[at] = cos_sum + sin_sum
        values[GY - at] = cos_sum - sin_sum
        values[half - at] = cos_dif + sin_dif
        values[half + at] = cos_dif - sin_dif

    if 2 * y == quarter:
        put(y, kept[0] - kept[4], spun[2] - spun[6])
        return values
    cos_same = kept[0] + cos_y(4, y) * kept[4]
    cos_turn = cos_y(2, y) * kept[2] + cos_y(6, y) * kept[6]
    sin_same = sin_y(2, y) * spun[2] + sin_y(6, y) * spun[6]
    sin_turn = sin_y(4, y) * spun[4]
    put(y, cos_same + cos_turn, sin_same + sin_turn)
    put(quarter - y, cos_same - cos_turn, sin_same - sin_turn)
    return values


def inverse_kernel(modes_ref, field_ref, table_ref, out_hbm, kept_ref, lhs_ref, out_ref, out_sem):
    def each_plane(plane, carry):
        inverse_modes(modes_ref, kept_ref, plane)
        for quarter in range(4):
            places = []
            for y in ((1, 2), (3, 4), (5, 6), (7, 8, 0))[quarter]:
                first = len(places)
                for group in range(CL // 16):
                    values = inverse_y(kept_ref, y, pl.ds(group * 16, 16))
                    if group == 0:
                        places += values
                    for at, value in enumerate(values.values()):
                        high = value.astype(jnp.bfloat16)
                        low = (value - high.astype(jnp.float32)).astype(jnp.bfloat16)
                        rows = pl.ds((first + at) * CL + group * 16, 16)
                        even = jnp.concatenate([high[:, :64], low[:, :64]], axis=1)
                        odd = jnp.concatenate([high[:, 64:], low[:, 64:]], axis=1)
                        lhs_ref[quarter, rows, :LANES] = even
                        lhs_ref[quarter, rows, LANES : 2 * LANES] = high
                        lhs_ref[quarter, rows, 2 * LANES :] = odd
            even = dot(lhs_ref[quarter, :, : 2 * LANES], table_ref[:, : ZT // 2])
            odd = dot(lhs_ref[quarter, :, LANES:], table_ref[:, ZT // 2 :])
            for at, y in enumerate(places):
                part_even = even[at * CL : at * CL + CL]
                part_odd = odd[at * CL : at * CL + CL]
                sides = ((part_even + part_odd, 0), (part_even - part_odd, ZT // 2))
                for scaled, start in sides:
                    value = (ROOT_HALF * scaled) * (1.0 + lax.erf(scaled))
                    cells = pl.ds(start, ZT // 2)
                    out_ref[plane, y, :, cells] = (
                        field_ref[plane, y, :, cells] + value
                    )
                pltpu.make_async_copy(out_ref.at[plane, y], out_hbm.at[plane, y], out_sem).start()
        return carry

    lax.fori_loop(0, XL, each_plane, 0)
    pltpu.make_async_copy(out_ref, out_hbm, out_sem).wait()


def inverse(*operands):
    return pl.pallas_call(
        inverse_kernel,
        in_specs=[pl.BlockSpec(memory_space=pltpu.VMEM)] * len(operands),
        out_specs=pl.BlockSpec(memory_space=pl.ANY),
        out_shape=jax.ShapeDtypeStruct((XL, GY, CL, ZT), jnp.float32),
        scratch_shapes=[
            pltpu.VMEM((2, MY, CL, LANES), jnp.float32),
            pltpu.VMEM((4, GY // 4 * CL, 3 * LANES), jnp.bfloat16),
            pltpu.VMEM((XL, GY, CL, ZT), jnp.float32),
            pltpu.SemaphoreType.DMA,
        ],
        compiler_params=pltpu.CompilerParams(vmem_limit_bytes=VMEM_LIMIT),
    )(*[pltpu.with_memory_space_constraint(operand, pltpu.VMEM) for operand in operands])


def shards(field, spectral_weights, bias):
    weights = spectral_weights.reshape(2, QL * MX, MY * CL, LANES)
    modes, field_near, zt_back = exchange(
        field,
        weights,
        jnp.asarray(forward_zt_table()),
        jnp.asarray(forward_x_table()),
        jnp.asarray(inverse_x_table()),
        jnp.asarray(inverse_zt_table()),
        bias.reshape(1, CL),
    )
    return inverse(modes, field_near, zt_back)


def solution(mesh):
    return jax.shard_map(
        shards,
        mesh=mesh,
        in_specs=(
            P("slab", None, "chan", None),
            P(None, "slab", None, None, "chan", None),
            P("chan"),
        ),
        out_specs=P("slab", None, "chan", None),
        check_vma=False,
    )
```

```python
import functools
import math

import jax
import jax.numpy as jnp
import ml_dtypes
import numpy as np
from jax import lax
from jax.experimental import pallas as pl
from jax.experimental.pallas import tpu as pltpu
from jax.sharding import PartitionSpec as P

GX, GY, GZ, GT = 64, 64, 32, 16
MX, MY, MT = 8, 8, 8
KQ, ZT = 64, 512
SLABS, CHANS = 32, 4
XL = GX // SLABS
QL = KQ // SLABS
CL = 32
LANES = 128
BLOCK = 8
MESH = pl.DeviceIdType.MESH
VMEM_LIMIT = 40 << 20
HALF = CL // 2

DC_SCALE = float(GX * GY * GZ * GT)
ROOT_HALF = math.sqrt(0.5)


FAR_FIRST = sorted(
    [(z, y, c) for z in range(4) for y in range(4) for c in range(2) if (z, y, c) != (0, 0, 0)],
    key=lambda step: -min(step[0], 4 - step[0]) - min(step[1], 4 - step[1]),
)


def split_bf16(table):
    high = table.astype(np.float32).astype(ml_dtypes.bfloat16)
    low = (table - high.astype(np.float64)).astype(np.float32).astype(ml_dtypes.bfloat16)
    return high, low


def zt_angles():
    cells = np.arange(ZT)[:, None]
    lanes = np.arange(KQ)[None, :]
    modes = (lanes % SLABS) * QL + lanes // SLABS
    counted = (modes // MT) * (cells // GT) % GZ * GT + (modes % MT) * (cells % GT) % GT * GZ
    return 2.0 * math.pi * counted / (GZ * GT), modes


def forward_zt_table():
    angles, _ = zt_angles()
    high, low = split_bf16(np.concatenate([np.cos(angles), -np.sin(angles)], axis=1))
    return np.concatenate([high, low], axis=1)


def inverse_zt_table():
    cells = np.arange(ZT // 2)[None, :]
    row = np.arange(KQ // 2)[:, None]
    tables = []
    for odd in range(2):
        kz = 2 * (row // 4 % 4) + odd
        kt = 2 * (row % 4) + row // 16
        counted = kz * (cells // GT) % GZ * GT + kt * (cells % GT) % GT * GZ
        angles = 2.0 * math.pi * counted / (GZ * GT)
        weight = np.where(kt == 0, 1.0, 2.0) * (ROOT_HALF / (GX * GY * GZ * GT))
        tables.append(np.concatenate([weight * np.cos(angles), -weight * np.sin(angles)], axis=0))
    (even, even_low), (odd, odd_low) = map(split_bf16, tables)
    zero = np.zeros_like(even)
    return np.concatenate(
        [
            np.concatenate([even, even, even_low, zero], axis=0),
            np.concatenate([zero, odd_low, odd, odd], axis=0),
        ],
        axis=1,
    )


def forward_x_table():
    angles = 2.0 * math.pi * (np.arange(MX)[:, None] * np.arange(GX)[None, :] % GX) / GX
    cos, sin = np.cos(angles), np.sin(angles)
    real = np.concatenate([cos, sin], axis=1)
    imag = np.concatenate([-sin, cos], axis=1)
    return np.stack([real, imag], axis=1).reshape(2 * MX, 2 * GX).astype(np.float32)


def inverse_x_table():
    angles = 2.0 * math.pi * (np.arange(GX)[:, None] * np.arange(MX)[None, :] % GX) / GX
    cos, sin = np.cos(angles), np.sin(angles)
    real = np.stack([cos, -sin], axis=2).reshape(GX, 2 * MX)
    imag = np.stack([sin, cos], axis=2).reshape(GX, 2 * MX)
    return np.concatenate([real, imag], axis=0).astype(np.float32)


def cos_y(k, y):
    return math.cos(2.0 * math.pi * (k * y % GY) / GY)


def sin_y(k, y):
    return math.sin(2.0 * math.pi * (k * y % GY) / GY)


def dot(a, b, precision=None):
    return jnp.dot(a, b, preferred_element_type=jnp.float32, precision=precision)


def total(terms):
    terms = list(terms)
    while len(terms) > 1:
        terms = [
            terms[i] + terms[i + 1] if i + 1 < len(terms) else terms[i]
            for i in range(0, len(terms), 2)
        ]
    return terms[0]


def rotate_forward(values):
    lane = lax.broadcasted_iota(jnp.int32, values.shape, 1)
    swapped = pltpu.roll(values, LANES // 2, 1)
    return jnp.where(lane < LANES // 2, swapped, -swapped)


def rotate_inverse(values):
    lane = lax.broadcasted_iota(jnp.int32, values.shape, 1)
    ahead = pltpu.roll(values, LANES - 32, 1)
    behind = pltpu.roll(values, 32, 1)
    return jnp.where(lane % 64 < 32, -ahead, behind)


def forward_y(modes_ref, kept_ref, group):
    rows = pl.ds(group * 8, 8)
    half, quarter = GY // 2, GY // 4
    cosines, sines = [None] * MY, [None] * MY

    def load(y):
        return modes_ref[y, rows, :]

    def add(sums, k, factor, value):
        if factor == 1.0:
            term = value
        elif factor == -1.0:
            term = -value
        else:
            term = factor * value
        sums[k] = term if sums[k] is None else sums[k] + term

    def fold(y):
        a, b, c, d = load(y), load(GY - y), load(half - y), load(half + y)
        sum1, dif1, sum2, dif2 = a + b, a - b, c + d, c - d
        return sum1 + sum2, sum1 - sum2, dif1 - dif2, dif1 + dif2

    first, middle = load(0), load(half)
    low, high = load(quarter), load(quarter + half)
    ends = first + middle
    sides = low + high
    for k in range(MY):
        if k % 4 == 0:
            add(cosines, k, 1.0, ends + sides)
        elif k % 4 == 2:
            add(cosines, k, 1.0, ends - sides)
        else:
            add(cosines, k, 1.0, first - middle)
            add(sines, k, 1.0 if k % 4 == 1 else -1.0, low - high)
    for y in range(1, quarter // 2 + 1):
        pairs = [(y, fold(y))]
        if y < quarter // 2:
            pairs.append((quarter - y, fold(quarter - y)))
        for at, (_, cos_odd, _, sin_odd) in pairs:
            for k in range(1, MY, 2):
                add(cosines, k, cos_y(k, at), cos_odd)
                add(sines, k, sin_y(k, at), sin_odd)
        cos_even, sin_even = pairs[0][1][0], pairs[0][1][2]
        cos_sum = cos_dif = cos_even
        sin_sum = sin_dif = sin_even
        if len(pairs) > 1:
            cos_more, sin_more = pairs[1][1][0], pairs[1][1][2]
            cos_sum, cos_dif = cos_even + cos_more, cos_even - cos_more
            sin_sum, sin_dif = sin_even + sin_more, sin_even - sin_more
        add(cosines, 0, 1.0, cos_sum)
        add(cosines, 4, cos_y(4, y), cos_sum)
        for k in (2, 6):
            if len(pairs) > 1:
                add(cosines, k, cos_y(k, y), cos_dif)
            add(sines, k, sin_y(k, y), sin_sum)
        if len(pairs) > 1:
            add(sines, 4, sin_y(4, y), sin_dif)
    for k in range(MY):
        value = cosines[k]
        if k > 0:
            value = value + rotate_forward(sines[k])
        kept_ref[pl.ds(k * CL + group * 8, 8), :] = value


def forward_turn(kept_ref, out_ref, plane):
    for ky_half in range(2):
        turned = kept_ref[pl.ds(ky_half * LANES, LANES), :].T
        for at in range(4):
            part, parity = at // 2, at % 2
            for owners in range(SLABS // 8):
                start = owners * 8 * BLOCK + plane * 4 + ky_half * 2 + part
                out_ref[parity, pl.ds(start, 8, stride=BLOCK), :] = turned[
                    at * SLABS + owners * 8 : at * SLABS + owners * 8 + 8
                ]


def exchange_kernel(
    field_ref,
    weights_ref,
    zt_hbm,
    x_forward_hbm,
    x_inverse_hbm,
    zt_back_hbm,
    bias_hbm,
    out_ref,
    field_wide,
    zt_back_ref,
    field_in,
    zt_ref,
    x_forward_ref,
    x_inverse_ref,
    bias_ref,
    shift_ref,
    modes_even,
    modes_odd,
    kept_even,
    kept_odd,
    ready_ref,
    arrived,
    staged,
    high_ref,
    low_ref,
    spectrum_ref,
    partial_ref,
    parcels,
    parcels_in,
    outgoing,
    table_sem,
    field_sem,
    weight_sem,
    local_sem,
    send_sem,
    recv_sem,
    chan_send,
    chan_recv,
    back_local,
    back_send,
    back_recv,
):
    slab, chan = lax.axis_index("slab"), lax.axis_index("chan")

    def weight_copy(part):
        return pltpu.make_async_copy(weights_ref.at[part], staged.at[part], weight_sem.at[part])

    def field_copy(plane, piece):
        rows = pl.ds(piece * HALF, HALF)
        return pltpu.make_async_copy(
            field_ref.at[plane, :, rows], field_in.at[plane, :, rows], field_sem.at[plane, piece]
        )

    table_copies = [
        pltpu.make_async_copy(source, target, table_sem.at[i])
        for i, (source, target) in enumerate(
            [
                (zt_hbm, zt_ref),
                (x_forward_hbm, x_forward_ref),
                (x_inverse_hbm, x_inverse_ref),
                (bias_hbm, bias_ref),
                (zt_back_hbm, zt_back_ref),
            ]
        )
    ]
    table_copies[0].start()
    for plane in range(XL):
        for piece in range(2):
            field_copy(plane, piece).start()
    for copy in table_copies[1:4]:
        copy.start()

    barrier = pltpu.get_barrier_semaphore()

    def greet_slab(i, carry):
        pl.semaphore_signal(
            barrier, inc=1, device_id=(lax.rem(slab + i, SLABS), chan), device_id_type=MESH
        )
        return carry

    def greet_chan(i, carry):
        pl.semaphore_signal(
            barrier, inc=1, device_id=(slab, lax.rem(chan + i, CHANS)), device_id_type=MESH
        )
        return carry

    lax.fori_loop(1, SLABS, greet_slab, 0)
    lax.fori_loop(1, CHANS, greet_chan, 0)
    table_copies[0].wait()

    modes = (modes_even, modes_odd)
    kept = (kept_even, kept_odd)

    def forward_zt(plane, piece, first, count):
        at = (pl.ds(first, count), pl.ds(piece * HALF, HALF))
        both = dot(field_in[plane, *at].reshape(count * HALF, ZT), zt_ref[...])
        both = both[:, :LANES] + both[:, LANES:]
        modes[plane][at] = both.reshape(count, HALF, LANES)

    pieces = [(plane, piece) for plane in range(XL) for piece in range(2)]
    for at, (plane, piece) in enumerate(pieces):
        field_copy(plane, piece).wait()
        if at == len(pieces) - 1:
            for part in range(2):
                weight_copy(part).start()
            table_copies[4].start()
        for part in range(2):
            forward_zt(plane, piece, part * (GY // 2), GY // 2)
            if at > 0:
                before, group = pieces[at - 1][0], pieces[at - 1][1] * 2 + part
                forward_y(modes[before], kept[before], group)
        if at == 2:
            forward_turn(kept[0], ready_ref, 0)
    for part in range(2):
        forward_y(modes[1], kept[1], 2 + part)
    forward_turn(kept[1], ready_ref, 1)

    pl.semaphore_wait(barrier, SLABS + CHANS - 2)

    def wrapped(position, size):
        ahead = [position + step for step in range(size)]
        return [jnp.where(at >= size, at - size, at) for at in ahead]

    z = lax.div(slab, 8)
    y = lax.div(slab - z * 8, 2)
    at_z = [at * 8 for at in wrapped(z, 4)]
    at_y = [at * 2 for at in wrapped(y, 4)]
    at_core = wrapped(slab - z * 8 - y * 2, 2)

    def block_of(owner):
        return pl.ds(pl.multiple_of(owner * BLOCK, BLOCK), BLOCK)

    def send_all(source, target, place, parity, local, send, recv):
        for dz, dy, dc in FAR_FIRST:
            other = at_z[dz] + at_y[dy] + at_core[dc]
            pltpu.make_async_remote_copy(
                src_ref=source.at[parity, block_of(other)],
                dst_ref=target.at[parity, block_of(place)],
                send_sem=send.at[parity],
                recv_sem=recv.at[parity],
                device_id=(other, chan),
                device_id_type=MESH,
            ).start()
        own = pltpu.make_async_copy(
            source.at[parity, block_of(slab)], target.at[parity, block_of(place)], local.at[parity]
        )
        own.start()
        return own

    def wait_sent(ref, parity, sem):
        piece = ref.at[parity, pl.ds(0, (SLABS - 1) * BLOCK)]
        pltpu.make_async_copy(piece, piece, sem.at[parity]).wait()

    owns = [
        send_all(ready_ref, arrived, slab, parity, local_sem, send_sem, recv_sem)
        for parity in range(QL)
    ]

    for part in range(2):
        weight_copy(part).wait()

        def split_weights(i, carry, part=part):
            value = staged[part, i]
            high = value.astype(jnp.bfloat16)
            low = (value - high.astype(jnp.float32)).astype(jnp.bfloat16)
            high_ref[i, :, part * LANES : (part + 1) * LANES] = high
            low_ref[i, :, part * LANES : (part + 1) * LANES] = low
            return carry

        lax.fori_loop(0, QL * MX, split_weights, 0)

    def widen(i, carry):
        field_wide[i // GY, i % GY] = field_in[i // GY, i % GY].astype(jnp.float32)
        return carry

    lax.fori_loop(0, XL * GY, widen, 0)

    for copy in table_copies[1:]:
        copy.wait()
    row = lax.broadcasted_iota(jnp.int32, (MY, 256), 0)
    lane = lax.broadcasted_iota(jnp.int32, (MY, 256), 1)
    own_ky = row == lane // CL
    out_lane = lax.broadcasted_iota(jnp.int32, (8, LANES), 1) // CL
    chan_copies = []

    for parity in range(QL):
        owns[parity].wait()
        wait_sent(arrived, parity, recv_sem)
        columns = [
            jnp.concatenate(
                [
                    arrived[parity, pl.ds(ky_half * 2 + part, GX, stride=4), :]
                    for part in range(2)
                ],
                axis=0,
            )
            for ky_half in range(2)
        ]
        spectrum_ref[...] = dot(
            x_forward_ref[...], jnp.concatenate(columns, axis=1), lax.Precision.HIGH
        )

        for kx in range(MX):
            spread = jnp.concatenate(
                [
                    jnp.where(own_ky, spectrum_ref[pl.ds(2 * kx + part, 1), :], 0.0)
                    for part in range(2)
                ],
                axis=0,
            )
            high = spread.astype(jnp.bfloat16)
            low = (spread - high.astype(jnp.float32)).astype(jnp.bfloat16)
            main = dot(jnp.concatenate([high, low], axis=0), high_ref[parity * MX + kx])
            rest = dot(high, low_ref[parity * MX + kx])
            both = main[:16] + main[16:] + rest
            partial_ref[pl.ds(kx * 16, 8), :] = both[:8, :LANES] - both[8:, LANES:]
            partial_ref[pl.ds(kx * 16 + 8, 8), :] = both[:8, LANES:] + both[8:, :LANES]

        for ky_half in range(2):
            for rows in range(2):
                pieces = [
                    partial_ref[pl.ds(rows * 64 + ky_half * 4 + ky, 8, stride=8), :]
                    for ky in range(4)
                ]
                for other in range(CHANS):
                    packed = None
                    for ky in range(4):
                        shift = (ky - other) % CHANS * CL
                        moved = pltpu.roll(pieces[ky], shift, 1) if shift else pieces[ky]
                        packed = (
                            moved if packed is None else jnp.where(out_lane == ky, moved, packed)
                        )
                    parcels[parity, other, pl.ds(ky_half * 16 + rows * 8, 8), :] = packed

        copies = []
        for i in (2, 1, 3):
            other = lax.rem(chan + i, CHANS)
            copy = pltpu.make_async_remote_copy(
                src_ref=parcels.at[parity, other],
                dst_ref=parcels_in.at[parity, i - 1],
                send_sem=chan_send.at[parity, i - 1],
                recv_sem=chan_recv.at[parity, i - 1],
                device_id=(slab, other),
                device_id_type=MESH,
            )
            copy.start()
            copies.append(copy)
        chan_copies.append([copies[1], copies[0], copies[2]])

    shift_ref[...] = jnp.zeros_like(shift_ref)
    shift_ref[0:1, :CL] = bias_ref[...] * DC_SCALE
    bias_shift = jnp.where(slab == 0, shift_ref[...], 0.0)
    place = slab // 4 % 2 * 16 + slab // 8 * 4 + slab % 4
    owns = []

    for parity in range(QL):
        mixed = parcels[parity, chan]
        for i in range(1, CHANS):
            chan_copies[parity][i - 1].wait_recv()
            mixed = mixed + parcels_in[parity, i - 1]
        if parity == 0:
            mixed = jnp.concatenate([mixed[:8] + bias_shift, mixed[8:]], axis=0)
        side = jnp.concatenate([mixed[:16], mixed[16:]], axis=1)
        spatial = dot(x_inverse_ref[...], side, lax.Precision.HIGH)
        for ky_half in range(2):
            for part in range(2):
                outgoing[parity, pl.ds(ky_half * 2 + part, GX, stride=4), :] = spatial[
                    part * GX : (part + 1) * GX, ky_half * LANES : (ky_half + 1) * LANES
                ]
        owns.append(
            send_all(outgoing, out_ref, place, parity, back_local, back_send, back_recv)
        )

    for parity in range(QL):
        owns[parity].wait()
        for copy in chan_copies[parity]:
            copy.wait_send()
        wait_sent(ready_ref, parity, send_sem)
        wait_sent(out_ref, parity, back_recv)
        wait_sent(outgoing, parity, back_send)


def exchange(*operands):
    blocks = (QL, SLABS * BLOCK, LANES)
    return pl.pallas_call(
        exchange_kernel,
        in_specs=[pl.BlockSpec(memory_space=pl.ANY)] * len(operands),
        out_specs=[pl.BlockSpec(memory_space=pltpu.VMEM)] * 3,
        out_shape=[
            pltpu.VMEM(blocks, jnp.float32),
            pltpu.VMEM((XL, GY, CL, ZT), jnp.float32),
            pltpu.VMEM((2 * LANES, ZT), jnp.bfloat16),
        ],
        scratch_shapes=[
            pltpu.VMEM((XL, GY, CL, ZT), jnp.bfloat16),
            pltpu.VMEM((ZT, 2 * LANES), jnp.bfloat16),
            pltpu.VMEM((2 * MX, 2 * GX), jnp.float32),
            pltpu.VMEM((2 * GX, 2 * MX), jnp.float32),
            pltpu.VMEM((1, CL), jnp.float32),
            pltpu.VMEM((8, LANES), jnp.float32),
            pltpu.VMEM((GY, CL, LANES), jnp.float32),
            pltpu.VMEM((GY, CL, LANES), jnp.float32),
            pltpu.VMEM((MY * CL, LANES), jnp.float32),
            pltpu.VMEM((MY * CL, LANES), jnp.float32),
            pltpu.VMEM(blocks, jnp.float32),
            pltpu.VMEM(blocks, jnp.float32),
            pltpu.VMEM((2, QL * MX, 256, LANES), jnp.float32),
            pltpu.VMEM((QL * MX, 256, 256), jnp.bfloat16),
            pltpu.VMEM((QL * MX, 256, 256), jnp.bfloat16),
            pltpu.VMEM((16, 256), jnp.float32),
            pltpu.VMEM((LANES, LANES), jnp.float32),
            pltpu.VMEM((QL, CHANS, 32, LANES), jnp.float32),
            pltpu.VMEM((QL, CHANS - 1, 32, LANES), jnp.float32),
            pltpu.VMEM(blocks, jnp.float32),
            pltpu.SemaphoreType.DMA((5,)),
            pltpu.SemaphoreType.DMA((XL, 2)),
            pltpu.SemaphoreType.DMA((2,)),
            pltpu.SemaphoreType.DMA((QL,)),
            pltpu.SemaphoreType.DMA((QL,)),
            pltpu.SemaphoreType.DMA((QL,)),
            pltpu.SemaphoreType.DMA((QL, CHANS - 1)),
            pltpu.SemaphoreType.DMA((QL, CHANS - 1)),
            pltpu.SemaphoreType.DMA((QL,)),
            pltpu.SemaphoreType.DMA((QL,)),
            pltpu.SemaphoreType.DMA((QL,)),
        ],
        compiler_params=pltpu.CompilerParams(
            collective_id=0, has_side_effects=True, vmem_limit_bytes=VMEM_LIMIT
        ),
    )(*[pltpu.with_memory_space_constraint(operand, pltpu.HBM) for operand in operands])


def inverse_modes(modes_ref, kept_ref, plane):
    for ky_half in range(2):
        piece = jnp.concatenate(
            [
                modes_ref[
                    parity,
                    pl.ds(odd * (16 * BLOCK) + plane * 4 + ky_half * 2 + part, 16, stride=BLOCK),
                    :,
                ]
                for odd in range(2)
                for part in range(2)
                for parity in range(2)
            ],
            axis=0,
        )
        turned = piece.T
        for k in range(4):
            value = turned[k * CL : k * CL + CL]
            kept_ref[0, ky_half * 4 + k] = value
            kept_ref[1, ky_half * 4 + k] = rotate_inverse(value)


def inverse_y(kept_ref, y, rows):
    kept = [kept_ref[0, k, rows, :] for k in range(MY)]
    spun = [kept_ref[1, k, rows, :] for k in range(MY)]
    half, quarter = GY // 2, GY // 4
    if y == 0:
        even, odd = total(kept[0::2]), total(kept[1::2])
        values = {0: even + odd, half: even - odd}
        even = (kept[0] + kept[4]) - (kept[2] + kept[6])
        odd = (spun[1] + spun[5]) - (spun[3] + spun[7])
        values.update({quarter: even + odd, quarter + half: even - odd})
        return values
    values = {}

    def put(at, cos_even, sin_even):
        cos_odd = total([cos_y(k, at) * kept[k] for k in (1, 3, 5, 7)])
        sin_odd = total([sin_y(k, at) * spun[k] for k in (1, 3, 5, 7)])
        cos_sum, cos_dif = cos_even + cos_odd, cos_even - cos_odd
        sin_sum, sin_dif = sin_even + sin_odd, sin_odd - sin_even
        values[at] = cos_sum + sin_sum
        values[GY - at] = cos_sum - sin_sum
        values[half - at] = cos_dif + sin_dif
        values[half + at] = cos_dif - sin_dif

    if 2 * y == quarter:
        put(y, kept[0] - kept[4], spun[2] - spun[6])
        return values
    cos_same = kept[0] + cos_y(4, y) * kept[4]
    cos_turn = cos_y(2, y) * kept[2] + cos_y(6, y) * kept[6]
    sin_same = sin_y(2, y) * spun[2] + sin_y(6, y) * spun[6]
    sin_turn = sin_y(4, y) * spun[4]
    put(y, cos_same + cos_turn, sin_same + sin_turn)
    put(quarter - y, cos_same - cos_turn, sin_same - sin_turn)
    return values


def inverse_kernel(modes_ref, field_ref, table_ref, out_hbm, kept_ref, lhs_ref, out_ref, out_sem):
    def each_plane(plane, carry):
        inverse_modes(modes_ref, kept_ref, plane)
        for quarter in range(4):
            places = []
            for y in ((1, 2), (3, 4), (5, 6), (7, 8, 0))[quarter]:
                first = len(places)
                for group in range(CL // 16):
                    values = inverse_y(kept_ref, y, pl.ds(group * 16, 16))
                    if group == 0:
                        places += values
                    for at, value in enumerate(values.values()):
                        high = value.astype(jnp.bfloat16)
                        low = (value - high.astype(jnp.float32)).astype(jnp.bfloat16)
                        rows = pl.ds((first + at) * CL + group * 16, 16)
                        even = jnp.concatenate([high[:, :64], low[:, :64]], axis=1)
                        odd = jnp.concatenate([high[:, 64:], low[:, 64:]], axis=1)
                        lhs_ref[quarter, rows, :LANES] = even
                        lhs_ref[quarter, rows, LANES : 2 * LANES] = high
                        lhs_ref[quarter, rows, 2 * LANES :] = odd
            even = dot(lhs_ref[quarter, :, : 2 * LANES], table_ref[:, : ZT // 2])
            odd = dot(lhs_ref[quarter, :, LANES:], table_ref[:, ZT // 2 :])
            for at, y in enumerate(places):
                part_even = even[at * CL : at * CL + CL]
                part_odd = odd[at * CL : at * CL + CL]
                sides = ((part_even + part_odd, 0), (part_even - part_odd, ZT // 2))
                for scaled, start in sides:
                    value = (ROOT_HALF * scaled) * (1.0 + lax.erf(scaled))
                    cells = pl.ds(start, ZT // 2)
                    out_ref[plane, y, :, cells] = (
                        field_ref[plane, y, :, cells] + value
                    )
                pltpu.make_async_copy(out_ref.at[plane, y], out_hbm.at[plane, y], out_sem).start()
        return carry

    lax.fori_loop(0, XL, each_plane, 0)
    pltpu.make_async_copy(out_ref, out_hbm, out_sem).wait()


def inverse(*operands):
    return pl.pallas_call(
        inverse_kernel,
        in_specs=[pl.BlockSpec(memory_space=pltpu.VMEM)] * len(operands),
        out_specs=pl.BlockSpec(memory_space=pl.ANY),
        out_shape=jax.ShapeDtypeStruct((XL, GY, CL, ZT), jnp.float32),
        scratch_shapes=[
            pltpu.VMEM((2, MY, CL, LANES), jnp.float32),
            pltpu.VMEM((4, GY // 4 * CL, 3 * LANES), jnp.bfloat16),
            pltpu.VMEM((XL, GY, CL, ZT), jnp.float32),
            pltpu.SemaphoreType.DMA,
        ],
        compiler_params=pltpu.CompilerParams(vmem_limit_bytes=VMEM_LIMIT),
    )(*[pltpu.with_memory_space_constraint(operand, pltpu.VMEM) for operand in operands])


def shards(field, spectral_weights, bias):
    weights = spectral_weights.reshape(2, QL * MX, MY * CL, LANES)
    modes, field_near, zt_back = exchange(
        field,
        weights,
        jnp.asarray(forward_zt_table()),
        jnp.asarray(forward_x_table()),
        jnp.asarray(inverse_x_table()),
        jnp.asarray(inverse_zt_table()),
        bias.reshape(1, CL),
    )
    return inverse(modes, field_near, zt_back)


def solution(mesh):
    return jax.shard_map(
        shards,
        mesh=mesh,
        in_specs=(
            P("slab", None, "chan", None),
            P(None, "slab", None, None, "chan", None),
            P("chan"),
        ),
        out_specs=P("slab", None, "chan", None),
        check_vma=False,
    )
```

```python
import functools
import math

import jax
import jax.numpy as jnp
import ml_dtypes
import numpy as np
from jax import lax
from jax.experimental import pallas as pl
from jax.experimental.pallas import tpu as pltpu
from jax.sharding import PartitionSpec as P

GX, GY, GZ, GT = 64, 64, 32, 16
MX, MY, MT = 8, 8, 8
KQ, ZT = 64, 512
SLABS, CHANS = 32, 4
XL = GX // SLABS
QL = KQ // SLABS
CL = 32
LANES = 128
BLOCK = 8
MESH = pl.DeviceIdType.MESH
VMEM_LIMIT = 40 << 20
HALF = CL // 2

DC_SCALE = float(GX * GY * GZ * GT)
ROOT_HALF = math.sqrt(0.5)


FAR_FIRST = sorted(
    [(z, y, c) for z in range(4) for y in range(4) for c in range(2) if (z, y, c) != (0, 0, 0)],
    key=lambda step: -min(step[0], 4 - step[0]) - min(step[1], 4 - step[1]),
)


def split_bf16(table):
    high = table.astype(np.float32).astype(ml_dtypes.bfloat16)
    low = (table - high.astype(np.float64)).astype(np.float32).astype(ml_dtypes.bfloat16)
    return high, low


def zt_angles():
    cells = np.arange(ZT)[:, None]
    lanes = np.arange(KQ)[None, :]
    modes = (lanes % SLABS) * QL + lanes // SLABS
    counted = (modes // MT) * (cells // GT) % GZ * GT + (modes % MT) * (cells % GT) % GT * GZ
    return 2.0 * math.pi * counted / (GZ * GT), modes


def forward_zt_table():
    angles, _ = zt_angles()
    high, low = split_bf16(np.concatenate([np.cos(angles), -np.sin(angles)], axis=1))
    return np.concatenate([high, low], axis=1)


def inverse_zt_table():
    cells = np.arange(ZT // 2)[None, :]
    row = np.arange(KQ // 2)[:, None]
    tables = []
    for odd in range(2):
        kz = 2 * (row // 4 % 4) + odd
        kt = 2 * (row % 4) + row // 16
        counted = kz * (cells // GT) % GZ * GT + kt * (cells % GT) % GT * GZ
        angles = 2.0 * math.pi * counted / (GZ * GT)
        weight = np.where(kt == 0, 1.0, 2.0) * (ROOT_HALF / (GX * GY * GZ * GT))
        tables.append(np.concatenate([weight * np.cos(angles), -weight * np.sin(angles)], axis=0))
    (even, even_low), (odd, odd_low) = map(split_bf16, tables)
    zero = np.zeros_like(even)
    return np.concatenate(
        [
            np.concatenate([even, even, even_low, zero], axis=0),
            np.concatenate([zero, odd_low, odd, odd], axis=0),
        ],
        axis=1,
    )


def forward_x_table():
    angles = 2.0 * math.pi * (np.arange(MX)[:, None] * np.arange(GX)[None, :] % GX) / GX
    cos, sin = np.cos(angles), np.sin(angles)
    real = np.concatenate([cos, sin], axis=1)
    imag = np.concatenate([-sin, cos], axis=1)
    return np.stack([real, imag], axis=1).reshape(2 * MX, 2 * GX).astype(np.float32)


def inverse_x_table():
    angles = 2.0 * math.pi * (np.arange(GX)[:, None] * np.arange(MX)[None, :] % GX) / GX
    cos, sin = np.cos(angles), np.sin(angles)
    real = np.stack([cos, -sin], axis=2).reshape(GX, 2 * MX)
    imag = np.stack([sin, cos], axis=2).reshape(GX, 2 * MX)
    return np.concatenate([real, imag], axis=0).astype(np.float32)


def cos_y(k, y):
    return math.cos(2.0 * math.pi * (k * y % GY) / GY)


def sin_y(k, y):
    return math.sin(2.0 * math.pi * (k * y % GY) / GY)


def dot(a, b, precision=None):
    return jnp.dot(a, b, preferred_element_type=jnp.float32, precision=precision)


def total(terms):
    terms = list(terms)
    while len(terms) > 1:
        terms = [
            terms[i] + terms[i + 1] if i + 1 < len(terms) else terms[i]
            for i in range(0, len(terms), 2)
        ]
    return terms[0]


def rotate_forward(values):
    lane = lax.broadcasted_iota(jnp.int32, values.shape, 1)
    swapped = pltpu.roll(values, LANES // 2, 1)
    return jnp.where(lane < LANES // 2, swapped, -swapped)


def rotate_inverse(values):
    lane = lax.broadcasted_iota(jnp.int32, values.shape, 1)
    ahead = pltpu.roll(values, LANES - 32, 1)
    behind = pltpu.roll(values, 32, 1)
    return jnp.where(lane % 64 < 32, -ahead, behind)


def forward_y(modes_ref, kept_ref, group):
    rows = pl.ds(group * 8, 8)
    half, quarter = GY // 2, GY // 4
    cosines, sines = [None] * MY, [None] * MY

    def load(y):
        return modes_ref[y, rows, :]

    def add(sums, k, factor, value):
        if factor == 1.0:
            term = value
        elif factor == -1.0:
            term = -value
        else:
            term = factor * value
        sums[k] = term if sums[k] is None else sums[k] + term

    def fold(y):
        a, b, c, d = load(y), load(GY - y), load(half - y), load(half + y)
        sum1, dif1, sum2, dif2 = a + b, a - b, c + d, c - d
        return sum1 + sum2, sum1 - sum2, dif1 - dif2, dif1 + dif2

    first, middle = load(0), load(half)
    low, high = load(quarter), load(quarter + half)
    ends = first + middle
    sides = low + high
    for k in range(MY):
        if k % 4 == 0:
            add(cosines, k, 1.0, ends + sides)
        elif k % 4 == 2:
            add(cosines, k, 1.0, ends - sides)
        else:
            add(cosines, k, 1.0, first - middle)
            add(sines, k, 1.0 if k % 4 == 1 else -1.0, low - high)
    for y in range(1, quarter // 2 + 1):
        pairs = [(y, fold(y))]
        if y < quarter // 2:
            pairs.append((quarter - y, fold(quarter - y)))
        for at, (_, cos_odd, _, sin_odd) in pairs:
            for k in range(1, MY, 2):
                add(cosines, k, cos_y(k, at), cos_odd)
                add(sines, k, sin_y(k, at), sin_odd)
        cos_even, sin_even = pairs[0][1][0], pairs[0][1][2]
        cos_sum = cos_dif = cos_even
        sin_sum = sin_dif = sin_even
        if len(pairs) > 1:
            cos_more, sin_more = pairs[1][1][0], pairs[1][1][2]
            cos_sum, cos_dif = cos_even + cos_more, cos_even - cos_more
            sin_sum, sin_dif = sin_even + sin_more, sin_even - sin_more
        add(cosines, 0, 1.0, cos_sum)
        add(cosines, 4, cos_y(4, y), cos_sum)
        for k in (2, 6):
            if len(pairs) > 1:
                add(cosines, k, cos_y(k, y), cos_dif)
            add(sines, k, sin_y(k, y), sin_sum)
        if len(pairs) > 1:
            add(sines, 4, sin_y(4, y), sin_dif)
    for k in range(MY):
        value = cosines[k]
        if k > 0:
            value = value + rotate_forward(sines[k])
        kept_ref[pl.ds(k * CL + group * 8, 8), :] = value


def forward_turn(kept_ref, out_ref, plane):
    for ky_half in range(2):
        turned = kept_ref[pl.ds(ky_half * LANES, LANES), :].T
        for at in range(4):
            part, parity = at // 2, at % 2
            for owners in range(SLABS // 8):
                start = owners * 8 * BLOCK + plane * 4 + ky_half * 2 + part
                out_ref[parity, pl.ds(start, 8, stride=BLOCK), :] = turned[
                    at * SLABS + owners * 8 : at * SLABS + owners * 8 + 8
                ]


def exchange_kernel(
    field_ref,
    weights_ref,
    zt_hbm,
    x_forward_hbm,
    x_inverse_hbm,
    zt_back_hbm,
    bias_hbm,
    out_ref,
    field_wide,
    zt_back_ref,
    field_in,
    zt_ref,
    x_forward_ref,
    x_inverse_ref,
    bias_ref,
    shift_ref,
    modes_even,
    modes_odd,
    kept_even,
    kept_odd,
    ready_ref,
    arrived,
    staged,
    high_ref,
    low_ref,
    spectrum_ref,
    partial_ref,
    parcels,
    parcels_in,
    outgoing,
    table_sem,
    field_sem,
    weight_sem,
    local_sem,
    send_sem,
    recv_sem,
    chan_send,
    chan_recv,
    back_local,
    back_send,
    back_recv,
):
    slab, chan = lax.axis_index("slab"), lax.axis_index("chan")

    def weight_copy(part):
        return pltpu.make_async_copy(weights_ref.at[part], staged.at[part], weight_sem.at[part])

    def field_copy(plane, piece):
        rows = pl.ds(piece * HALF, HALF)
        return pltpu.make_async_copy(
            field_ref.at[plane, :, rows], field_in.at[plane, :, rows], field_sem.at[plane, piece]
        )

    table_copies = [
        pltpu.make_async_copy(source, target, table_sem.at[i])
        for i, (source, target) in enumerate(
            [
                (zt_hbm, zt_ref),
                (x_forward_hbm, x_forward_ref),
                (x_inverse_hbm, x_inverse_ref),
                (bias_hbm, bias_ref),
                (zt_back_hbm, zt_back_ref),
            ]
        )
    ]
    table_copies[0].start()
    for plane in range(XL):
        for piece in range(2):
            field_copy(plane, piece).start()
    for copy in table_copies[1:4]:
        copy.start()

    barrier = pltpu.get_barrier_semaphore()

    def greet_slab(i, carry):
        pl.semaphore_signal(
            barrier, inc=1, device_id=(lax.rem(slab + i, SLABS), chan), device_id_type=MESH
        )
        return carry

    def greet_chan(i, carry):
        pl.semaphore_signal(
            barrier, inc=1, device_id=(slab, lax.rem(chan + i, CHANS)), device_id_type=MESH
        )
        return carry

    lax.fori_loop(1, SLABS, greet_slab, 0)
    lax.fori_loop(1, CHANS, greet_chan, 0)
    table_copies[0].wait()

    modes = (modes_even, modes_odd)
    kept = (kept_even, kept_odd)

    def forward_zt(plane, piece, first, count):
        at = (pl.ds(first, count), pl.ds(piece * HALF, HALF))
        both = dot(field_in[plane, *at].reshape(count * HALF, ZT), zt_ref[...])
        both = both[:, :LANES] + both[:, LANES:]
        modes[plane][at] = both.reshape(count, HALF, LANES)

    pieces = [(plane, piece) for plane in range(XL) for piece in range(2)]
    for at, (plane, piece) in enumerate(pieces):
        field_copy(plane, piece).wait()
        if at == len(pieces) - 1:
            for part in range(2):
                weight_copy(part).start()
            table_copies[4].start()
        for part in range(2):
            forward_zt(plane, piece, part * (GY // 2), GY // 2)
            if at > 0:
                before, group = pieces[at - 1][0], pieces[at - 1][1] * 2 + part
                forward_y(modes[before], kept[before], group)
        if at == 2:
            forward_turn(kept[0], ready_ref, 0)
    for part in range(2):
        forward_y(modes[1], kept[1], 2 + part)
    forward_turn(kept[1], ready_ref, 1)

    pl.semaphore_wait(barrier, SLABS + CHANS - 2)

    def wrapped(position, size):
        ahead = [position + step for step in range(size)]
        return [jnp.where(at >= size, at - size, at) for at in ahead]

    z = lax.div(slab, 8)
    y = lax.div(slab - z * 8, 2)
    at_z = [at * 8 for at in wrapped(z, 4)]
    at_y = [at * 2 for at in wrapped(y, 4)]
    at_core = wrapped(slab - z * 8 - y * 2, 2)

    def block_of(owner):
        return pl.ds(pl.multiple_of(owner * BLOCK, BLOCK), BLOCK)

    def send_all(source, target, place, parity, local, send, recv):
        for dz, dy, dc in FAR_FIRST:
            other = at_z[dz] + at_y[dy] + at_core[dc]
            pltpu.make_async_remote_copy(
                src_ref=source.at[parity, block_of(other)],
                dst_ref=target.at[parity, block_of(place)],
                send_sem=send.at[parity],
                recv_sem=recv.at[parity],
                device_id=(other, chan),
                device_id_type=MESH,
            ).start()
        own = pltpu.make_async_copy(
            source.at[parity, block_of(slab)], target.at[parity, block_of(place)], local.at[parity]
        )
        own.start()
        return own

    def wait_sent(ref, parity, sem):
        piece = ref.at[parity, pl.ds(0, (SLABS - 1) * BLOCK)]
        pltpu.make_async_copy(piece, piece, sem.at[parity]).wait()

    owns = [
        send_all(ready_ref, arrived, slab, parity, local_sem, send_sem, recv_sem)
        for parity in range(QL)
    ]

    def widen(plane):
        def step(i, carry):
            field_wide[plane, i] = field_in[plane, i].astype(jnp.float32)
            return carry

        lax.fori_loop(0, GY, step, 0)

    widen(0)
    for part in range(2):
        weight_copy(part).wait()

        def split_weights(i, carry, part=part):
            value = staged[part, i]
            high = value.astype(jnp.bfloat16)
            low = (value - high.astype(jnp.float32)).astype(jnp.bfloat16)
            high_ref[i, :, part * LANES : (part + 1) * LANES] = high
            low_ref[i, :, part * LANES : (part + 1) * LANES] = low
            return carry

        lax.fori_loop(0, QL * MX, split_weights, 0)

    for copy in table_copies[1:]:
        copy.wait()
    row = lax.broadcasted_iota(jnp.int32, (MY, 256), 0)
    lane = lax.broadcasted_iota(jnp.int32, (MY, 256), 1)
    own_ky = row == lane // CL
    out_lane = lax.broadcasted_iota(jnp.int32, (8, LANES), 1) // CL
    chan_copies = []

    for parity in range(QL):
        owns[parity].wait()
        wait_sent(arrived, parity, recv_sem)
        columns = [
            jnp.concatenate(
                [
                    arrived[parity, pl.ds(ky_half * 2 + part, GX, stride=4), :]
                    for part in range(2)
                ],
                axis=0,
            )
            for ky_half in range(2)
        ]
        spectrum_ref[...] = dot(
            x_forward_ref[...], jnp.concatenate(columns, axis=1), lax.Precision.HIGH
        )

        for kx in range(MX):
            spread = jnp.concatenate(
                [
                    jnp.where(own_ky, spectrum_ref[pl.ds(2 * kx + part, 1), :], 0.0)
                    for part in range(2)
                ],
                axis=0,
            )
            high = spread.astype(jnp.bfloat16)
            low = (spread - high.astype(jnp.float32)).astype(jnp.bfloat16)
            main = dot(jnp.concatenate([high, low], axis=0), high_ref[parity * MX + kx])
            rest = dot(high, low_ref[parity * MX + kx])
            both = main[:16] + main[16:] + rest
            partial_ref[pl.ds(kx * 16, 8), :] = both[:8, :LANES] - both[8:, LANES:]
            partial_ref[pl.ds(kx * 16 + 8, 8), :] = both[:8, LANES:] + both[8:, :LANES]

        for ky_half in range(2):
            for rows in range(2):
                pieces = [
                    partial_ref[pl.ds(rows * 64 + ky_half * 4 + ky, 8, stride=8), :]
                    for ky in range(4)
                ]
                for other in range(CHANS):
                    packed = None
                    for ky in range(4):
                        shift = (ky - other) % CHANS * CL
                        moved = pltpu.roll(pieces[ky], shift, 1) if shift else pieces[ky]
                        packed = (
                            moved if packed is None else jnp.where(out_lane == ky, moved, packed)
                        )
                    parcels[parity, other, pl.ds(ky_half * 16 + rows * 8, 8), :] = packed

        copies = []
        for i in (2, 1, 3):
            other = lax.rem(chan + i, CHANS)
            copy = pltpu.make_async_remote_copy(
                src_ref=parcels.at[parity, other],
                dst_ref=parcels_in.at[parity, i - 1],
                send_sem=chan_send.at[parity, i - 1],
                recv_sem=chan_recv.at[parity, i - 1],
                device_id=(slab, other),
                device_id_type=MESH,
            )
            copy.start()
            copies.append(copy)
        chan_copies.append([copies[1], copies[0], copies[2]])

    widen(1)

    shift_ref[...] = jnp.zeros_like(shift_ref)
    shift_ref[0:1, :CL] = bias_ref[...] * DC_SCALE
    bias_shift = jnp.where(slab == 0, shift_ref[...], 0.0)
    place = slab // 4 % 2 * 16 + slab // 8 * 4 + slab % 4
    owns = []

    for parity in range(QL):
        mixed = parcels[parity, chan]
        for i in range(1, CHANS):
            chan_copies[parity][i - 1].wait_recv()
            mixed = mixed + parcels_in[parity, i - 1]
        if parity == 0:
            mixed = jnp.concatenate([mixed[:8] + bias_shift, mixed[8:]], axis=0)
        side = jnp.concatenate([mixed[:16], mixed[16:]], axis=1)
        spatial = dot(x_inverse_ref[...], side, lax.Precision.HIGH)
        for ky_half in range(2):
            for part in range(2):
                outgoing[parity, pl.ds(ky_half * 2 + part, GX, stride=4), :] = spatial[
                    part * GX : (part + 1) * GX, ky_half * LANES : (ky_half + 1) * LANES
                ]
        owns.append(
            send_all(outgoing, out_ref, place, parity, back_local, back_send, back_recv)
        )

    for parity in range(QL):
        owns[parity].wait()
        for copy in chan_copies[parity]:
            copy.wait_send()
        wait_sent(ready_ref, parity, send_sem)
        wait_sent(out_ref, parity, back_recv)
        wait_sent(outgoing, parity, back_send)


def exchange(*operands):
    blocks = (QL, SLABS * BLOCK, LANES)
    return pl.pallas_call(
        exchange_kernel,
        in_specs=[pl.BlockSpec(memory_space=pl.ANY)] * len(operands),
        out_specs=[pl.BlockSpec(memory_space=pltpu.VMEM)] * 3,
        out_shape=[
            pltpu.VMEM(blocks, jnp.float32),
            pltpu.VMEM((XL, GY, CL, ZT), jnp.float32),
            pltpu.VMEM((2 * LANES, ZT), jnp.bfloat16),
        ],
        scratch_shapes=[
            pltpu.VMEM((XL, GY, CL, ZT), jnp.bfloat16),
            pltpu.VMEM((ZT, 2 * LANES), jnp.bfloat16),
            pltpu.VMEM((2 * MX, 2 * GX), jnp.float32),
            pltpu.VMEM((2 * GX, 2 * MX), jnp.float32),
            pltpu.VMEM((1, CL), jnp.float32),
            pltpu.VMEM((8, LANES), jnp.float32),
            pltpu.VMEM((GY, CL, LANES), jnp.float32),
            pltpu.VMEM((GY, CL, LANES), jnp.float32),
            pltpu.VMEM((MY * CL, LANES), jnp.float32),
            pltpu.VMEM((MY * CL, LANES), jnp.float32),
            pltpu.VMEM(blocks, jnp.float32),
            pltpu.VMEM(blocks, jnp.float32),
            pltpu.VMEM((2, QL * MX, 256, LANES), jnp.float32),
            pltpu.VMEM((QL * MX, 256, 256), jnp.bfloat16),
            pltpu.VMEM((QL * MX, 256, 256), jnp.bfloat16),
            pltpu.VMEM((16, 256), jnp.float32),
            pltpu.VMEM((LANES, LANES), jnp.float32),
            pltpu.VMEM((QL, CHANS, 32, LANES), jnp.float32),
            pltpu.VMEM((QL, CHANS - 1, 32, LANES), jnp.float32),
            pltpu.VMEM(blocks, jnp.float32),
            pltpu.SemaphoreType.DMA((5,)),
            pltpu.SemaphoreType.DMA((XL, 2)),
            pltpu.SemaphoreType.DMA((2,)),
            pltpu.SemaphoreType.DMA((QL,)),
            pltpu.SemaphoreType.DMA((QL,)),
            pltpu.SemaphoreType.DMA((QL,)),
            pltpu.SemaphoreType.DMA((QL, CHANS - 1)),
            pltpu.SemaphoreType.DMA((QL, CHANS - 1)),
            pltpu.SemaphoreType.DMA((QL,)),
            pltpu.SemaphoreType.DMA((QL,)),
            pltpu.SemaphoreType.DMA((QL,)),
        ],
        compiler_params=pltpu.CompilerParams(
            collective_id=0, has_side_effects=True, vmem_limit_bytes=VMEM_LIMIT
        ),
    )(*[pltpu.with_memory_space_constraint(operand, pltpu.HBM) for operand in operands])


def inverse_modes(modes_ref, kept_ref, plane):
    for ky_half in range(2):
        piece = jnp.concatenate(
            [
                modes_ref[
                    parity,
                    pl.ds(odd * (16 * BLOCK) + plane * 4 + ky_half * 2 + part, 16, stride=BLOCK),
                    :,
                ]
                for odd in range(2)
                for part in range(2)
                for parity in range(2)
            ],
            axis=0,
        )
        turned = piece.T
        for k in range(4):
            value = turned[k * CL : k * CL + CL]
            kept_ref[0, ky_half * 4 + k] = value
            kept_ref[1, ky_half * 4 + k] = rotate_inverse(value)


def inverse_y(kept_ref, y, rows):
    kept = [kept_ref[0, k, rows, :] for k in range(MY)]
    spun = [kept_ref[1, k, rows, :] for k in range(MY)]
    half, quarter = GY // 2, GY // 4
    if y == 0:
        even, odd = total(kept[0::2]), total(kept[1::2])
        values = {0: even + odd, half: even - odd}
        even = (kept[0] + kept[4]) - (kept[2] + kept[6])
        odd = (spun[1] + spun[5]) - (spun[3] + spun[7])
        values.update({quarter: even + odd, quarter + half: even - odd})
        return values
    values = {}

    def put(at, cos_even, sin_even):
        cos_odd = total([cos_y(k, at) * kept[k] for k in (1, 3, 5, 7)])
        sin_odd = total([sin_y(k, at) * spun[k] for k in (1, 3, 5, 7)])
        cos_sum, cos_dif = cos_even + cos_odd, cos_even - cos_odd
        sin_sum, sin_dif = sin_even + sin_odd, sin_odd - sin_even
        values[at] = cos_sum + sin_sum
        values[GY - at] = cos_sum - sin_sum
        values[half - at] = cos_dif + sin_dif
        values[half + at] = cos_dif - sin_dif

    if 2 * y == quarter:
        put(y, kept[0] - kept[4], spun[2] - spun[6])
        return values
    cos_same = kept[0] + cos_y(4, y) * kept[4]
    cos_turn = cos_y(2, y) * kept[2] + cos_y(6, y) * kept[6]
    sin_same = sin_y(2, y) * spun[2] + sin_y(6, y) * spun[6]
    sin_turn = sin_y(4, y) * spun[4]
    put(y, cos_same + cos_turn, sin_same + sin_turn)
    put(quarter - y, cos_same - cos_turn, sin_same - sin_turn)
    return values


def inverse_kernel(modes_ref, field_ref, table_ref, out_hbm, kept_ref, lhs_ref, out_ref, out_sem):
    def each_plane(plane, carry):
        inverse_modes(modes_ref, kept_ref, plane)
        for quarter in range(4):
            places = []
            for y in ((1, 2), (3, 4), (5, 6), (7, 8, 0))[quarter]:
                first = len(places)
                for group in range(CL // 16):
                    values = inverse_y(kept_ref, y, pl.ds(group * 16, 16))
                    if group == 0:
                        places += values
                    for at, value in enumerate(values.values()):
                        high = value.astype(jnp.bfloat16)
                        low = (value - high.astype(jnp.float32)).astype(jnp.bfloat16)
                        rows = pl.ds((first + at) * CL + group * 16, 16)
                        even = jnp.concatenate([high[:, :64], low[:, :64]], axis=1)
                        odd = jnp.concatenate([high[:, 64:], low[:, 64:]], axis=1)
                        lhs_ref[quarter, rows, :LANES] = even
                        lhs_ref[quarter, rows, LANES : 2 * LANES] = high
                        lhs_ref[quarter, rows, 2 * LANES :] = odd
            even = dot(lhs_ref[quarter, :, : 2 * LANES], table_ref[:, : ZT // 2])
            odd = dot(lhs_ref[quarter, :, LANES:], table_ref[:, ZT // 2 :])
            for at, y in enumerate(places):
                part_even = even[at * CL : at * CL + CL]
                part_odd = odd[at * CL : at * CL + CL]
                sides = ((part_even + part_odd, 0), (part_even - part_odd, ZT // 2))
                for scaled, start in sides:
                    value = (ROOT_HALF * scaled) * (1.0 + lax.erf(scaled))
                    cells = pl.ds(start, ZT // 2)
                    out_ref[plane, y, :, cells] = (
                        field_ref[plane, y, :, cells] + value
                    )
                pltpu.make_async_copy(out_ref.at[plane, y], out_hbm.at[plane, y], out_sem).start()
        return carry

    lax.fori_loop(0, XL, each_plane, 0)
    pltpu.make_async_copy(out_ref, out_hbm, out_sem).wait()


def inverse(*operands):
    return pl.pallas_call(
        inverse_kernel,
        in_specs=[pl.BlockSpec(memory_space=pltpu.VMEM)] * len(operands),
        out_specs=pl.BlockSpec(memory_space=pl.ANY),
        out_shape=jax.ShapeDtypeStruct((XL, GY, CL, ZT), jnp.float32),
        scratch_shapes=[
            pltpu.VMEM((2, MY, CL, LANES), jnp.float32),
            pltpu.VMEM((4, GY // 4 * CL, 3 * LANES), jnp.bfloat16),
            pltpu.VMEM((XL, GY, CL, ZT), jnp.float32),
            pltpu.SemaphoreType.DMA,
        ],
        compiler_params=pltpu.CompilerParams(vmem_limit_bytes=VMEM_LIMIT),
    )(*[pltpu.with_memory_space_constraint(operand, pltpu.VMEM) for operand in operands])


def shards(field, spectral_weights, bias):
    weights = spectral_weights.reshape(2, QL * MX, MY * CL, LANES)
    modes, field_near, zt_back = exchange(
        field,
        weights,
        jnp.asarray(forward_zt_table()),
        jnp.asarray(forward_x_table()),
        jnp.asarray(inverse_x_table()),
        jnp.asarray(inverse_zt_table()),
        bias.reshape(1, CL),
    )
    return inverse(modes, field_near, zt_back)


def solution(mesh):
    return jax.shard_map(
        shards,
        mesh=mesh,
        in_specs=(
            P("slab", None, "chan", None),
            P(None, "slab", None, None, "chan", None),
            P("chan"),
        ),
        out_specs=P("slab", None, "chan", None),
        check_vma=False,
    )
```

```python
import functools
import math

import jax
import jax.numpy as jnp
import ml_dtypes
import numpy as np
from jax import lax
from jax.experimental import pallas as pl
from jax.experimental.pallas import tpu as pltpu
from jax.sharding import PartitionSpec as P

GX, GY, GZ, GT = 64, 64, 32, 16
MX, MY, MT = 8, 8, 8
KQ, ZT = 64, 512
SLABS, CHANS = 32, 4
XL = GX // SLABS
QL = KQ // SLABS
CL = 32
LANES = 128
BLOCK = 8
MESH = pl.DeviceIdType.MESH
VMEM_LIMIT = 40 << 20
HALF = CL // 2

DC_SCALE = float(GX * GY * GZ * GT)
ROOT_HALF = math.sqrt(0.5)


FAR_FIRST = sorted(
    [(z, y, c) for z in range(4) for y in range(4) for c in range(2) if (z, y, c) != (0, 0, 0)],
    key=lambda step: -min(step[0], 4 - step[0]) - min(step[1], 4 - step[1]),
)


def split_bf16(table):
    high = table.astype(np.float32).astype(ml_dtypes.bfloat16)
    low = (table - high.astype(np.float64)).astype(np.float32).astype(ml_dtypes.bfloat16)
    return high, low


def zt_angles():
    cells = np.arange(ZT)[:, None]
    lanes = np.arange(KQ)[None, :]
    modes = (lanes % SLABS) * QL + lanes // SLABS
    counted = (modes // MT) * (cells // GT) % GZ * GT + (modes % MT) * (cells % GT) % GT * GZ
    return 2.0 * math.pi * counted / (GZ * GT), modes


def forward_zt_table():
    angles, _ = zt_angles()
    high, low = split_bf16(np.concatenate([np.cos(angles), -np.sin(angles)], axis=1))
    return np.concatenate([high, low], axis=1)


def inverse_zt_table():
    cells = np.arange(ZT // 2)[None, :]
    row = np.arange(KQ // 2)[:, None]
    tables = []
    for odd in range(2):
        kz = 2 * (row // 4 % 4) + odd
        kt = 2 * (row % 4) + row // 16
        counted = kz * (cells // GT) % GZ * GT + kt * (cells % GT) % GT * GZ
        angles = 2.0 * math.pi * counted / (GZ * GT)
        weight = np.where(kt == 0, 1.0, 2.0) * (ROOT_HALF / (GX * GY * GZ * GT))
        tables.append(np.concatenate([weight * np.cos(angles), -weight * np.sin(angles)], axis=0))
    (even, even_low), (odd, odd_low) = map(split_bf16, tables)
    zero = np.zeros_like(even)
    return np.concatenate(
        [
            np.concatenate([even, even, even_low, zero], axis=0),
            np.concatenate([zero, odd_low, odd, odd], axis=0),
        ],
        axis=1,
    )


def forward_x_table():
    angles = 2.0 * math.pi * (np.arange(MX)[:, None] * np.arange(GX)[None, :] % GX) / GX
    cos, sin = np.cos(angles), np.sin(angles)
    real = np.concatenate([cos, sin], axis=1)
    imag = np.concatenate([-sin, cos], axis=1)
    return np.stack([real, imag], axis=1).reshape(2 * MX, 2 * GX).astype(np.float32)


def inverse_x_table():
    angles = 2.0 * math.pi * (np.arange(GX)[:, None] * np.arange(MX)[None, :] % GX) / GX
    cos, sin = np.cos(angles), np.sin(angles)
    real = np.stack([cos, -sin], axis=2).reshape(GX, 2 * MX)
    imag = np.stack([sin, cos], axis=2).reshape(GX, 2 * MX)
    return np.concatenate([real, imag], axis=0).astype(np.float32)


def cos_y(k, y):
    return math.cos(2.0 * math.pi * (k * y % GY) / GY)


def sin_y(k, y):
    return math.sin(2.0 * math.pi * (k * y % GY) / GY)


def dot(a, b, precision=None):
    return jnp.dot(a, b, preferred_element_type=jnp.float32, precision=precision)


def total(terms):
    terms = list(terms)
    while len(terms) > 1:
        terms = [
            terms[i] + terms[i + 1] if i + 1 < len(terms) else terms[i]
            for i in range(0, len(terms), 2)
        ]
    return terms[0]


def rotate_forward(values):
    lane = lax.broadcasted_iota(jnp.int32, values.shape, 1)
    swapped = pltpu.roll(values, LANES // 2, 1)
    return jnp.where(lane < LANES // 2, swapped, -swapped)


def rotate_inverse(values):
    lane = lax.broadcasted_iota(jnp.int32, values.shape, 1)
    ahead = pltpu.roll(values, LANES - 32, 1)
    behind = pltpu.roll(values, 32, 1)
    return jnp.where(lane % 64 < 32, -ahead, behind)


def forward_y(modes_ref, kept_ref, group):
    rows = pl.ds(group * 8, 8)
    half, quarter = GY // 2, GY // 4
    cosines, sines = [None] * MY, [None] * MY

    def load(y):
        return modes_ref[y, rows, :]

    def add(sums, k, factor, value):
        if factor == 1.0:
            term = value
        elif factor == -1.0:
            term = -value
        else:
            term = factor * value
        sums[k] = term if sums[k] is None else sums[k] + term

    def fold(y):
        a, b, c, d = load(y), load(GY - y), load(half - y), load(half + y)
        sum1, dif1, sum2, dif2 = a + b, a - b, c + d, c - d
        return sum1 + sum2, sum1 - sum2, dif1 - dif2, dif1 + dif2

    first, middle = load(0), load(half)
    low, high = load(quarter), load(quarter + half)
    ends = first + middle
    sides = low + high
    for k in range(MY):
        if k % 4 == 0:
            add(cosines, k, 1.0, ends + sides)
        elif k % 4 == 2:
            add(cosines, k, 1.0, ends - sides)
        else:
            add(cosines, k, 1.0, first - middle)
            add(sines, k, 1.0 if k % 4 == 1 else -1.0, low - high)
    for y in range(1, quarter // 2 + 1):
        pairs = [(y, fold(y))]
        if y < quarter // 2:
            pairs.append((quarter - y, fold(quarter - y)))
        for at, (_, cos_odd, _, sin_odd) in pairs:
            for k in range(1, MY, 2):
                add(cosines, k, cos_y(k, at), cos_odd)
                add(sines, k, sin_y(k, at), sin_odd)
        cos_even, sin_even = pairs[0][1][0], pairs[0][1][2]
        cos_sum = cos_dif = cos_even
        sin_sum = sin_dif = sin_even
        if len(pairs) > 1:
            cos_more, sin_more = pairs[1][1][0], pairs[1][1][2]
            cos_sum, cos_dif = cos_even + cos_more, cos_even - cos_more
            sin_sum, sin_dif = sin_even + sin_more, sin_even - sin_more
        add(cosines, 0, 1.0, cos_sum)
        add(cosines, 4, cos_y(4, y), cos_sum)
        for k in (2, 6):
            if len(pairs) > 1:
                add(cosines, k, cos_y(k, y), cos_dif)
            add(sines, k, sin_y(k, y), sin_sum)
        if len(pairs) > 1:
            add(sines, 4, sin_y(4, y), sin_dif)
    for k in range(MY):
        value = cosines[k]
        if k > 0:
            value = value + rotate_forward(sines[k])
        kept_ref[pl.ds(k * CL + group * 8, 8), :] = value


def forward_turn(kept_ref, out_ref, plane):
    for ky_half in range(2):
        turned = kept_ref[pl.ds(ky_half * LANES, LANES), :].T
        for at in range(4):
            part, parity = at // 2, at % 2
            for owners in range(SLABS // 8):
                start = owners * 8 * BLOCK + plane * 4 + ky_half * 2 + part
                out_ref[parity, pl.ds(start, 8, stride=BLOCK), :] = turned[
                    at * SLABS + owners * 8 : at * SLABS + owners * 8 + 8
                ]


def exchange_kernel(
    field_ref,
    weights_ref,
    zt_hbm,
    x_forward_hbm,
    x_inverse_hbm,
    zt_back_hbm,
    bias_hbm,
    out_ref,
    field_wide,
    zt_back_ref,
    field_in,
    zt_ref,
    x_forward_ref,
    x_inverse_ref,
    bias_ref,
    shift_ref,
    modes_even,
    modes_odd,
    kept_even,
    kept_odd,
    ready_ref,
    arrived,
    staged,
    high_ref,
    low_ref,
    spectrum_ref,
    partial_ref,
    parcels,
    parcels_in,
    outgoing,
    table_sem,
    field_sem,
    weight_sem,
    local_sem,
    send_sem,
    recv_sem,
    chan_send,
    chan_recv,
    back_local,
    back_send,
    back_recv,
):
    slab, chan = lax.axis_index("slab"), lax.axis_index("chan")

    def weight_copy(part):
        return pltpu.make_async_copy(weights_ref.at[part], staged.at[part], weight_sem.at[part])

    def field_copy(plane, piece):
        rows = pl.ds(piece * HALF, HALF)
        return pltpu.make_async_copy(
            field_ref.at[plane, :, rows], field_in.at[plane, :, rows], field_sem.at[plane, piece]
        )

    table_copies = [
        pltpu.make_async_copy(source, target, table_sem.at[i])
        for i, (source, target) in enumerate(
            [
                (zt_hbm, zt_ref),
                (x_forward_hbm, x_forward_ref),
                (x_inverse_hbm, x_inverse_ref),
                (bias_hbm, bias_ref),
                (zt_back_hbm, zt_back_ref),
            ]
        )
    ]
    table_copies[0].start()
    for plane in range(XL):
        for piece in range(2):
            field_copy(plane, piece).start()
    for copy in table_copies[1:4]:
        copy.start()

    barrier = pltpu.get_barrier_semaphore()

    def wrapped(position, size):
        ahead = [position + step for step in range(size)]
        return [jnp.where(at >= size, at - size, at) for at in ahead]

    z = lax.div(slab, 8)
    y = lax.div(slab - z * 8, 2)
    at_z = [at * 8 for at in wrapped(z, 4)]
    at_y = [at * 2 for at in wrapped(y, 4)]
    at_core = wrapped(slab - z * 8 - y * 2, 2)

    def greet_chan(i, carry):
        pl.semaphore_signal(
            barrier, inc=1, device_id=(slab, lax.rem(chan + i, CHANS)), device_id_type=MESH
        )
        return carry

    for dz, dy, dc in FAR_FIRST:
        other = at_z[dz] + at_y[dy] + at_core[dc]
        pl.semaphore_signal(barrier, inc=1, device_id=(other, chan), device_id_type=MESH)
    lax.fori_loop(1, CHANS, greet_chan, 0)
    table_copies[0].wait()

    modes = (modes_even, modes_odd)
    kept = (kept_even, kept_odd)

    def forward_zt(plane, piece, first, count):
        at = (pl.ds(first, count), pl.ds(piece * HALF, HALF))
        both = dot(field_in[plane, *at].reshape(count * HALF, ZT), zt_ref[...])
        both = both[:, :LANES] + both[:, LANES:]
        modes[plane][at] = both.reshape(count, HALF, LANES)

    pieces = [(plane, piece) for plane in range(XL) for piece in range(2)]
    for at, (plane, piece) in enumerate(pieces):
        field_copy(plane, piece).wait()
        if at == len(pieces) - 1:
            for part in range(2):
                weight_copy(part).start()
            table_copies[4].start()
        for part in range(2):
            forward_zt(plane, piece, part * (GY // 2), GY // 2)
            if at > 0:
                before, group = pieces[at - 1][0], pieces[at - 1][1] * 2 + part
                forward_y(modes[before], kept[before], group)
        if at == 2:
            forward_turn(kept[0], ready_ref, 0)
    for part in range(2):
        forward_y(modes[1], kept[1], 2 + part)
    forward_turn(kept[1], ready_ref, 1)

    pl.semaphore_wait(barrier, SLABS + CHANS - 2)

    def block_of(owner):
        return pl.ds(pl.multiple_of(owner * BLOCK, BLOCK), BLOCK)

    def send_all(source, target, place, parity, local, send, recv):
        for dz, dy, dc in FAR_FIRST:
            other = at_z[dz] + at_y[dy] + at_core[dc]
            pltpu.make_async_remote_copy(
                src_ref=source.at[parity, block_of(other)],
                dst_ref=target.at[parity, block_of(place)],
                send_sem=send.at[parity],
                recv_sem=recv.at[parity],
                device_id=(other, chan),
                device_id_type=MESH,
            ).start()
        own = pltpu.make_async_copy(
            source.at[parity, block_of(slab)], target.at[parity, block_of(place)], local.at[parity]
        )
        own.start()
        return own

    def wait_sent(ref, parity, sem):
        piece = ref.at[parity, pl.ds(0, (SLABS - 1) * BLOCK)]
        pltpu.make_async_copy(piece, piece, sem.at[parity]).wait()

    owns = [
        send_all(ready_ref, arrived, slab, parity, local_sem, send_sem, recv_sem)
        for parity in range(QL)
    ]

    def widen(plane):
        def step(i, carry):
            field_wide[plane, i] = field_in[plane, i].astype(jnp.float32)
            return carry

        lax.fori_loop(0, GY, step, 0)

    widen(0)
    for part in range(2):
        weight_copy(part).wait()

        def split_weights(i, carry, part=part):
            value = staged[part, i]
            high = value.astype(jnp.bfloat16)
            low = (value - high.astype(jnp.float32)).astype(jnp.bfloat16)
            high_ref[i, :, part * LANES : (part + 1) * LANES] = high
            low_ref[i, :, part * LANES : (part + 1) * LANES] = low
            return carry

        lax.fori_loop(0, QL * MX, split_weights, 0)

    for copy in table_copies[1:]:
        copy.wait()
    row = lax.broadcasted_iota(jnp.int32, (MY, 256), 0)
    lane = lax.broadcasted_iota(jnp.int32, (MY, 256), 1)
    own_ky = row == lane // CL
    out_lane = lax.broadcasted_iota(jnp.int32, (8, LANES), 1) // CL
    chan_copies = []

    for parity in range(QL):
        owns[parity].wait()
        wait_sent(arrived, parity, recv_sem)
        columns = [
            jnp.concatenate(
                [
                    arrived[parity, pl.ds(ky_half * 2 + part, GX, stride=4), :]
                    for part in range(2)
                ],
                axis=0,
            )
            for ky_half in range(2)
        ]
        spectrum_ref[...] = dot(
            x_forward_ref[...], jnp.concatenate(columns, axis=1), lax.Precision.HIGH
        )

        for kx in range(MX):
            spread = jnp.concatenate(
                [
                    jnp.where(own_ky, spectrum_ref[pl.ds(2 * kx + part, 1), :], 0.0)
                    for part in range(2)
                ],
                axis=0,
            )
            high = spread.astype(jnp.bfloat16)
            low = (spread - high.astype(jnp.float32)).astype(jnp.bfloat16)
            main = dot(jnp.concatenate([high, low], axis=0), high_ref[parity * MX + kx])
            rest = dot(high, low_ref[parity * MX + kx])
            both = main[:16] + main[16:] + rest
            partial_ref[pl.ds(kx * 16, 8), :] = both[:8, :LANES] - both[8:, LANES:]
            partial_ref[pl.ds(kx * 16 + 8, 8), :] = both[:8, LANES:] + both[8:, :LANES]

        for ky_half in range(2):
            for rows in range(2):
                pieces = [
                    partial_ref[pl.ds(rows * 64 + ky_half * 4 + ky, 8, stride=8), :]
                    for ky in range(4)
                ]
                for other in range(CHANS):
                    packed = None
                    for ky in range(4):
                        shift = (ky - other) % CHANS * CL
                        moved = pltpu.roll(pieces[ky], shift, 1) if shift else pieces[ky]
                        packed = (
                            moved if packed is None else jnp.where(out_lane == ky, moved, packed)
                        )
                    parcels[parity, other, pl.ds(ky_half * 16 + rows * 8, 8), :] = packed

        copies = []
        for i in (2, 1, 3):
            other = lax.rem(chan + i, CHANS)
            copy = pltpu.make_async_remote_copy(
                src_ref=parcels.at[parity, other],
                dst_ref=parcels_in.at[parity, i - 1],
                send_sem=chan_send.at[parity, i - 1],
                recv_sem=chan_recv.at[parity, i - 1],
                device_id=(slab, other),
                device_id_type=MESH,
            )
            copy.start()
            copies.append(copy)
        chan_copies.append([copies[1], copies[0], copies[2]])

    widen(1)

    shift_ref[...] = jnp.zeros_like(shift_ref)
    shift_ref[0:1, :CL] = bias_ref[...] * DC_SCALE
    bias_shift = jnp.where(slab == 0, shift_ref[...], 0.0)
    place = slab // 4 % 2 * 16 + slab // 8 * 4 + slab % 4
    owns = []

    for parity in range(QL):
        mixed = parcels[parity, chan]
        for i in range(1, CHANS):
            chan_copies[parity][i - 1].wait_recv()
            mixed = mixed + parcels_in[parity, i - 1]
        if parity == 0:
            mixed = jnp.concatenate([mixed[:8] + bias_shift, mixed[8:]], axis=0)
        side = jnp.concatenate([mixed[:16], mixed[16:]], axis=1)
        spatial = dot(x_inverse_ref[...], side, lax.Precision.HIGH)
        for ky_half in range(2):
            for part in range(2):
                outgoing[parity, pl.ds(ky_half * 2 + part, GX, stride=4), :] = spatial[
                    part * GX : (part + 1) * GX, ky_half * LANES : (ky_half + 1) * LANES
                ]
        owns.append(
            send_all(outgoing, out_ref, place, parity, back_local, back_send, back_recv)
        )

    for parity in range(QL):
        owns[parity].wait()
        for copy in chan_copies[parity]:
            copy.wait_send()
        wait_sent(ready_ref, parity, send_sem)
        wait_sent(out_ref, parity, back_recv)
        wait_sent(outgoing, parity, back_send)


def exchange(*operands):
    blocks = (QL, SLABS * BLOCK, LANES)
    return pl.pallas_call(
        exchange_kernel,
        in_specs=[pl.BlockSpec(memory_space=pl.ANY)] * len(operands),
        out_specs=[pl.BlockSpec(memory_space=pltpu.VMEM)] * 3,
        out_shape=[
            pltpu.VMEM(blocks, jnp.float32),
            pltpu.VMEM((XL, GY, CL, ZT), jnp.float32),
            pltpu.VMEM((2 * LANES, ZT), jnp.bfloat16),
        ],
        scratch_shapes=[
            pltpu.VMEM((XL, GY, CL, ZT), jnp.bfloat16),
            pltpu.VMEM((ZT, 2 * LANES), jnp.bfloat16),
            pltpu.VMEM((2 * MX, 2 * GX), jnp.float32),
            pltpu.VMEM((2 * GX, 2 * MX), jnp.float32),
            pltpu.VMEM((1, CL), jnp.float32),
            pltpu.VMEM((8, LANES), jnp.float32),
            pltpu.VMEM((GY, CL, LANES), jnp.float32),
            pltpu.VMEM((GY, CL, LANES), jnp.float32),
            pltpu.VMEM((MY * CL, LANES), jnp.float32),
            pltpu.VMEM((MY * CL, LANES), jnp.float32),
            pltpu.VMEM(blocks, jnp.float32),
            pltpu.VMEM(blocks, jnp.float32),
            pltpu.VMEM((2, QL * MX, 256, LANES), jnp.float32),
            pltpu.VMEM((QL * MX, 256, 256), jnp.bfloat16),
            pltpu.VMEM((QL * MX, 256, 256), jnp.bfloat16),
            pltpu.VMEM((16, 256), jnp.float32),
            pltpu.VMEM((LANES, LANES), jnp.float32),
            pltpu.VMEM((QL, CHANS, 32, LANES), jnp.float32),
            pltpu.VMEM((QL, CHANS - 1, 32, LANES), jnp.float32),
            pltpu.VMEM(blocks, jnp.float32),
            pltpu.SemaphoreType.DMA((5,)),
            pltpu.SemaphoreType.DMA((XL, 2)),
            pltpu.SemaphoreType.DMA((2,)),
            pltpu.SemaphoreType.DMA((QL,)),
            pltpu.SemaphoreType.DMA((QL,)),
            pltpu.SemaphoreType.DMA((QL,)),
            pltpu.SemaphoreType.DMA((QL, CHANS - 1)),
            pltpu.SemaphoreType.DMA((QL, CHANS - 1)),
            pltpu.SemaphoreType.DMA((QL,)),
            pltpu.SemaphoreType.DMA((QL,)),
            pltpu.SemaphoreType.DMA((QL,)),
        ],
        compiler_params=pltpu.CompilerParams(
            collective_id=0, has_side_effects=True, vmem_limit_bytes=VMEM_LIMIT
        ),
    )(*[pltpu.with_memory_space_constraint(operand, pltpu.HBM) for operand in operands])


def inverse_modes(modes_ref, kept_ref, plane):
    for ky_half in range(2):
        piece = jnp.concatenate(
            [
                modes_ref[
                    parity,
                    pl.ds(odd * (16 * BLOCK) + plane * 4 + ky_half * 2 + part, 16, stride=BLOCK),
                    :,
                ]
                for odd in range(2)
                for part in range(2)
                for parity in range(2)
            ],
            axis=0,
        )
        turned = piece.T
        for k in range(4):
            value = turned[k * CL : k * CL + CL]
            kept_ref[0, ky_half * 4 + k] = value
            kept_ref[1, ky_half * 4 + k] = rotate_inverse(value)


def inverse_y(kept_ref, y, rows):
    kept = [kept_ref[0, k, rows, :] for k in range(MY)]
    spun = [kept_ref[1, k, rows, :] for k in range(MY)]
    half, quarter = GY // 2, GY // 4
    if y == 0:
        even, odd = total(kept[0::2]), total(kept[1::2])
        values = {0: even + odd, half: even - odd}
        even = (kept[0] + kept[4]) - (kept[2] + kept[6])
        odd = (spun[1] + spun[5]) - (spun[3] + spun[7])
        values.update({quarter: even + odd, quarter + half: even - odd})
        return values
    values = {}

    def put(at, cos_even, sin_even):
        cos_odd = total([cos_y(k, at) * kept[k] for k in (1, 3, 5, 7)])
        sin_odd = total([sin_y(k, at) * spun[k] for k in (1, 3, 5, 7)])
        cos_sum, cos_dif = cos_even + cos_odd, cos_even - cos_odd
        sin_sum, sin_dif = sin_even + sin_odd, sin_odd - sin_even
        values[at] = cos_sum + sin_sum
        values[GY - at] = cos_sum - sin_sum
        values[half - at] = cos_dif + sin_dif
        values[half + at] = cos_dif - sin_dif

    if 2 * y == quarter:
        put(y, kept[0] - kept[4], spun[2] - spun[6])
        return values
    cos_same = kept[0] + cos_y(4, y) * kept[4]
    cos_turn = cos_y(2, y) * kept[2] + cos_y(6, y) * kept[6]
    sin_same = sin_y(2, y) * spun[2] + sin_y(6, y) * spun[6]
    sin_turn = sin_y(4, y) * spun[4]
    put(y, cos_same + cos_turn, sin_same + sin_turn)
    put(quarter - y, cos_same - cos_turn, sin_same - sin_turn)
    return values


def inverse_kernel(modes_ref, field_ref, table_ref, out_hbm, kept_ref, lhs_ref, out_ref, out_sem):
    def each_plane(plane, carry):
        inverse_modes(modes_ref, kept_ref, plane)
        for quarter in range(4):
            places = []
            for y in ((1, 2), (3, 4), (5, 6), (7, 8, 0))[quarter]:
                first = len(places)
                for group in range(CL // 16):
                    values = inverse_y(kept_ref, y, pl.ds(group * 16, 16))
                    if group == 0:
                        places += values
                    for at, value in enumerate(values.values()):
                        high = value.astype(jnp.bfloat16)
                        low = (value - high.astype(jnp.float32)).astype(jnp.bfloat16)
                        rows = pl.ds((first + at) * CL + group * 16, 16)
                        even = jnp.concatenate([high[:, :64], low[:, :64]], axis=1)
                        odd = jnp.concatenate([high[:, 64:], low[:, 64:]], axis=1)
                        lhs_ref[quarter, rows, :LANES] = even
                        lhs_ref[quarter, rows, LANES : 2 * LANES] = high
                        lhs_ref[quarter, rows, 2 * LANES :] = odd
            even = dot(lhs_ref[quarter, :, : 2 * LANES], table_ref[:, : ZT // 2])
            odd = dot(lhs_ref[quarter, :, LANES:], table_ref[:, ZT // 2 :])
            for at, y in enumerate(places):
                part_even = even[at * CL : at * CL + CL]
                part_odd = odd[at * CL : at * CL + CL]
                sides = ((part_even + part_odd, 0), (part_even - part_odd, ZT // 2))
                for scaled, start in sides:
                    value = (ROOT_HALF * scaled) * (1.0 + lax.erf(scaled))
                    cells = pl.ds(start, ZT // 2)
                    out_ref[plane, y, :, cells] = (
                        field_ref[plane, y, :, cells] + value
                    )
                pltpu.make_async_copy(out_ref.at[plane, y], out_hbm.at[plane, y], out_sem).start()
        return carry

    lax.fori_loop(0, XL, each_plane, 0)
    pltpu.make_async_copy(out_ref, out_hbm, out_sem).wait()


def inverse(*operands):
    return pl.pallas_call(
        inverse_kernel,
        in_specs=[pl.BlockSpec(memory_space=pltpu.VMEM)] * len(operands),
        out_specs=pl.BlockSpec(memory_space=pl.ANY),
        out_shape=jax.ShapeDtypeStruct((XL, GY, CL, ZT), jnp.float32),
        scratch_shapes=[
            pltpu.VMEM((2, MY, CL, LANES), jnp.float32),
            pltpu.VMEM((4, GY // 4 * CL, 3 * LANES), jnp.bfloat16),
            pltpu.VMEM((XL, GY, CL, ZT), jnp.float32),
            pltpu.SemaphoreType.DMA,
        ],
        compiler_params=pltpu.CompilerParams(vmem_limit_bytes=VMEM_LIMIT),
    )(*[pltpu.with_memory_space_constraint(operand, pltpu.VMEM) for operand in operands])


def shards(field, spectral_weights, bias):
    weights = spectral_weights.reshape(2, QL * MX, MY * CL, LANES)
    modes, field_near, zt_back = exchange(
        field,
        weights,
        jnp.asarray(forward_zt_table()),
        jnp.asarray(forward_x_table()),
        jnp.asarray(inverse_x_table()),
        jnp.asarray(inverse_zt_table()),
        bias.reshape(1, CL),
    )
    return inverse(modes, field_near, zt_back)


def solution(mesh):
    return jax.shard_map(
        shards,
        mesh=mesh,
        in_specs=(
            P("slab", None, "chan", None),
            P(None, "slab", None, None, "chan", None),
            P("chan"),
        ),
        out_specs=P("slab", None, "chan", None),
        check_vma=False,
    )
```
